32 devices in a mesh: comp: 2 (over x), py: 4 (over y, core), px: 4 (over z).
Axes of the slice: x: 2, y: 2, z: 4, core: 2. Of those that a mesh axis runs over, the one named last changes fastest.
Arguments:
- current_speeds: float32 [2, 64, 128, 256], P(None, 'py', 'px'), may hold values from -1.2 to 1.2
- thermal_anomaly: float32 [64, 128, 256], P('py', 'px'), may hold values from -6 to 6
- solute_amounts: float32 [16, 16, 512, 256], P(None, ('py', 'px')), may hold values from -6 to 6
- delayed_link_source: float32 [2, 2, 16, 512, 256], P('comp', None, ('py', 'px')), may hold values from -6 to 6
- marine_indicator: int32 [64, 128], replicated, may hold values 0 or 1
- floor_layer_index: int32 [64, 128], replicated, may hold values from 1 to 256
- holder_rank: int32 [16, 16], replicated, may hold values from 0 to 15, each once within a row
- biota_exchange_matrix: float32 [16, 16], replicated, may hold values from -1.5 to 1.5
- photic_absorb_share: float32 [16], replicated, may hold values from -4 to 4
- chroma_loading: float32 [16], replicated, may hold values from -3 to 3
Outputs:
- coupling_out: float32 [2, 2, 16, 512, 256], P('comp', None, ('py', 'px'))
The draws below stay inside these ranges and needn't reach their ends.
Inputs may be any that keep to these rules, and one draw needn't show every extreme that they name: `holder_rank`: each row of owner names every tracer owner once.
All inputs are finite; a program needn't handle non-finite values.
Results may differ from the reference program's by a relative error of at most 0.0001.
Values sent between devices are 32-bit elements; how exact they have to be, the bound alone decides.
No kernel may reach another device: no remote copies, remote signals or barrier semaphores. Data moves between devices by JAX's collectives and lax.ppermute only.
A program may use at most 128 MiB of HBM per device.

```python
import jax
import jax.numpy as jnp
from jax import lax

NTR = 16
CY = 16
CX = 32
DEPTH_LAYERS = 256
STEPS = 3
GRID_NORTHINGS = 64
GRID_EASTINGS = 128
NP = 16
CP = 512
SC = 32
N_PY = 4
N_PX = 4


def touch_ends(entries, own_key, low, high):
    dims = entries.shape
    place = [jax.random.randint(jax.random.fold_in(own_key, axis), (), 0, dims[axis]) for axis in range(len(dims))]
    entries = entries.at[tuple(place)].set(low)
    longest = dims.index(max(dims))
    place[longest] = (place[longest] + 1) % dims[longest]
    return entries.at[tuple(place)].set(high)


def level_of(own_key, extent, pieces, least, largest):
    factor_of, own = 1.0, jax.random.fold_in(own_key, 6)
    for dim, shards_of in pieces:
        heights = jnp.exp(jax.random.uniform(jax.random.fold_in(own, dim), (shards_of,), jnp.float32, least / len(pieces), largest / len(pieces)))
        factor_of = factor_of * jnp.repeat(heights, extent[dim] // shards_of).reshape([-1 if axis == dim else 1 for axis in range(len(extent))])
    return factor_of


def scatter_about(stream_key, dims, spread, limit, split=(), held_as=jnp.bfloat16):
    array = spread * jax.random.normal(stream_key, dims, jnp.float32)
    if split:
        array = array * level_of(stream_key, dims, split, -0.22, 0.18)
    return jnp.clip(array, -limit, limit).astype(held_as)


def setup_inputs(seed: int = 0) -> dict:
    keys = jax.random.split(jax.random.key(seed), 11)
    return {
        "current_speeds": scatter_about(keys[0], (2, GRID_NORTHINGS, GRID_EASTINGS, DEPTH_LAYERS), 0.2, 1.2, ((1, 4), (2, 4)), jnp.float32),
        "thermal_anomaly": scatter_about(keys[1], (GRID_NORTHINGS, GRID_EASTINGS, DEPTH_LAYERS), 1.0, 6.0, ((0, 4), (1, 4)), jnp.float32),
        "solute_amounts": scatter_about(keys[2], (NTR, NP, CP, DEPTH_LAYERS), 1.0, 6.0, ((1, 16),), jnp.float32),
        "delayed_link_source": scatter_about(keys[3], (2, 2, NP, CP, DEPTH_LAYERS), 1.0, 6.0, ((0, 2), (2, 16)), jnp.float32),
        "marine_indicator": touch_ends((jax.random.randint(keys[4], (GRID_NORTHINGS, GRID_EASTINGS), 0, 5) < 4).astype(jnp.int32), jax.random.fold_in(keys[4], 1), 0, 1),
        "floor_layer_index": touch_ends(jax.random.randint(keys[5], (GRID_NORTHINGS, GRID_EASTINGS), 1, DEPTH_LAYERS + 1), jax.random.fold_in(keys[5], 1), 1, DEPTH_LAYERS).astype(jnp.int32),
        "holder_rank": jax.vmap(lambda own: jax.random.permutation(own, NP))(jax.random.split(keys[6], NP)).reshape((NP, NP)).astype(jnp.int32),
        "biota_exchange_matrix": scatter_about(keys[7], (NTR, NTR), NTR ** -0.5, 1.5, (), jnp.float32),
        "photic_absorb_share": scatter_about(keys[8], (NTR,), 1.0, 4.0, (), jnp.float32),
        "chroma_loading": scatter_about(keys[9], (NTR,), 0.5, 3.0, (), jnp.float32),
    }


advance_marine = 0.1
spreading = 0.1
viscosity = 0.1
damping = 0.05
heat_gain = 0.2
weight_pull_factor = 0.05
coriolis_scale = 1.0
step_tracer = 0.1
heating_speed = 0.06
uptake_rate = 0.01
water_absorb = (0.02, 0.003)
pigment_absorb = (0.03, 0.004)
surface_light = (40.0, 60.0)


def wet_levels(column_depth):
    levels = jnp.arange(DEPTH_LAYERS, dtype=jnp.int32)
    return (levels < column_depth[..., None]).astype(jnp.float32)


def layer_lookup(pattern):
    row_ids = jnp.arange(DEPTH_LAYERS, dtype=jnp.int32)[:, None]
    col_ids = jnp.arange(DEPTH_LAYERS, dtype=jnp.int32)[None, :]
    if pattern == "above":
        return jnp.where(row_ids < col_ids, 1.0, jnp.where(row_ids == col_ids, 0.5, 0.0)).astype(jnp.float32)
    if pattern == "below":
        return jnp.where(row_ids >= col_ids, 1.0, 0.0).astype(jnp.float32)
    return jnp.where(row_ids < col_ids, 1.0, 0.0).astype(jnp.float32)


def profile_product(values, table):
    return jnp.einsum('...j,jk->...k', values, table, precision=lax.Precision.HIGHEST)


def hydro_balance(thermal_grid):
    return weight_pull_factor * profile_product(thermal_grid, layer_lookup("above"))


def second_derivative_sum(values, submerged_flag):
    return (submerged_flag[1] * (values[1] - values[0]) + submerged_flag[2] * (values[2] - values[0])
            + submerged_flag[3] * (values[3] - values[0]) + submerged_flag[4] * (values[4] - values[0]))


def marine_interior(eastward_speed, northward_speed, thermal_grid, hydraulic_head, submerged_flag, soak_factor, rotation_term):
    eastern_boundary = 0.5 * (eastward_speed[0] + eastward_speed[1]) * submerged_flag[0] * submerged_flag[1]
    western_boundary = 0.5 * (eastward_speed[2] + eastward_speed[0]) * submerged_flag[2] * submerged_flag[0]
    northern_boundary = 0.5 * (northward_speed[0] + northward_speed[3]) * submerged_flag[0] * submerged_flag[3]
    southern_boundary = 0.5 * (northward_speed[4] + northward_speed[0]) * submerged_flag[4] * submerged_flag[0]
    carry_along = (eastern_boundary * 0.5 * (thermal_grid[0] + thermal_grid[1]) - western_boundary * 0.5 * (thermal_grid[2] + thermal_grid[0])
              + northern_boundary * 0.5 * (thermal_grid[0] + thermal_grid[3]) - southern_boundary * 0.5 * (thermal_grid[4] + thermal_grid[0]))
    warming_source = heat_gain * (soak_factor[0] + soak_factor[1])
    warmth_following = submerged_flag[0] * (thermal_grid[0] + advance_marine * (spreading * second_derivative_sum(thermal_grid, submerged_flag) - carry_along + warming_source))
    zonal_push = 0.5 * (submerged_flag[1] * (hydraulic_head[1] - hydraulic_head[0]) + submerged_flag[2] * (hydraulic_head[0] - hydraulic_head[2]))
    merid_push = 0.5 * (submerged_flag[3] * (hydraulic_head[3] - hydraulic_head[0]) + submerged_flag[4] * (hydraulic_head[0] - hydraulic_head[4]))
    zonal_next = submerged_flag[0] * (eastward_speed[0] + advance_marine * (rotation_term * northward_speed[0] - zonal_push
                                                            + viscosity * second_derivative_sum(eastward_speed, submerged_flag) - damping * eastward_speed[0]))
    merid_next = submerged_flag[0] * (northward_speed[0] + advance_marine * (-rotation_term * eastward_speed[0] - merid_push
                                                            + viscosity * second_derivative_sum(northward_speed, submerged_flag) - damping * northward_speed[0]))
    divergence = eastern_boundary - western_boundary + northern_boundary - southern_boundary
    upright_passage = -profile_product(divergence, layer_lookup("below"))
    return warmth_following, zonal_next, merid_next, upright_passage


def solute_interior(solute_amount_status, upright_passage, thermal_grid, radiance_grid, submerged_flag, speed_operator, profit_series):
    empty_level = jnp.zeros_like(solute_amount_status[..., :1])
    upper_passage = jnp.concatenate([empty_level, 0.5 * (solute_amount_status[..., 1:] + solute_amount_status[..., :-1]) * upright_passage[..., 1:]], axis=-1)
    lower_passage = jnp.concatenate([upper_passage[..., 1:], empty_level], axis=-1)
    blending = jnp.einsum('ij,j...->i...', speed_operator, solute_amount_status, precision=lax.Precision.HIGHEST)
    nutrient = solute_amount_status[0]
    saturation = nutrient * nutrient / (1.0 + nutrient * nutrient)
    expansion = uptake_rate * radiance_grid * saturation
    profit_profile = profit_series.reshape((-1,) + (1,) * (solute_amount_status.ndim - 1))
    increment = jnp.exp(heating_speed * thermal_grid) * blending + profit_profile * expansion + lower_passage - upper_passage
    return submerged_flag * (solute_amount_status + step_tracer * increment)


def light_profile(solute_amount_status, submerged_flag, weights):
    chlorophyll = jax.nn.softplus(jnp.einsum('f...,f->...', solute_amount_status, weights, precision=lax.Precision.HIGHEST))
    prefix = layer_lookup("prefix")
    absorbed = []
    radiance_grid = jnp.zeros_like(chlorophyll)
    for band_index in range(2):
        attenuation = water_absorb[band_index] + pigment_absorb[band_index] * chlorophyll
        intensity = surface_light[band_index] * jnp.exp(-profile_product(attenuation, prefix))
        absorbed.append(submerged_flag * intensity * (1.0 - jnp.exp(-attenuation)))
        radiance_grid = radiance_grid + intensity * jnp.exp(-0.5 * attenuation)
    return jnp.stack(absorbed), radiance_grid


def adjoining_cells(values):
    east_side = jnp.roll(values, -1, axis=1)
    west_side = jnp.roll(values, 1, axis=1)
    empty_row = jnp.zeros_like(values[:1])
    north_side = jnp.concatenate([values[1:], empty_row], axis=0)
    south_side = jnp.concatenate([empty_row, values[:-1]], axis=0)
    return (values, east_side, west_side, north_side, south_side)


def to_patches(values):
    fields = values.shape[0]
    return values.reshape(fields, N_PY, CY, N_PX, CX, DEPTH_LAYERS).transpose(0, 1, 3, 2, 4, 5).reshape(fields, NP, CP, DEPTH_LAYERS)


def from_patches(values):
    fields = values.shape[0]
    return values.reshape(fields, N_PY, N_PX, CY, CX, DEPTH_LAYERS).transpose(0, 1, 3, 2, 4, 5).reshape(fields, GRID_NORTHINGS, GRID_EASTINGS, DEPTH_LAYERS)


def owner_inverse(holder_rank):
    indices = jnp.arange(NP, dtype=jnp.int32)
    matches = holder_rank[:, :, None] == indices[None, None, :]
    return jnp.sum(jnp.where(matches, indices[None, :, None], 0), axis=1).astype(jnp.int32)


def to_tracer(patched, inverse):
    fields = patched.shape[0]
    blocks = patched.reshape(fields, NP, NP, SC, DEPTH_LAYERS)
    index_full = jnp.broadcast_to(inverse[None, :, :, None, None], blocks.shape)
    picked = jnp.take_along_axis(blocks, index_full, axis=2)
    return picked.transpose(0, 2, 1, 3, 4).reshape(fields, NP, CP, DEPTH_LAYERS)


def from_tracer(tracer_form, holder_rank):
    fields = tracer_form.shape[0]
    blocks = tracer_form.reshape(fields, NP, NP, SC, DEPTH_LAYERS).transpose(0, 2, 1, 3, 4)
    index_full = jnp.broadcast_to(holder_rank[None, :, :, None, None], blocks.shape)
    picked = jnp.take_along_axis(blocks, index_full, axis=2)
    return picked.reshape(fields, NP, CP, DEPTH_LAYERS)


def reference(current_speeds, thermal_anomaly, solute_amounts, delayed_link_source, marine_indicator, floor_layer_index, holder_rank, biota_exchange_matrix, photic_absorb_share, chroma_loading):
    wet_flow = wet_levels(marine_indicator * floor_layer_index)
    submerged_flag = adjoining_cells(wet_flow)
    inverse = owner_inverse(holder_rank)
    wet_tracer = to_tracer(to_patches(wet_flow[None]), inverse)[0]
    row_ids = jnp.arange(GRID_NORTHINGS, dtype=jnp.int32).astype(jnp.float32)
    rotation_term = (coriolis_scale * (2.0 * (row_ids + 0.5) / GRID_NORTHINGS - 1.0)).reshape(GRID_NORTHINGS, 1, 1)
    eastward_speed = current_speeds[0]
    northward_speed = current_speeds[1]
    thermal_grid = thermal_anomaly
    soak_factor = from_patches(delayed_link_source[0])
    fluxes = delayed_link_source[1]
    solute_amount_status = solute_amounts
    radiance_grid = light_profile(solute_amounts, wet_tracer, chroma_loading)[1]
    for lagged in range(STEPS):
        hydraulic_head = hydro_balance(thermal_grid)
        warmth_following, zonal_next, merid_next, upright_passage = marine_interior(
            adjoining_cells(eastward_speed), adjoining_cells(northward_speed), adjoining_cells(thermal_grid), adjoining_cells(hydraulic_head),
            submerged_flag, soak_factor, rotation_term)
        solute_amount_status = solute_interior(solute_amount_status, fluxes[0], fluxes[1], radiance_grid, wet_tracer, biota_exchange_matrix, photic_absorb_share)
        absorbed, radiance_grid = light_profile(solute_amount_status, wet_tracer, chroma_loading)
        soak_factor = from_patches(from_tracer(absorbed, holder_rank))
        fluxes = to_tracer(to_patches(jnp.stack([upright_passage, warmth_following])), inverse)
        eastward_speed = zonal_next
        northward_speed = merid_next
        thermal_grid = warmth_following
    return jnp.stack([to_patches(soak_factor), fluxes])
```

```python
import functools

import jax
import jax.numpy as jnp
from jax import lax
from jax.experimental import pallas as pl
from jax.experimental.pallas import tpu as pltpu
from jax.sharding import PartitionSpec as P

advance_marine = 0.1
spreading = 0.1
viscosity = 0.1
damping = 0.05
heat_gain = 0.2
weight_pull_factor = 0.05
coriolis_scale = 1.0
step_tracer = 0.1
heating_speed = 0.06
uptake_rate = 0.01
water_absorb = (0.02, 0.003)
pigment_absorb = (0.03, 0.004)
surface_light = (40.0, 60.0)
CY = 16
CX = 32
KEPT = (0, 1, 2, 4, 5)
VMEM = pl.BlockSpec(memory_space=pltpu.VMEM)
SMEM = pl.BlockSpec(memory_space=pltpu.SMEM)
PARAMS = pltpu.CompilerParams(vmem_limit_bytes=40 * 1024 * 1024)


def shape_of(*dims):
    return jax.ShapeDtypeStruct(dims, jnp.float32)


def level_matrix(levels, pattern):
    row = lax.broadcasted_iota(jnp.int32, (levels, levels), 0)
    col = lax.broadcasted_iota(jnp.int32, (levels, levels), 1)
    if pattern == "above":
        m = jnp.where(row < col, 1.0, jnp.where(row == col, 0.5, 0.0))
    elif pattern == "below":
        m = jnp.where(row >= col, 1.0, 0.0)
    else:
        m = jnp.where(row < col, 1.0, 0.0)
    return m.astype(jnp.bfloat16)


def level_sums(x, matrix):
    hi = x.astype(jnp.bfloat16)
    rest = x - hi.astype(jnp.float32)
    mid = rest.astype(jnp.bfloat16)
    low = (rest - mid.astype(jnp.float32)).astype(jnp.bfloat16)
    dot = functools.partial(jnp.dot, preferred_element_type=jnp.float32)
    return dot(hi, matrix) + dot(mid, matrix) + dot(low, matrix)


def softplus(x):
    return jnp.maximum(x, 0.0) + jnp.log1p(jnp.exp(-jnp.abs(x)))


def light(chl, sums, level):
    absorbed, irradiance = [], None
    for water, pigment, surface in zip(water_absorb, pigment_absorb, surface_light):
        fade = jnp.exp(-0.5 * (water + pigment * chl))
        intensity = surface * jnp.exp(-(water * level + pigment * sums))
        absorbed.append(intensity * (1.0 - fade * fade))
        part = intensity * fade
        irradiance = part if irradiance is None else irradiance + part
    return absorbed, irradiance


def saturation(n):
    return n * n / (1.0 + n * n)


def transport(rise_half, y):
    top = rise_half * (y + pltpu.roll(y, 1, 1))
    return pltpu.roll(top, top.shape[1] - 1, 1) - top


def wet_of(depth, shape):
    level = lax.broadcasted_iota(jnp.int32, shape, len(shape) - 1)
    return jnp.where(level < depth, 1.0, 0.0)


def level_of(shape):
    return lax.broadcasted_iota(jnp.int32, shape, len(shape) - 1).astype(jnp.float32)


def half_rise(rise):
    k = lax.broadcasted_iota(jnp.int32, rise.shape, 1)
    return jnp.where(k > 0, 0.5 * rise, 0.0)


def project_kernel(sc, x_ref, w_ref, depth_ref, y_ref, g_ref, chl_ref):
    fields, patches, cols, levels = x_ref.shape

    def one(q, carry):
        values = [x_ref[j, q] for j in range(fields)]
        for k in range(y_ref.shape[0]):
            total = w_ref[k, 0] * values[0]
            for j in range(1, fields):
                total = total + w_ref[k, j] * values[j]
            y_ref[k, q] = total
            if k == 0:
                chl_ref[q] = softplus(total)
        return carry

    lax.fori_loop(0, patches, one, 0)
    flat = (patches * cols, levels)
    chl = chl_ref[...].reshape(flat)
    sums = level_sums(chl, level_matrix(levels, "prefix"))
    _, irradiance = light(chl, sums, level_of(flat))
    n = x_ref[0].reshape(flat)
    g_ref[...] = (uptake_rate * irradiance * saturation(n)).reshape(patches, cols, levels)


def project(comp, tracers, weights, depth):
    fields, patches, strip, levels = tracers.shape
    half = strip // 2
    block = 4
    kinds = weights.shape[0]
    return pl.pallas_call(
        project_kernel,
        grid_spec=pltpu.PrefetchScalarGridSpec(
            num_scalar_prefetch=1,
            grid=(patches // block,),
            in_specs=[
                pl.BlockSpec((fields, block, half, levels), lambda i, c: (0, i, c[0], 0)),
                SMEM,
                pl.BlockSpec((block, half, 1), lambda i, c: (i, 0, 0)),
            ],
            out_specs=[
                pl.BlockSpec((kinds, block, half, levels), lambda i, c: (0, i, 0, 0)),
                pl.BlockSpec((block, half, levels), lambda i, c: (i, 0, 0)),
            ],
            scratch_shapes=[pltpu.VMEM((block, half, levels), jnp.float32)],
        ),
        out_shape=(shape_of(kinds, patches, half, levels), shape_of(patches, half, levels)),
        compiler_params=PARAMS,
        name="project",
    )(comp, tracers, weights, depth)


def first_tracer_kernel(sc, y_ref, g_ref, got_ref, own_ref, depth_ref, share_ref, out_ref):
    patches, cols, levels = g_ref.shape
    first = sc[0] == 0

    def one(q, carry):
        rise = jnp.where(first, got_ref[0, q], own_ref[0, q])
        heat = jnp.where(first, got_ref[1, q], own_ref[1, q])
        warm = jnp.exp(heating_speed * heat)
        wet = wet_of(depth_ref[q], (cols, levels))
        up = half_rise(rise)
        g = g_ref[q]
        for place, k in enumerate(KEPT):
            y = y_ref[k, q]
            change = warm * y_ref[k + 1, q] + share_ref[k] * g + transport(up, y)
            out_ref[q, place] = wet * (y + step_tracer * change)
        return carry

    lax.fori_loop(0, patches, one, 0)


def half_spec(lead, cols, levels):
    zeros = (0,) * len(lead)
    return pl.BlockSpec(lead + (cols, levels), lambda i, c: zeros + (c[0], 0))


def first_tracer(comp, projected, g, got, linked, depth, shares):
    _, patches, half, levels = projected.shape
    return pl.pallas_call(
        first_tracer_kernel,
        grid_spec=pltpu.PrefetchScalarGridSpec(
            num_scalar_prefetch=1,
            grid=(1,),
            in_specs=[VMEM, VMEM, VMEM, half_spec((2, patches), half, levels), VMEM, SMEM],
            out_specs=VMEM,
        ),
        out_shape=shape_of(patches, len(KEPT), half, levels),
        compiler_params=PARAMS,
        name="first_tracer",
    )(comp, projected, g, got, linked, depth, shares)


def ocean_kernel(
    advance, sc, coriolis_ref, u_ref, v_ref, t_ref, north_ref, south_ref, east_ref, west_ref, depth_ref,
    *rest,
):
    rest = list(rest)
    if advance == 1:
        linked_ref, got_ref = rest[:2]
        rest = rest[2:]
    if advance < 3:
        un_ref, vn_ref, tn_ref, rise_ref, row0_ref, row1_ref, col0_ref, col1_ref = rest[:8]
        p_ref, pn_ref, ps_ref, pe_ref, pw_ref, div_ref = rest[8:]
    else:
        face_ref, rise_ref, div_ref = rest
    rows, cols, levels = u_ref.shape
    if advance < 3:
        above = level_matrix(levels, "above")
        p_ref[...] = (
            weight_pull_factor * level_sums(t_ref[...].reshape(rows * cols, levels), above)
        ).reshape(rows, cols, levels)
        for target, source in ((pn_ref, north_ref), (ps_ref, south_ref), (pe_ref, east_ref), (pw_ref, west_ref)):
            target[...] = weight_pull_factor * level_sums(source[2], above)
    place = lax.broadcasted_iota(jnp.int32, (cols, levels), 0)

    def row(y, at):
        shape = (cols, levels)
        north_in = at < rows - 1
        south_in = at > 0

        def around(ref, f):
            x = ref[y]
            e = east_ref[f, pl.ds(y, 1)]
            w = west_ref[f, pl.ds(y, 1)]
            return (
                x,
                jnp.where(place == cols - 1, e, pltpu.roll(x, cols - 1, 0)),
                jnp.where(place == 0, w, pltpu.roll(x, 1, 0)),
                ref[y + 1] if north_in else north_ref[f],
                ref[y - 1] if south_in else south_ref[f],
            )

        wet = [wet_of(depth_ref[i, y], shape) for i in range(5)]
        u = around(u_ref, 0)
        v = around(v_ref, 1)
        east = 0.5 * (u[0] + u[1]) * wet[0] * wet[1]
        west = 0.5 * (u[2] + u[0]) * wet[2] * wet[0]
        north = 0.5 * (v[0] + v[3]) * wet[0] * wet[3]
        south = 0.5 * (v[4] + v[0]) * wet[4] * wet[0]
        div_ref[y] = east - west + north - south
        if advance == 3:
            for i, face in enumerate((east, west, north, south)):
                face_ref[i, y] = face
            return
        t = around(t_ref, 2)
        pe = pe_ref[pl.ds(y, 1)]
        pw = pw_ref[pl.ds(y, 1)]
        p0 = p_ref[y]
        p = (
            p0,
            jnp.where(place == cols - 1, pe, pltpu.roll(p0, cols - 1, 0)),
            jnp.where(place == 0, pw, pltpu.roll(p0, 1, 0)),
            p_ref[y + 1] if north_in else pn_ref[...],
            p_ref[y - 1] if south_in else ps_ref[...],
        )

        def spread(x):
            return (
                wet[1] * (x[1] - x[0]) + wet[2] * (x[2] - x[0])
                + wet[3] * (x[3] - x[0]) + wet[4] * (x[4] - x[0])
            )

        carry_along = 0.5 * (
            east * (t[0] + t[1]) - west * (t[2] + t[0]) + north * (t[0] + t[3]) - south * (t[4] + t[0])
        )
        change = spreading * spread(t) - carry_along
        if advance == 1:
            absorb = jnp.where(
                sc[0] == 0, linked_ref[0, y] + linked_ref[1, y],
                jnp.concatenate([got_ref[0, y], got_ref[1, y]], axis=0),
            )
            change = change + heat_gain * absorb
        zonal = 0.5 * (wet[1] * (p[1] - p[0]) + wet[2] * (p[0] - p[2]))
        merid = 0.5 * (wet[3] * (p[3] - p[0]) + wet[4] * (p[0] - p[4]))
        turn = coriolis_ref[y]
        results = (
            wet[0] * (u[0] + advance_marine * (turn * v[0] - zonal + viscosity * spread(u) - damping * u[0])),
            wet[0] * (v[0] + advance_marine * (-turn * u[0] - merid + viscosity * spread(v) - damping * v[0])),
            wet[0] * (t[0] + advance_marine * change),
        )
        for f, (ref, value) in enumerate(zip((un_ref, vn_ref, tn_ref), results)):
            ref[y] = value
            col0_ref[f, pl.ds(y, 1)] = value[:1]
            col1_ref[f, pl.ds(y, 1)] = value[cols - 1 :]
            if not south_in:
                row0_ref[f] = value
            if not north_in:
                row1_ref[f] = value

    row(0, 0)

    def inner(y, carry):
        row(y, 1)
        return carry

    lax.fori_loop(1, rows - 1, inner, 0)
    row(rows - 1, rows - 1)
    sums = level_sums(div_ref[...].reshape(rows * cols, levels), level_matrix(levels, "below"))
    rise_ref[...] = -sums.reshape(rows, cols, levels)


def ocean(advance, comp, coriolis, fields, halos, depth, linked=None, got=None):
    rows, cols, levels = fields[0].shape
    grid = shape_of(rows, cols, levels)
    count = len(halos[0])
    if advance < 3:
        outs = (
            grid, grid, grid, grid,
            shape_of(3, cols, levels), shape_of(3, cols, levels), shape_of(3, rows, levels), shape_of(3, rows, levels),
        )
        scratch = [
            (rows, cols, levels), (cols, levels), (cols, levels), (rows, levels), (rows, levels), (rows, cols, levels),
        ]
    else:
        outs = (shape_of(4, rows, cols, levels), grid)
        scratch = [(rows, cols, levels)]
    args = [coriolis, *fields, *halos, depth] + ([linked, got] if advance == 1 else [])
    return pl.pallas_call(
        functools.partial(ocean_kernel, advance),
        grid_spec=pltpu.PrefetchScalarGridSpec(
            num_scalar_prefetch=1,
            grid=(1,),
            in_specs=[SMEM] + [VMEM] * (len(args) - 1),
            out_specs=[VMEM] * len(outs),
            scratch_shapes=[pltpu.VMEM(s, jnp.float32) for s in scratch],
        ),
        out_shape=outs,
        compiler_params=PARAMS,
        name=f"ocean{advance}",
    )(comp, *args)


def absorb_kernel(sc, y_ref, t_ref, t2_ref, irr_ref, row0_ref, row1_ref, col0_ref, col1_ref, depth_ref, chl_ref):
    patches, _, cols, levels = y_ref.shape
    flat = (patches * cols, levels)

    def gather(s, carry):
        chl_ref[s] = softplus(y_ref[sc[1 + s], 0])
        return carry

    lax.fori_loop(0, patches, gather, 0)
    chl = chl_ref[...].reshape(flat)
    sums = level_sums(chl, level_matrix(levels, "prefix"))
    absorbed, irradiance = light(chl, sums, level_of(flat))
    wet = wet_of(depth_ref[0], (patches, cols, levels))
    both = (absorbed[0] + absorbed[1]).reshape(patches, cols, levels)
    t2 = t_ref[...] + advance_marine * heat_gain * (wet * both)
    t2_ref[...] = t2
    irr_ref[...] = irradiance.reshape(patches, cols, levels)
    row0_ref[...] = t2_ref[0]
    row1_ref[...] = t2_ref[patches - 1]
    for s in range(patches):
        col0_ref[pl.ds(s, 1)] = t2_ref[s, :1]
        col1_ref[pl.ds(s, 1)] = t2_ref[s, cols - 1 :]


def two_steps_kernel(
    sc, y_ref, t2_ref, irr_ref, t1_ref, r1_ref, r2_ref, depth_ref, share_ref,
    heat_ref, absorbed_ref, a_ref, b_ref, n_ref, chl_ref,
):
    patches, _, cols, levels = y_ref.shape
    flat = (patches * cols, levels)
    whole = (patches, cols, levels)
    prefix = level_matrix(levels, "prefix")

    def second(s, carry):
        owner = sc[1 + s]
        wet = wet_of(depth_ref[0, s], (cols, levels))
        warm = jnp.exp(heating_speed * t1_ref[s])
        up = half_rise(r1_ref[s])
        y = [y_ref[owner, i] for i in range(len(KEPT))]
        g = uptake_rate * irr_ref[s] * saturation(y[3])
        for ref, i, k in ((a_ref, 0, 0), (b_ref, 1, 1), (n_ref, 3, 4)):
            change = warm * y[i + 1] + share_ref[k] * g + transport(up, y[i])
            ref[s] = wet * (y[i] + step_tracer * change)
        chl_ref[s] = softplus(a_ref[s])
        return carry

    lax.fori_loop(0, patches, second, 0)
    chl = chl_ref[...].reshape(flat)
    absorbed, irradiance = light(chl, level_sums(chl, prefix), level_of(flat))
    wet = wet_of(depth_ref[0], whole)
    heat_ref[...] = advance_marine * heat_gain * (wet * (absorbed[0] + absorbed[1]).reshape(whole))
    n_ref[...] = uptake_rate * irradiance.reshape(whole) * saturation(n_ref[...])

    def third(s, carry):
        wet = wet_of(depth_ref[0, s], (cols, levels))
        warm = jnp.exp(heating_speed * t2_ref[s])
        up = half_rise(r2_ref[s])
        a = a_ref[s]
        change = warm * b_ref[s] + share_ref[0] * n_ref[s] + transport(up, a)
        chl_ref[s] = softplus(wet * (a + step_tracer * change))
        return carry

    lax.fori_loop(0, patches, third, 0)
    chl = chl_ref[...].reshape(flat)
    absorbed, _ = light(chl, level_sums(chl, prefix), level_of(flat))
    for band in range(2):
        absorbed_ref[:, band] = wet * absorbed[band].reshape(whole)


def last_heat_kernel(sc, t_ref, north_ref, south_ref, east_ref, west_ref, face_ref, depth_ref, heat_ref, rise_ref, out_ref):
    rows, cols, levels = t_ref.shape
    place = lax.broadcasted_iota(jnp.int32, (cols, levels), 0)
    for y in range(rows):
        wet = [wet_of(depth_ref[i, y], (cols, levels)) for i in range(5)]
        t = t_ref[y]
        e = jnp.where(place == cols - 1, east_ref[pl.ds(y, 1)], pltpu.roll(t, cols - 1, 0))
        w = jnp.where(place == 0, west_ref[pl.ds(y, 1)], pltpu.roll(t, 1, 0))
        n = t_ref[y + 1] if y < rows - 1 else north_ref[...]
        s = t_ref[y - 1] if y > 0 else south_ref[...]
        spread = wet[1] * (e - t) + wet[2] * (w - t) + wet[3] * (n - t) + wet[4] * (s - t)
        carry_along = 0.5 * (
            face_ref[0, y] * (t + e) - face_ref[1, y] * (w + t) + face_ref[2, y] * (t + n) - face_ref[3, y] * (s + t)
        )
        owner = sc[1 + y]
        out_ref[owner, 0] = rise_ref[y]
        out_ref[owner, 1] = wet[0] * (t + advance_marine * (spreading * spread - carry_along)) + heat_ref[y]


def join_kernel(sc, absorbed_ref, flux_ref, other_ref, out_ref):
    patches, _, half, levels = absorbed_ref.shape
    first = sc[0] == 0
    own = pl.multiple_of(sc[0] * half, half)
    rest = pl.multiple_of((1 - sc[0]) * half, half)
    for s in range(patches):
        for f in range(2):
            mine = jnp.where(first, absorbed_ref[s, f], flux_ref[s, f])
            out_ref[f, s, pl.ds(own, half)] = mine
            out_ref[f, s, pl.ds(rest, half)] = other_ref[s, f]


def call(kernel, comp, args, specs, outs, scratch=(), name=None):
    return pl.pallas_call(
        kernel,
        grid_spec=pltpu.PrefetchScalarGridSpec(
            num_scalar_prefetch=1,
            grid=(1,),
            in_specs=specs,
            out_specs=[VMEM] * len(outs),
            scratch_shapes=[pltpu.VMEM(s, jnp.float32) for s in scratch],
        ),
        out_shape=outs,
        compiler_params=PARAMS,
        name=name,
    )(comp, *args)


def exchange_rows(low, high):
    count = lax.axis_size("py")
    north = lax.ppermute(low, "py", [(i + 1, i) for i in range(count - 1)])
    south = lax.ppermute(high, "py", [(i, i + 1) for i in range(count - 1)])
    return north, south


def exchange_cols(low, high):
    count = lax.axis_size("px")
    east = lax.ppermute(low, "px", [((i + 1) % count, i) for i in range(count)])
    west = lax.ppermute(high, "px", [(i, (i + 1) % count) for i in range(count)])
    return east, west


def exchange_half_cols(low, high):
    count = lax.axis_size("px")
    line = [(h % 2) * count + h // 2 for h in range(2 * count)]
    ahead = [(line[h], line[(h + 1) % len(line)]) for h in range(len(line))]
    east = lax.ppermute(low, ("comp", "px"), [(b, a) for a, b in ahead])
    west = lax.ppermute(high, ("comp", "px"), ahead)
    return east, west


def swap(block):
    return lax.ppermute(block, "comp", [(0, 1), (1, 0)])


def pick(blocks, order, axis):
    return jnp.stack(
        [lax.dynamic_index_in_dim(blocks, order[k], axis, keepdims=False) for k in range(order.shape[0])], axis
    )


def table(levels, pattern):
    return level_matrix(levels, pattern).astype(jnp.float32)


def product(values, matrix):
    return jnp.einsum("...j,jk->...k", values, matrix, precision=lax.Precision.HIGHEST)


def general_light(conc, wet, loading):
    chl = jax.nn.softplus(jnp.einsum("f...,f->...", conc, loading, precision=lax.Precision.HIGHEST))
    levels = chl.shape[-1]
    absorbed, irradiance = light(chl, product(chl, table(levels, "prefix")), level_of(chl.shape))
    return wet * jnp.stack(absorbed), irradiance


def general_tracers(conc, rise, heat, irradiance, wet, matrix, share):
    none = jnp.zeros_like(conc[..., :1])
    top = jnp.concatenate([none, 0.5 * (conc[..., 1:] + conc[..., :-1]) * rise[..., 1:]], axis=-1)
    below = jnp.concatenate([top[..., 1:], none], axis=-1)
    mixed = jnp.einsum("ij,j...->i...", matrix, conc, precision=lax.Precision.HIGHEST)
    growth = uptake_rate * irradiance * saturation(conc[0])
    change = (
        jnp.exp(heating_speed * heat) * mixed
        + share.reshape((-1,) + (1,) * (conc.ndim - 1)) * growth + below - top
    )
    return wet * (conc + step_tracer * change)


def general_ocean(u, v, t, absorb, depth, coriolis):
    levels = t.shape[-1]
    fields = jnp.stack([u, v, t])
    north, south = exchange_rows(fields[:, 0], fields[:, -1])
    east, west = exchange_cols(fields[:, :, 0], fields[:, :, -1])
    tall = jnp.concatenate([south[:, None], fields, north[:, None]], axis=1)
    wide = jnp.concatenate([west[:, :, None], fields, east[:, :, None]], axis=2)
    around = (fields, wide[:, :, 2:], wide[:, :, :-2], tall[:, 2:], tall[:, :-2])
    above = table(levels, "above")
    u, v, t = ([x[f] for x in around] for f in range(3))
    p = [weight_pull_factor * product(x, above) for x in t]
    wet = [wet_of(depth[i], t[0].shape) for i in range(5)]

    def spread(x):
        return sum(wet[i] * (x[i] - x[0]) for i in range(1, 5))

    east = 0.5 * (u[0] + u[1]) * wet[0] * wet[1]
    west = 0.5 * (u[2] + u[0]) * wet[2] * wet[0]
    north = 0.5 * (v[0] + v[3]) * wet[0] * wet[3]
    south = 0.5 * (v[4] + v[0]) * wet[4] * wet[0]
    carry_along = 0.5 * (
        east * (t[0] + t[1]) - west * (t[2] + t[0]) + north * (t[0] + t[3]) - south * (t[4] + t[0])
    )
    zonal = 0.5 * (wet[1] * (p[1] - p[0]) + wet[2] * (p[0] - p[2]))
    merid = 0.5 * (wet[3] * (p[3] - p[0]) + wet[4] * (p[0] - p[4]))
    turn = coriolis[:, None, None]
    rise = -product(east - west + north - south, table(levels, "below"))
    return (
        wet[0] * (u[0] + advance_marine * (turn * v[0] - zonal + viscosity * spread(u) - damping * u[0])),
        wet[0] * (v[0] + advance_marine * (-turn * u[0] - merid + viscosity * spread(v) - damping * v[0])),
        wet[0] * (t[0] + advance_marine * (spreading * spread(t) - carry_along + heat_gain * (absorb[0] + absorb[1]))),
        rise,
    )


def general(linked, u, v, t, tracers, depth, tracer_depth, holder_rank, patch_index, coriolis, matrix, share, loading):
    comp_index = lax.axis_index("comp")
    first = comp_index == 0
    fields, patches, strip, levels = tracers.shape
    half = strip // 2
    indices = jnp.arange(patches, dtype=jnp.int32)
    owner_row = lax.dynamic_index_in_dim(holder_rank, patch_index, 0, keepdims=False)
    inverse_row = jnp.sum(jnp.where(owner_row[:, None] == indices[None], indices[:, None], 0), axis=0)

    def own_half(x):
        return lax.dynamic_slice_in_dim(x, comp_index * half, half, x.ndim - 2)

    partner = swap(linked)
    absorb = jnp.where(first, linked, partner)
    flux = own_half(jnp.where(first, partner, linked))
    conc = own_half(tracers)
    wet = wet_of(tracer_depth, conc.shape[1:])
    irradiance = general_light(conc, wet, loading)[1]
    grid = t.shape
    for _ in range(3):
        u, v, t, rise = general_ocean(u, v, t, absorb.reshape((2,) + grid), depth, coriolis)
        conc = general_tracers(conc, flux[0], flux[1], irradiance, wet, matrix, share)
        absorbed, irradiance = general_light(conc, wet, loading)
        both = own_half(pick(jnp.stack([rise, t]).reshape(2, patches, strip, levels), inverse_row, 1))
        send = jnp.concatenate([both, absorbed])
        back = lax.all_to_all(send, ("py", "px"), split_axis=1, concat_axis=1, tiled=True)
        flux = back[:2]
        mine = pick(back[2:], owner_row, 1)
        other = swap(mine)
        absorb = jnp.where(first, jnp.concatenate([mine, other], 2), jnp.concatenate([other, mine], 2))
    other = swap(flux)
    joined = jnp.where(first, jnp.concatenate([flux, other], 2), jnp.concatenate([other, flux], 2))
    return jnp.where(first, absorb, joined)


def shards(
    current_speeds,
    thermal_anomaly,
    solute_amounts,
    delayed_link_source,
    marine_indicator,
    floor_layer_index,
    holder_rank,
    biota_exchange_matrix,
    photic_absorb_share,
    chroma_loading,
):
    comp_index = lax.axis_index("comp")
    row_index = lax.axis_index("py")
    col_index = lax.axis_index("px")
    rows_mesh = lax.axis_size("py")
    cols_mesh = lax.axis_size("px")
    patches = rows_mesh * cols_mesh
    fields, _, columns, levels = solute_amounts.shape
    strip = columns // patches
    half = strip // 2
    patch_index = row_index * cols_mesh + col_index
    first = comp_index == 0

    linked = delayed_link_source.reshape(2, patches, strip, levels)
    tracers = solute_amounts.reshape(fields, patches, strip, levels)
    u0, v0 = current_speeds[0], current_speeds[1]

    column_depth = marine_indicator * floor_layer_index
    wrapped = jnp.concatenate([column_depth[:, -1:], column_depth, column_depth[:, :1]], axis=1)
    padded = jnp.pad(wrapped, ((1, 1), (0, 0)))
    local = lax.dynamic_slice(padded, (row_index * CY, col_index * CX), (CY + 2, CX + 2))
    depth = jnp.stack([local[1:-1, 1:-1], local[1:-1, 2:], local[1:-1, :-2], local[2:, 1:-1], local[:-2, 1:-1]])
    depth = depth[..., None]
    by_strip = (
        column_depth.reshape(rows_mesh, CY, cols_mesh, CX).transpose(0, 2, 1, 3).reshape(patches, patches, strip)
    )
    here = (holder_rank == patch_index)[:, :, None]
    tracer_depth = jnp.sum(jnp.where(here, by_strip, 0), axis=1)
    tracer_depth = lax.dynamic_slice_in_dim(tracer_depth, comp_index * half, half, 1)[..., None]
    owner_row = lax.dynamic_index_in_dim(holder_rank, patch_index, 0, keepdims=False)
    comp = jnp.concatenate([comp_index.astype(jnp.int32)[None], owner_row])
    ys = (row_index * CY + jnp.arange(CY, dtype=jnp.int32)).astype(jnp.float32)
    coriolis = coriolis_scale * (2.0 * (ys + 0.5) / (CY * rows_mesh) - 1.0)

    if half % 8:
        out = general(
            linked, u0, v0, thermal_anomaly, tracers, depth, tracer_depth, holder_rank, patch_index, coriolis,
            biota_exchange_matrix, photic_absorb_share, chroma_loading,
        )
        return out.reshape(1, 2, 1, columns, levels)

    absorb = linked[0] + linked[1]
    sent = jnp.where(
        first, jnp.stack([absorb[:, :half], absorb[:, half:]]), linked[:, :, :half]
    )
    got = swap(sent)
    start = jnp.stack([u0, v0, thermal_anomaly])
    halos0 = exchange_rows(start[:, 0], start[:, -1]) + exchange_cols(start[:, :, 0], start[:, :, -1])

    times = functools.partial(jnp.dot, precision=lax.Precision.HIGHEST)
    unit = (jnp.arange(fields) == 0).astype(jnp.float32)
    chain = [jnp.stack([chroma_loading, unit])]
    for _ in range(3):
        chain.append(times(chain[-1], biota_exchange_matrix))
    weights = jnp.stack([c[0] for c in chain] + [c[1] for c in chain[:3]])
    shares = times(weights, photic_absorb_share)

    projected, g = project(comp, tracers, weights, tracer_depth)
    kept = first_tracer(comp, projected, g, got, linked, tracer_depth, shares)
    arrived = lax.all_to_all(kept, ("py", "px"), split_axis=0, concat_axis=0, tiled=True)

    u1, v1, t1, r1, *edges = ocean(1, comp, coriolis, (u0, v0, thermal_anomaly), halos0, depth, linked, got)
    halos1 = exchange_rows(edges[0], edges[1]) + exchange_cols(edges[2], edges[3])
    u2, v2, t2, r2, *edges = ocean(2, comp, coriolis, (u1, v1, t1), halos1, depth)
    halos2 = exchange_rows(edges[0], edges[1]) + exchange_cols(edges[2], edges[3])
    faces, r3 = ocean(3, comp, coriolis, (u2, v2, t2), halos2, depth)

    patch_half = half_spec((CY,), half, levels)
    depth_half = pl.BlockSpec((5, CY, half, 1), lambda i, c: (0, 0, c[0], 0))
    piece = shape_of(CY, half, levels)
    line = shape_of(half, levels)
    side = shape_of(CY, levels)

    def absorb_step(sc, y_ref, t_ref, depth_ref, *rest):
        absorb_kernel(sc, y_ref, t_ref, *rest[:6], depth_ref, rest[6])

    t2, irr1, *edges = call(
        absorb_step, comp, (arrived, t2, depth), [VMEM, patch_half, depth_half],
        (piece, piece, line, line, side, side), [(CY, half, levels)], "absorb",
    )
    halo = exchange_rows(edges[0], edges[1]) + exchange_half_cols(edges[2], edges[3])
    heat, absorbed = call(
        two_steps_kernel, comp, (arrived, t2, irr1, t1, r1, r2, depth, shares),
        [VMEM, VMEM, VMEM, patch_half, patch_half, patch_half, depth_half, SMEM],
        (piece, shape_of(CY, 2, half, levels)), [(CY, half, levels)] * 4, "two_steps",
    )
    [back] = call(
        last_heat_kernel, comp, (t2, *halo, faces, depth, heat, r3),
        [VMEM] * 5 + [half_spec((4, CY), half, levels), depth_half, VMEM, patch_half],
        (shape_of(patches, 2, half, levels),), (), "last_heat",
    )
    flux = lax.all_to_all(back, ("py", "px"), split_axis=0, concat_axis=0, tiled=True)
    other = swap(jnp.where(first, flux, absorbed))
    [out] = call(
        join_kernel, comp, (absorbed, flux, other), [VMEM] * 3, (shape_of(2, patches, strip, levels),), (), "join"
    )
    return out.reshape(1, 2, 1, columns, levels)


def solution(mesh):
    placed = (
        P(None, "py", "px", None),
        P("py", "px", None),
        P(None, ("py", "px"), None, None),
        P("comp", None, ("py", "px"), None, None),
        P(),
        P(),
        P(),
        P(),
        P(),
        P(),
    )
    return jax.shard_map(
        shards,
        mesh=mesh,
        in_specs=placed,
        out_specs=P("comp", None, ("py", "px"), None, None),
        check_vma=False,
    )
```

```python
import functools

import jax
import jax.numpy as jnp
from jax import lax
from jax.experimental import pallas as pl
from jax.experimental.pallas import tpu as pltpu
from jax.sharding import PartitionSpec as P

advance_marine = 0.1
spreading = 0.1
viscosity = 0.1
damping = 0.05
heat_gain = 0.2
weight_pull_factor = 0.05
coriolis_scale = 1.0
step_tracer = 0.1
heating_speed = 0.06
uptake_rate = 0.01
water_absorb = (0.02, 0.003)
pigment_absorb = (0.03, 0.004)
surface_light = (40.0, 60.0)
CY = 16
CX = 32
KEPT = (0, 1, 2, 4, 5)
SMEM = pl.BlockSpec(memory_space=pltpu.SMEM)
PARAMS = pltpu.CompilerParams(vmem_limit_bytes=24 * 1024 * 1024)
STREAMED = pltpu.CompilerParams(vmem_limit_bytes=60 * 1024 * 1024)


def whole(array):
    zeros = (0,) * len(array.shape)
    return pl.BlockSpec(array.shape, lambda i, c: zeros)


def shape_of(*dims):
    return jax.ShapeDtypeStruct(dims, jnp.float32)


def level_matrix(levels, pattern):
    row = lax.broadcasted_iota(jnp.int32, (levels, levels), 0)
    col = lax.broadcasted_iota(jnp.int32, (levels, levels), 1)
    if pattern == "above":
        m = jnp.where(row < col, 1.0, jnp.where(row == col, 0.5, 0.0))
    elif pattern == "below":
        m = jnp.where(row >= col, 1.0, 0.0)
    else:
        m = jnp.where(row < col, 1.0, 0.0)
    return m.astype(jnp.bfloat16)


def level_sums(x, matrix):
    hi = x.astype(jnp.bfloat16)
    rest = x - hi.astype(jnp.float32)
    mid = rest.astype(jnp.bfloat16)
    low = (rest - mid.astype(jnp.float32)).astype(jnp.bfloat16)
    dot = functools.partial(jnp.dot, preferred_element_type=jnp.float32)
    return dot(hi, matrix) + dot(mid, matrix) + dot(low, matrix)


def softplus(x):
    return jnp.maximum(x, 0.0) + jnp.log1p(jnp.exp(-jnp.abs(x)))


def light(chl, sums, level):
    absorbed, irradiance = [], None
    for water, pigment, surface in zip(water_absorb, pigment_absorb, surface_light):
        fade = jnp.exp(-0.5 * (water + pigment * chl))
        intensity = surface * jnp.exp(-(water * level + pigment * sums))
        absorbed.append(intensity * (1.0 - fade * fade))
        part = intensity * fade
        irradiance = part if irradiance is None else irradiance + part
    return absorbed, irradiance


def saturation(n):
    return n * n / (1.0 + n * n)


def transport(rise_half, y):
    top = rise_half * (y + pltpu.roll(y, 1, 1))
    return pltpu.roll(top, top.shape[1] - 1, 1) - top


def wet_of(depth, shape):
    level = lax.broadcasted_iota(jnp.int32, shape, len(shape) - 1)
    return jnp.where(level < depth, 1.0, 0.0)


def level_of(shape):
    return lax.broadcasted_iota(jnp.int32, shape, len(shape) - 1).astype(jnp.float32)


def half_rise(rise):
    k = lax.broadcasted_iota(jnp.int32, rise.shape, 1)
    return jnp.where(k > 0, 0.5 * rise, 0.0)


def project_kernel(sc, x_ref, w_ref, depth_ref, y_ref, g_ref, chl_ref):
    fields, patches, cols, levels = x_ref.shape

    mixed = [k for k in range(y_ref.shape[0]) if k != 4]

    def one(q, carry):
        value = x_ref[0, q]
        y_ref[4, q] = value
        totals = [w_ref[k, 0] * value for k in mixed]
        for j in range(1, fields):
            value = x_ref[j, q]
            totals = [t + w_ref[k, j] * value for t, k in zip(totals, mixed)]
        for k, total in zip(mixed, totals):
            y_ref[k, q] = total
        chl_ref[q] = softplus(totals[0])
        return carry

    lax.fori_loop(0, patches, one, 0)
    flat = (patches * cols, levels)
    chl = chl_ref[...].reshape(flat)
    sums = level_sums(chl, level_matrix(levels, "prefix"))
    _, irradiance = light(chl, sums, level_of(flat))
    n = x_ref[0].reshape(flat)
    g_ref[...] = (uptake_rate * irradiance * saturation(n)).reshape(patches, cols, levels)


def project(comp, tracers, weights, depth):
    fields, patches, strip, levels = tracers.shape
    half = strip // 2
    block = 4
    kinds = weights.shape[0]
    return pl.pallas_call(
        project_kernel,
        grid_spec=pltpu.PrefetchScalarGridSpec(
            num_scalar_prefetch=1,
            grid=(patches // block,),
            in_specs=[
                pl.BlockSpec((fields, block, half, levels), lambda i, c: (0, i, c[0], 0)),
                SMEM,
                pl.BlockSpec((block, half, 1), lambda i, c: (i, 0, 0)),
            ],
            out_specs=[
                pl.BlockSpec((kinds, block, half, levels), lambda i, c: (0, i, 0, 0)),
                pl.BlockSpec((block, half, levels), lambda i, c: (i, 0, 0)),
            ],
            scratch_shapes=[pltpu.VMEM((block, half, levels), jnp.float32)],
        ),
        out_shape=(shape_of(kinds, patches, half, levels), shape_of(patches, half, levels)),
        compiler_params=STREAMED,
        name="project",
    )(comp, tracers, weights, depth)


def first_tracer_kernel(sc, y_ref, g_ref, got_ref, own_ref, depth_ref, share_ref, out_ref):
    patches, cols, levels = g_ref.shape
    first = sc[0] == 0

    def one(q, carry):
        rise = jnp.where(first, got_ref[0, q], own_ref[0, q])
        heat = jnp.where(first, got_ref[1, q], own_ref[1, q])
        warm = jnp.exp(heating_speed * heat)
        wet = wet_of(depth_ref[q], (cols, levels))
        up = half_rise(rise)
        g = g_ref[q]
        for place, k in enumerate(KEPT):
            y = y_ref[k, q]
            change = warm * y_ref[k + 1, q] + share_ref[k] * g + transport(up, y)
            out_ref[q, place] = wet * (y + step_tracer * change)
        return carry

    lax.fori_loop(0, patches, one, 0, unroll=2)


def half_spec(lead, cols, levels):
    zeros = (0,) * len(lead)
    return pl.BlockSpec(lead + (cols, levels), lambda i, c: zeros + (c[0], 0))


def first_tracer(comp, projected, g, got, linked, depth, shares):
    kinds, patches, half, levels = projected.shape
    block = 4
    return pl.pallas_call(
        first_tracer_kernel,
        grid_spec=pltpu.PrefetchScalarGridSpec(
            num_scalar_prefetch=1,
            grid=(patches // block,),
            in_specs=[
                pl.BlockSpec((kinds, block, half, levels), lambda i, c: (0, i, 0, 0)),
                pl.BlockSpec((block, half, levels), lambda i, c: (i, 0, 0)),
                pl.BlockSpec((2, block, half, levels), lambda i, c: (0, i, 0, 0)),
                pl.BlockSpec((2, block, half, levels), lambda i, c: (0, i, c[0], 0)),
                pl.BlockSpec((block, half, 1), lambda i, c: (i, 0, 0)),
                SMEM,
            ],
            out_specs=pl.BlockSpec((block, len(KEPT), half, levels), lambda i, c: (i, 0, 0, 0)),
        ),
        out_shape=shape_of(patches, len(KEPT), half, levels),
        compiler_params=STREAMED,
        name="first_tracer",
    )(comp, projected, g, got, linked, depth, shares)


def pack_kernel(sc, linked_ref, row0_ref, row1_ref, col0_ref, col1_ref, t0_ref, t1_ref, tc0_ref, tc1_ref,
                sent_ref, low_ref, high_ref, left_ref, right_ref):
    _, strips, strip, levels = linked_ref.shape
    half = strip // 2

    @pl.when(sc[0] == 0)
    def _():
        for part in range(2):
            cols = slice(part * half, (part + 1) * half)
            sent_ref[part] = linked_ref[0, :, cols] + linked_ref[1, :, cols]

    @pl.when(sc[0] != 0)
    def _():
        sent_ref[...] = linked_ref[:, :, :half]

    last = col1_ref.shape[2] - 1
    for f in range(2):
        low_ref[f] = row0_ref[f, 0]
        high_ref[f] = row1_ref[f, 0]
        left_ref[f] = col0_ref[f, :, 0]
        right_ref[f] = col1_ref[f, :, last]
    low_ref[2] = t0_ref[0]
    high_ref[2] = t1_ref[0]
    left_ref[2] = tc0_ref[:, 0]
    right_ref[2] = tc1_ref[:, last]


def pack(comp, linked, speeds, heat):
    _, strips, strip, levels = linked.shape
    rows, cols, _ = heat.shape
    outs = (
        shape_of(2, strips, strip // 2, levels), shape_of(3, cols, levels), shape_of(3, cols, levels),
        shape_of(3, rows, levels), shape_of(3, rows, levels),
    )
    edge = min(8, cols)
    return pl.pallas_call(
        pack_kernel,
        grid_spec=pltpu.PrefetchScalarGridSpec(
            num_scalar_prefetch=1,
            grid=(1,),
            in_specs=[
                whole(linked),
                pl.BlockSpec((2, 1, cols, levels), lambda i, c: (0, 0, 0, 0)),
                pl.BlockSpec((2, 1, cols, levels), lambda i, c: (0, rows - 1, 0, 0)),
                pl.BlockSpec((2, rows, edge, levels), lambda i, c: (0, 0, 0, 0)),
                pl.BlockSpec((2, rows, edge, levels), lambda i, c: (0, 0, cols // edge - 1, 0)),
                pl.BlockSpec((1, cols, levels), lambda i, c: (0, 0, 0)),
                pl.BlockSpec((1, cols, levels), lambda i, c: (rows - 1, 0, 0)),
                pl.BlockSpec((rows, edge, levels), lambda i, c: (0, 0, 0)),
                pl.BlockSpec((rows, edge, levels), lambda i, c: (0, cols // edge - 1, 0)),
            ],
            out_specs=[whole(o) for o in outs],
        ),
        out_shape=outs,
        compiler_params=STREAMED,
        name="pack",
    )(comp, linked, speeds, speeds, speeds, speeds, heat, heat, heat, heat)


def ocean_kernel(
    advance, sc, coriolis_ref, speed_ref, t_ref, north_ref, south_ref, east_ref, west_ref, depth_ref,
    *rest,
):
    rest = list(rest)
    u_ref, v_ref = speed_ref.at[0], speed_ref.at[1]
    if advance == 1:
        linked_ref, got_ref = rest[:2]
        rest = rest[2:]
    next_ref, tn_ref, rise_ref = rest[:3]
    edge_refs = rest[3:7] if advance == 1 else ()
    un_ref, vn_ref = next_ref.at[0], next_ref.at[1]
    p_ref, pn_ref, ps_ref, pe_ref, pw_ref, div_ref = rest[-6:]
    rows, cols, levels = t_ref.shape
    above = level_matrix(levels, "above")
    p_ref[...] = (
        weight_pull_factor * level_sums(t_ref[...].reshape(rows * cols, levels), above)
    ).reshape(rows, cols, levels)
    for target, source in ((pn_ref, north_ref), (ps_ref, south_ref), (pe_ref, east_ref), (pw_ref, west_ref)):
        target[...] = weight_pull_factor * level_sums(source[2], above)
    lanes = min(128, levels)
    place = lax.broadcasted_iota(jnp.int32, (cols, lanes), 0)
    at_east, at_west = place == cols - 1, place == 0

    def piece(y, at, lane):
        north_in = at < rows - 1
        south_in = at > 0
        part = slice(lane, lane + lanes)
        level = lane + lax.broadcasted_iota(jnp.int32, (cols, lanes), 1)

        def around(x, e, w, n, s):
            return (
                x, jnp.where(at_east, e, pltpu.roll(x, cols - 1, 0)), jnp.where(at_west, w, pltpu.roll(x, 1, 0)), n, s
            )

        def field(ref, f):
            return around(
                ref[y, :, part],
                east_ref[f, pl.ds(y, 1)][:, part],
                west_ref[f, pl.ds(y, 1)][:, part],
                ref[y + 1, :, part] if north_in else north_ref[f, :, part],
                ref[y - 1, :, part] if south_in else south_ref[f, :, part],
            )

        wet = [jnp.where(level < depth_ref[i, y], 1.0, 0.0) for i in range(5)]
        u = field(u_ref, 0)
        v = field(v_ref, 1)
        own = 0.5 * wet[0]
        east = (u[0] + u[1]) * (own * wet[1])
        west = (u[2] + u[0]) * (own * wet[2])
        north = (v[0] + v[3]) * (own * wet[3])
        south = (v[4] + v[0]) * (own * wet[4])
        div_ref[y, :, part] = east - west + north - south
        t = field(t_ref, 2)
        p = around(
            p_ref[y, :, part],
            pe_ref[pl.ds(y, 1)][:, part],
            pw_ref[pl.ds(y, 1)][:, part],
            p_ref[y + 1, :, part] if north_in else pn_ref[:, part],
            p_ref[y - 1, :, part] if south_in else ps_ref[:, part],
        )
        wets = wet[1] + wet[2] + wet[3] + wet[4]

        def spread(x):
            return wet[1] * x[1] + wet[2] * x[2] + wet[3] * x[3] + wet[4] * x[4] - wets * x[0]

        carry_along = 0.5 * (
            east * (t[0] + t[1]) - west * (t[2] + t[0]) + north * (t[0] + t[3]) - south * (t[4] + t[0])
        )
        change = spreading * spread(t) - carry_along
        if advance == 1:
            halves = [got_ref[i, y, :, part] for i in range(2)]
            absorb = jnp.where(
                sc[0] == 0, linked_ref[0, y, :, part] + linked_ref[1, y, :, part], jnp.concatenate(halves, axis=0)
            )
            change = change + heat_gain * absorb
        zonal = 0.5 * (wet[1] * (p[1] - p[0]) + wet[2] * (p[0] - p[2]))
        merid = 0.5 * (wet[3] * (p[3] - p[0]) + wet[4] * (p[0] - p[4]))
        turn = coriolis_ref[y]
        results = (
            wet[0] * (u[0] + advance_marine * (turn * v[0] - zonal + viscosity * spread(u) - damping * u[0])),
            wet[0] * (v[0] + advance_marine * (-turn * u[0] - merid + viscosity * spread(v) - damping * v[0])),
            wet[0] * (t[0] + advance_marine * change),
        )
        for f, (ref, value) in enumerate(zip((un_ref, vn_ref, tn_ref), results)):
            ref[y, :, part] = value

    def row(y, at):
        for lane in range(0, levels, lanes):
            piece(y, at, lane)
        if edge_refs:
            for f, ref in enumerate((un_ref, vn_ref, tn_ref)):
                edge_refs[2][f, pl.ds(y, 1)] = ref[y, :1]
                edge_refs[3][f, pl.ds(y, 1)] = ref[y, cols - 1 :]

    row(0, 0)

    def inner(y, carry):
        row(y, 1)
        return carry

    lax.fori_loop(1, rows - 1, inner, 0)
    row(rows - 1, rows - 1)
    if edge_refs:
        for f, ref in enumerate((un_ref, vn_ref, tn_ref)):
            edge_refs[0][f] = ref[0]
            edge_refs[1][f] = ref[rows - 1]
    sums = level_sums(div_ref[...].reshape(rows * cols, levels), level_matrix(levels, "below"))
    rise_ref[...] = -sums.reshape(rows, cols, levels)


def ocean(advance, comp, coriolis, speeds, heat, halos, depth, linked=None, got=None):
    rows, cols, levels = heat.shape
    grid = shape_of(rows, cols, levels)
    outs = (shape_of(2, rows, cols, levels), grid, grid)
    if advance == 1:
        outs += (
            shape_of(3, cols, levels), shape_of(3, cols, levels), shape_of(3, rows, levels), shape_of(3, rows, levels),
        )
    scratch = [
        (rows, cols, levels), (cols, levels), (cols, levels), (rows, levels), (rows, levels), (rows, cols, levels),
    ]
    args = [coriolis, speeds, heat, *halos, depth] + ([linked, got] if advance == 1 else [])
    return pl.pallas_call(
        functools.partial(ocean_kernel, advance),
        grid_spec=pltpu.PrefetchScalarGridSpec(
            num_scalar_prefetch=1,
            grid=(1,),
            in_specs=[SMEM] + [whole(a) for a in args[1:]],
            out_specs=[whole(o) for o in outs],
            scratch_shapes=[pltpu.VMEM(s, jnp.float32) for s in scratch],
        ),
        out_shape=outs,
        compiler_params=STREAMED if advance == 1 else PARAMS,
        name=f"ocean{advance}",
    )(comp, *args)


def absorb_kernel(
    sc, y_ref, t_ref, speed_ref, depth_ref, t2_ref, irr_ref, row0_ref, row1_ref, col0_ref, col1_ref, chl_ref
):
    rows, cols, levels = t_ref.shape
    flat = (rows * cols, levels)

    def gather(s, carry):
        chl_ref[s] = softplus(y_ref[sc[1 + s], 0])
        return carry

    lax.fori_loop(0, rows, gather, 0, unroll=2)
    chl = chl_ref[...].reshape(flat)
    sums = level_sums(chl, level_matrix(levels, "prefix"))
    absorbed, irradiance = light(chl, sums, level_of(flat))
    wet = wet_of(depth_ref[0], t_ref.shape)
    both = (absorbed[0] + absorbed[1]).reshape(t_ref.shape)
    t2_ref[...] = t_ref[...] + advance_marine * heat_gain * (wet * both)
    irr_ref[...] = irradiance.reshape(t_ref.shape)
    for f, ref in enumerate((speed_ref.at[0], speed_ref.at[1], t2_ref)):
        row0_ref[f] = ref[0]
        row1_ref[f] = ref[rows - 1]
        for y in range(rows):
            col0_ref[f, pl.ds(y, 1)] = ref[y, :1]
            col1_ref[f, pl.ds(y, 1)] = ref[y, cols - 1 :]


def second_kernel(
    sc, y_ref, irr_ref, t1_ref, r1_ref, depth_ref, share_ref, heat_ref, a_ref, b_ref, g_ref, n_ref, chl_ref
):
    patches, _, cols, levels = y_ref.shape
    flat = (patches * cols, levels)
    whole = (patches, cols, levels)

    def one(s, carry):
        owner = sc[1 + s]
        wet = wet_of(depth_ref[0, s], (cols, levels))
        warm = jnp.exp(heating_speed * t1_ref[s])
        up = half_rise(r1_ref[s])
        y = [y_ref[owner, i] for i in range(len(KEPT))]
        g = uptake_rate * irr_ref[s] * saturation(y[3])
        for ref, i, k in ((a_ref, 0, 0), (b_ref, 1, 1), (n_ref, 3, 4)):
            change = warm * y[i + 1] + share_ref[k] * g + transport(up, y[i])
            ref[s] = wet * (y[i] + step_tracer * change)
        chl_ref[s] = softplus(a_ref[s])
        return carry

    lax.fori_loop(0, patches, one, 0, unroll=4)
    chl = chl_ref[...].reshape(flat)
    absorbed, irradiance = light(chl, level_sums(chl, level_matrix(levels, "prefix")), level_of(flat))
    wet = wet_of(depth_ref[0], whole)
    heat_ref[...] = advance_marine * heat_gain * (wet * (absorbed[0] + absorbed[1]).reshape(whole))
    g_ref[...] = uptake_rate * irradiance.reshape(whole) * saturation(n_ref[...])


def third_kernel(sc, a_ref, b_ref, g_ref, t2_ref, r2_ref, depth_ref, share_ref, band_ref, chl_ref):
    patches, cols, levels = a_ref.shape
    flat = (patches * cols, levels)
    whole = (patches, cols, levels)

    def one(s, carry):
        wet = wet_of(depth_ref[0, s], (cols, levels))
        warm = jnp.exp(heating_speed * t2_ref[s])
        a = a_ref[s]
        change = warm * b_ref[s] + share_ref[0] * g_ref[s] + transport(half_rise(r2_ref[s]), a)
        chl_ref[s] = softplus(wet * (a + step_tracer * change))
        return carry

    lax.fori_loop(0, patches, one, 0, unroll=4)
    chl = chl_ref[...].reshape(flat)
    absorbed, _ = light(chl, level_sums(chl, level_matrix(levels, "prefix")), level_of(flat))
    wet = wet_of(depth_ref[0], whole)
    for band in range(2):
        band_ref[:, band] = wet * absorbed[band].reshape(whole)


def last_ocean_kernel(
    sc, speed_ref, t_ref, north_ref, south_ref, east_ref, west_ref, depth_ref, heat_ref, out_ref, div_ref
):
    rows, cols, levels = t_ref.shape
    place = lax.broadcasted_iota(jnp.int32, (cols, levels), 0)
    sources = (speed_ref.at[0], speed_ref.at[1], t_ref)
    for y in range(rows):
        wet = [wet_of(depth_ref[i, y], (cols, levels)) for i in range(5)]

        def east_of(f):
            return jnp.where(place == cols - 1, east_ref[f, pl.ds(y, 1)], pltpu.roll(sources[f][y], cols - 1, 0))

        def west_of(f):
            return jnp.where(place == 0, west_ref[f, pl.ds(y, 1)], pltpu.roll(sources[f][y], 1, 0))

        def north_of(f):
            return sources[f][y + 1] if y < rows - 1 else north_ref[f]

        def south_of(f):
            return sources[f][y - 1] if y > 0 else south_ref[f]

        u, v, t = (ref[y] for ref in sources)
        own = 0.5 * wet[0]
        east = (u + east_of(0)) * (own * wet[1])
        west = (west_of(0) + u) * (own * wet[2])
        north = (v + north_of(1)) * (own * wet[3])
        south = (south_of(1) + v) * (own * wet[4])
        div_ref[y] = east - west + north - south
        e, w, n, s = east_of(2), west_of(2), north_of(2), south_of(2)
        spread = wet[1] * (e - t) + wet[2] * (w - t) + wet[3] * (n - t) + wet[4] * (s - t)
        carry_along = 0.5 * (east * (t + e) - west * (w + t) + north * (t + n) - south * (s + t))
        change = spreading * spread - carry_along
        out_ref[sc[1 + y], 1] = wet[0] * (t + advance_marine * change) + heat_ref[y]
    sums = level_sums(div_ref[...].reshape(rows * cols, levels), level_matrix(levels, "below"))
    div_ref[...] = -sums.reshape(rows, cols, levels)
    for y in range(rows):
        out_ref[sc[1 + y], 0] = div_ref[y]


def join_kernel(sc, absorbed_ref, flux_ref, other_ref, out_ref):
    patches, _, half, levels = absorbed_ref.shape
    first = sc[0] == 0
    own = pl.multiple_of(sc[0] * half, half)
    rest = pl.multiple_of((1 - sc[0]) * half, half)
    for s in range(patches):
        for f in range(2):
            out_ref[f, s, pl.ds(own, half)] = jnp.where(first, absorbed_ref[s, f], flux_ref[s, f])
            out_ref[f, s, pl.ds(rest, half)] = other_ref[s, f]


def call(kernel, comp, args, specs, outs, scratch=(), name=None):
    return pl.pallas_call(
        kernel,
        grid_spec=pltpu.PrefetchScalarGridSpec(
            num_scalar_prefetch=1,
            grid=(1,),
            in_specs=[spec or whole(a) for spec, a in zip(specs, args)],
            out_specs=[whole(o) for o in outs],
            scratch_shapes=[pltpu.VMEM(s, jnp.float32) for s in scratch],
        ),
        out_shape=outs,
        compiler_params=PARAMS,
        name=name,
    )(comp, *args)


def exchange_rows(low, high):
    count = lax.axis_size("py")
    north = lax.ppermute(low, "py", [(i + 1, i) for i in range(count - 1)])
    south = lax.ppermute(high, "py", [(i, i + 1) for i in range(count - 1)])
    return north, south


def exchange_cols(low, high):
    count = lax.axis_size("px")
    east = lax.ppermute(low, "px", [((i + 1) % count, i) for i in range(count)])
    west = lax.ppermute(high, "px", [(i, (i + 1) % count) for i in range(count)])
    return east, west


def exchange_half_cols(low, high):
    count = lax.axis_size("px")
    line = [(h % 2) * count + h // 2 for h in range(2 * count)]
    ahead = [(line[h], line[(h + 1) % len(line)]) for h in range(len(line))]
    east = lax.ppermute(low, ("comp", "px"), [(b, a) for a, b in ahead])
    west = lax.ppermute(high, ("comp", "px"), ahead)
    return east, west


def to_owners(blocks):
    return lax.all_to_all(blocks, ("py", "px"), split_axis=0, concat_axis=0, tiled=True)


def swap(block):
    return lax.ppermute(block, "comp", [(0, 1), (1, 0)])


def pick(blocks, order, axis):
    return jnp.stack(
        [lax.dynamic_index_in_dim(blocks, order[k], axis, keepdims=False) for k in range(order.shape[0])], axis
    )


def table(levels, pattern):
    return level_matrix(levels, pattern).astype(jnp.float32)


def product(values, matrix):
    return jnp.einsum("...j,jk->...k", values, matrix, precision=lax.Precision.HIGHEST)


def general_light(conc, wet, loading):
    chl = jax.nn.softplus(jnp.einsum("f...,f->...", conc, loading, precision=lax.Precision.HIGHEST))
    levels = chl.shape[-1]
    absorbed, irradiance = light(chl, product(chl, table(levels, "prefix")), level_of(chl.shape))
    return wet * jnp.stack(absorbed), irradiance


def general_tracers(conc, rise, heat, irradiance, wet, matrix, share):
    none = jnp.zeros_like(conc[..., :1])
    top = jnp.concatenate([none, 0.5 * (conc[..., 1:] + conc[..., :-1]) * rise[..., 1:]], axis=-1)
    below = jnp.concatenate([top[..., 1:], none], axis=-1)
    mixed = jnp.einsum("ij,j...->i...", matrix, conc, precision=lax.Precision.HIGHEST)
    growth = uptake_rate * irradiance * saturation(conc[0])
    change = (
        jnp.exp(heating_speed * heat) * mixed
        + share.reshape((-1,) + (1,) * (conc.ndim - 1)) * growth + below - top
    )
    return wet * (conc + step_tracer * change)


def general_ocean(u, v, t, absorb, depth, coriolis):
    levels = t.shape[-1]
    fields = jnp.stack([u, v, t])
    north, south = exchange_rows(fields[:, 0], fields[:, -1])
    east, west = exchange_cols(fields[:, :, 0], fields[:, :, -1])
    tall = jnp.concatenate([south[:, None], fields, north[:, None]], axis=1)
    wide = jnp.concatenate([west[:, :, None], fields, east[:, :, None]], axis=2)
    around = (fields, wide[:, :, 2:], wide[:, :, :-2], tall[:, 2:], tall[:, :-2])
    above = table(levels, "above")
    u, v, t = ([x[f] for x in around] for f in range(3))
    p = [weight_pull_factor * product(x, above) for x in t]
    wet = [wet_of(depth[i], t[0].shape) for i in range(5)]

    def spread(x):
        return sum(wet[i] * (x[i] - x[0]) for i in range(1, 5))

    east = 0.5 * (u[0] + u[1]) * wet[0] * wet[1]
    west = 0.5 * (u[2] + u[0]) * wet[2] * wet[0]
    north = 0.5 * (v[0] + v[3]) * wet[0] * wet[3]
    south = 0.5 * (v[4] + v[0]) * wet[4] * wet[0]
    carry_along = 0.5 * (
        east * (t[0] + t[1]) - west * (t[2] + t[0]) + north * (t[0] + t[3]) - south * (t[4] + t[0])
    )
    zonal = 0.5 * (wet[1] * (p[1] - p[0]) + wet[2] * (p[0] - p[2]))
    merid = 0.5 * (wet[3] * (p[3] - p[0]) + wet[4] * (p[0] - p[4]))
    turn = coriolis[:, None, None]
    rise = -product(east - west + north - south, table(levels, "below"))
    return (
        wet[0] * (u[0] + advance_marine * (turn * v[0] - zonal + viscosity * spread(u) - damping * u[0])),
        wet[0] * (v[0] + advance_marine * (-turn * u[0] - merid + viscosity * spread(v) - damping * v[0])),
        wet[0] * (t[0] + advance_marine * (spreading * spread(t) - carry_along + heat_gain * (absorb[0] + absorb[1]))),
        rise,
    )


def general(linked, u, v, t, tracers, depth, tracer_depth, holder_rank, patch_index, coriolis, matrix, share, loading):
    comp_index = lax.axis_index("comp")
    first = comp_index == 0
    fields, patches, strip, levels = tracers.shape
    half = strip // 2
    indices = jnp.arange(patches, dtype=jnp.int32)
    owner_row = lax.dynamic_index_in_dim(holder_rank, patch_index, 0, keepdims=False)
    inverse_row = jnp.sum(jnp.where(owner_row[:, None] == indices[None], indices[:, None], 0), axis=0)

    def own_half(x):
        return lax.dynamic_slice_in_dim(x, comp_index * half, half, x.ndim - 2)

    partner = swap(linked)
    absorb = jnp.where(first, linked, partner)
    flux = own_half(jnp.where(first, partner, linked))
    conc = own_half(tracers)
    wet = wet_of(tracer_depth, conc.shape[1:])
    irradiance = general_light(conc, wet, loading)[1]
    grid = t.shape
    for _ in range(3):
        u, v, t, rise = general_ocean(u, v, t, absorb.reshape((2,) + grid), depth, coriolis)
        conc = general_tracers(conc, flux[0], flux[1], irradiance, wet, matrix, share)
        absorbed, irradiance = general_light(conc, wet, loading)
        both = own_half(pick(jnp.stack([rise, t]).reshape(2, patches, strip, levels), inverse_row, 1))
        send = jnp.concatenate([both, absorbed])
        back = lax.all_to_all(send, ("py", "px"), split_axis=1, concat_axis=1, tiled=True)
        flux = back[:2]
        mine = pick(back[2:], owner_row, 1)
        other = swap(mine)
        absorb = jnp.where(first, jnp.concatenate([mine, other], 2), jnp.concatenate([other, mine], 2))
    other = swap(flux)
    joined = jnp.where(first, jnp.concatenate([flux, other], 2), jnp.concatenate([other, flux], 2))
    return jnp.where(first, absorb, joined)


def shards(
    current_speeds,
    thermal_anomaly,
    solute_amounts,
    delayed_link_source,
    marine_indicator,
    floor_layer_index,
    holder_rank,
    biota_exchange_matrix,
    photic_absorb_share,
    chroma_loading,
):
    comp_index = lax.axis_index("comp")
    row_index = lax.axis_index("py")
    col_index = lax.axis_index("px")
    rows_mesh = lax.axis_size("py")
    cols_mesh = lax.axis_size("px")
    patches = rows_mesh * cols_mesh
    fields, _, columns, levels = solute_amounts.shape
    strip = columns // patches
    half = strip // 2
    patch_index = row_index * cols_mesh + col_index
    first = comp_index == 0

    linked = delayed_link_source.reshape(2, patches, strip, levels)
    tracers = solute_amounts.reshape(fields, patches, strip, levels)
    u0, v0 = current_speeds[0], current_speeds[1]

    column_depth = marine_indicator * floor_layer_index
    wrapped = jnp.concatenate([column_depth[:, -1:], column_depth, column_depth[:, :1]], axis=1)
    padded = jnp.pad(wrapped, ((1, 1), (0, 0)))
    local = lax.dynamic_slice(padded, (row_index * CY, col_index * CX), (CY + 2, CX + 2))
    depth = jnp.stack([local[1:-1, 1:-1], local[1:-1, 2:], local[1:-1, :-2], local[2:, 1:-1], local[:-2, 1:-1]])
    depth = depth[..., None]
    by_strip = (
        column_depth.reshape(rows_mesh, CY, cols_mesh, CX).transpose(0, 2, 1, 3).reshape(patches, patches, strip)
    )
    here = (holder_rank == patch_index)[:, :, None]
    tracer_depth = jnp.sum(jnp.where(here, by_strip, 0), axis=1)
    tracer_depth = lax.dynamic_slice_in_dim(tracer_depth, comp_index * half, half, 1)[..., None]
    owner_row = lax.dynamic_index_in_dim(holder_rank, patch_index, 0, keepdims=False)
    comp = jnp.concatenate([comp_index.astype(jnp.int32)[None], owner_row])
    ys = (row_index * CY + jnp.arange(CY, dtype=jnp.int32)).astype(jnp.float32)
    coriolis = coriolis_scale * (2.0 * (ys + 0.5) / (CY * rows_mesh) - 1.0)

    if half % 8:
        out = general(
            linked, u0, v0, thermal_anomaly, tracers, depth, tracer_depth, holder_rank, patch_index, coriolis,
            biota_exchange_matrix, photic_absorb_share, chroma_loading,
        )
        return out.reshape(1, 2, 1, columns, levels)

    sent, *edges = pack(comp, linked, current_speeds, thermal_anomaly)
    got = swap(sent)
    times = functools.partial(jnp.dot, precision=lax.Precision.HIGHEST)
    unit = (jnp.arange(fields) == 0).astype(jnp.float32)
    chain = [jnp.stack([chroma_loading, unit])]
    for _ in range(3):
        chain.append(times(chain[-1], biota_exchange_matrix))
    weights = jnp.stack([c[0] for c in chain] + [c[1] for c in chain[:3]])
    shares = times(weights, photic_absorb_share)

    projected, g = project(comp, tracers, weights, tracer_depth)
    edges, projected, g = lax.optimization_barrier((edges, projected, g))
    halos0 = exchange_rows(edges[0], edges[1]) + exchange_cols(edges[2], edges[3])
    kept = first_tracer(comp, projected, g, got, linked, tracer_depth, shares)
    kept, halos0 = lax.optimization_barrier((kept, halos0))
    arrived = to_owners(kept)

    speeds1, t1, r1, *edges = ocean(1, comp, coriolis, current_speeds, thermal_anomaly, halos0, depth, linked, got)
    halos1 = exchange_rows(edges[0], edges[1]) + exchange_cols(edges[2], edges[3])
    speeds2, t2, r2 = ocean(2, comp, coriolis, speeds1, t1, halos1, depth)
    arrived, speeds2, t2 = lax.optimization_barrier((arrived, speeds2, t2))

    patch_half = half_spec((CY,), half, levels)
    speeds_half = half_spec((2, CY), half, levels)
    depth_half = pl.BlockSpec((5, CY, half, 1), lambda i, c: (0, 0, c[0], 0))
    piece = shape_of(CY, half, levels)
    scratch = (CY, half, levels)
    line = shape_of(3, half, levels)
    side = shape_of(3, CY, levels)

    t2, irr1, *edges = call(
        absorb_kernel, comp, (arrived, t2, speeds2, depth), [None, patch_half, speeds_half, depth_half],
        (piece, piece, line, line, side, side), [scratch], "absorb",
    )
    halos2 = exchange_rows(edges[0], edges[1]) + exchange_half_cols(edges[2], edges[3])
    heat, a, b, g = call(
        second_kernel, comp, (arrived, irr1, t1, r1, depth, shares),
        [None, None, patch_half, patch_half, depth_half, SMEM],
        (piece,) * 4, [scratch] * 2, "second",
    )
    [back] = call(
        last_ocean_kernel, comp, (speeds2, t2, *halos2, depth, heat),
        [speeds_half] + [None] * 5 + [depth_half, None],
        (shape_of(patches, 2, half, levels),), [scratch], "last_ocean",
    )
    flux = to_owners(back)
    [absorbed] = call(
        third_kernel, comp, (a, b, g, t2, r2, depth, shares),
        [None] * 4 + [patch_half, depth_half, SMEM], (shape_of(CY, 2, half, levels),), [scratch], "third",
    )
    other = swap(jnp.where(first, flux, absorbed))
    [out] = call(
        join_kernel, comp, (absorbed, flux, other), [None] * 3, (shape_of(2, patches, strip, levels),), (), "join"
    )
    return out.reshape(1, 2, 1, columns, levels)


def solution(mesh):
    placed = (
        P(None, "py", "px", None),
        P("py", "px", None),
        P(None, ("py", "px"), None, None),
        P("comp", None, ("py", "px"), None, None),
        P(),
        P(),
        P(),
        P(),
        P(),
        P(),
    )
    return jax.shard_map(
        shards,
        mesh=mesh,
        in_specs=placed,
        out_specs=P("comp", None, ("py", "px"), None, None),
        check_vma=False,
    )
```

```python
import functools

import jax
import jax.numpy as jnp
from jax import lax
from jax.experimental import pallas as pl
from jax.experimental.pallas import tpu as pltpu
from jax.sharding import PartitionSpec as P

advance_marine = 0.1
spreading = 0.1
viscosity = 0.1
damping = 0.05
heat_gain = 0.2
weight_pull_factor = 0.05
coriolis_scale = 1.0
step_tracer = 0.1
heating_speed = 0.06
uptake_rate = 0.01
water_absorb = (0.02, 0.003)
pigment_absorb = (0.03, 0.004)
surface_light = (40.0, 60.0)
CY = 16
CX = 32
KEPT = (0, 1, 2, 4, 5)
SMEM = pl.BlockSpec(memory_space=pltpu.SMEM)
PARAMS = pltpu.CompilerParams(vmem_limit_bytes=24 * 1024 * 1024)
PROJECT = pltpu.CompilerParams(vmem_limit_bytes=57 * 1024 * 1024)
STREAMED = pltpu.CompilerParams(vmem_limit_bytes=60 * 1024 * 1024)


def whole(array):
    zeros = (0,) * len(array.shape)
    return pl.BlockSpec(array.shape, lambda i, c: zeros)


def shape_of(*dims):
    return jax.ShapeDtypeStruct(dims, jnp.float32)


def level_matrix(levels, pattern):
    row = lax.broadcasted_iota(jnp.int32, (levels, levels), 0)
    col = lax.broadcasted_iota(jnp.int32, (levels, levels), 1)
    if pattern == "above":
        m = jnp.where(row < col, 1.0, jnp.where(row == col, 0.5, 0.0))
    elif pattern == "below":
        m = jnp.where(row >= col, 1.0, 0.0)
    else:
        m = jnp.where(row < col, 1.0, 0.0)
    return m.astype(jnp.bfloat16)


def level_sums(x, matrix):
    hi = x.astype(jnp.bfloat16)
    rest = x - hi.astype(jnp.float32)
    mid = rest.astype(jnp.bfloat16)
    low = (rest - mid.astype(jnp.float32)).astype(jnp.bfloat16)
    dot = functools.partial(jnp.dot, preferred_element_type=jnp.float32)
    return dot(hi, matrix) + dot(mid, matrix) + dot(low, matrix)


def softplus(x):
    return jnp.maximum(x, 0.0) + jnp.log1p(jnp.exp(-jnp.abs(x)))


def light(chl, sums, level):
    absorbed, irradiance = [], None
    for water, pigment, surface in zip(water_absorb, pigment_absorb, surface_light):
        fade = jnp.exp(-0.5 * (water + pigment * chl))
        intensity = surface * jnp.exp(-(water * level + pigment * sums))
        absorbed.append(intensity * (1.0 - fade * fade))
        part = intensity * fade
        irradiance = part if irradiance is None else irradiance + part
    return absorbed, irradiance


def saturation(n):
    return n * n / (1.0 + n * n)


def transport(rise_half, y):
    top = rise_half * (y + pltpu.roll(y, 1, 1))
    return pltpu.roll(top, top.shape[1] - 1, 1) - top


def wet_of(depth, shape):
    level = lax.broadcasted_iota(jnp.int32, shape, len(shape) - 1)
    return jnp.where(level < depth, 1.0, 0.0)


def level_of(shape):
    return lax.broadcasted_iota(jnp.int32, shape, len(shape) - 1).astype(jnp.float32)


def half_rise(rise):
    k = lax.broadcasted_iota(jnp.int32, rise.shape, 1)
    return jnp.where(k > 0, 0.5 * rise, 0.0)


def project_kernel(sc, x_ref, w_ref, depth_ref, y_ref, g_ref, chl_ref):
    fields, patches, cols, levels = x_ref.shape

    mixed = [k for k in range(y_ref.shape[0]) if k != 4]

    def one(q, carry):
        value = x_ref[0, q]
        y_ref[4, q] = value
        totals = [w_ref[k, 0] * value for k in mixed]
        for j in range(1, fields):
            value = x_ref[j, q]
            totals = [t + w_ref[k, j] * value for t, k in zip(totals, mixed)]
        for k, total in zip(mixed, totals):
            y_ref[k, q] = total
        chl_ref[q] = softplus(totals[0])
        return carry

    lax.fori_loop(0, patches, one, 0)
    flat = (patches * cols, levels)
    chl = chl_ref[...].reshape(flat)
    sums = level_sums(chl, level_matrix(levels, "prefix"))
    _, irradiance = light(chl, sums, level_of(flat))
    n = x_ref[0].reshape(flat)
    g_ref[...] = (uptake_rate * irradiance * saturation(n)).reshape(patches, cols, levels)


def project(comp, tracers, weights, depth):
    fields, patches, strip, levels = tracers.shape
    half = strip // 2
    block = 4
    kinds = weights.shape[0]
    return pl.pallas_call(
        project_kernel,
        grid_spec=pltpu.PrefetchScalarGridSpec(
            num_scalar_prefetch=1,
            grid=(patches // block,),
            in_specs=[
                pl.BlockSpec((fields, block, half, levels), lambda i, c: (0, i, c[0], 0)),
                SMEM,
                pl.BlockSpec((block, half, 1), lambda i, c: (i, 0, 0)),
            ],
            out_specs=[
                pl.BlockSpec((kinds, block, half, levels), lambda i, c: (0, i, 0, 0)),
                pl.BlockSpec((block, half, levels), lambda i, c: (i, 0, 0)),
            ],
            scratch_shapes=[pltpu.VMEM((block, half, levels), jnp.float32)],
        ),
        out_shape=(shape_of(kinds, patches, half, levels), shape_of(patches, half, levels)),
        compiler_params=PROJECT,
        name="project",
    )(comp, tracers, weights, depth)


def first_tracer_kernel(sc, y_ref, g_ref, got_ref, own_ref, depth_ref, share_ref, out_ref):
    patches, cols, levels = g_ref.shape
    first = sc[0] == 0

    def one(q, carry):
        rise = jnp.where(first, got_ref[0, q], own_ref[0, q])
        heat = jnp.where(first, got_ref[1, q], own_ref[1, q])
        warm = jnp.exp(heating_speed * heat)
        wet = wet_of(depth_ref[q], (cols, levels))
        up = half_rise(rise)
        g = g_ref[q]
        for place, k in enumerate(KEPT):
            y = y_ref[k, q]
            change = warm * y_ref[k + 1, q] + share_ref[k] * g + transport(up, y)
            out_ref[q, place] = wet * (y + step_tracer * change)
        return carry

    lax.fori_loop(0, patches, one, 0, unroll=2)


def half_spec(lead, cols, levels):
    zeros = (0,) * len(lead)
    return pl.BlockSpec(lead + (cols, levels), lambda i, c: zeros + (c[0], 0))


def first_tracer(comp, projected, g, got, linked, depth, shares):
    kinds, patches, half, levels = projected.shape
    block = 4
    return pl.pallas_call(
        first_tracer_kernel,
        grid_spec=pltpu.PrefetchScalarGridSpec(
            num_scalar_prefetch=1,
            grid=(patches // block,),
            in_specs=[
                pl.BlockSpec((kinds, block, half, levels), lambda i, c: (0, i, 0, 0)),
                pl.BlockSpec((block, half, levels), lambda i, c: (i, 0, 0)),
                pl.BlockSpec((2, block, half, levels), lambda i, c: (0, i, 0, 0)),
                pl.BlockSpec((2, block, half, levels), lambda i, c: (0, i, c[0], 0)),
                pl.BlockSpec((block, half, 1), lambda i, c: (i, 0, 0)),
                SMEM,
            ],
            out_specs=pl.BlockSpec((block, len(KEPT), half, levels), lambda i, c: (i, 0, 0, 0)),
        ),
        out_shape=shape_of(patches, len(KEPT), half, levels),
        compiler_params=PARAMS,
        name="first_tracer",
    )(comp, projected, g, got, linked, depth, shares)


def pack_kernel(sc, linked_ref, row0_ref, row1_ref, col0_ref, col1_ref, t0_ref, t1_ref, tc0_ref, tc1_ref,
                sent_ref, low_ref, high_ref, left_ref, right_ref):
    _, strips, strip, levels = linked_ref.shape
    half = strip // 2

    @pl.when(sc[0] == 0)
    def _():
        for part in range(2):
            cols = slice(part * half, (part + 1) * half)
            sent_ref[part] = linked_ref[0, :, cols] + linked_ref[1, :, cols]

    @pl.when(sc[0] != 0)
    def _():
        sent_ref[...] = linked_ref[:, :, :half]

    last = col1_ref.shape[2] - 1
    for f in range(2):
        low_ref[f] = row0_ref[f, 0]
        high_ref[f] = row1_ref[f, 0]
        left_ref[f] = col0_ref[f, :, 0]
        right_ref[f] = col1_ref[f, :, last]
    low_ref[2] = t0_ref[0]
    high_ref[2] = t1_ref[0]
    left_ref[2] = tc0_ref[:, 0]
    right_ref[2] = tc1_ref[:, last]


def pack(comp, linked, speeds, heat):
    _, strips, strip, levels = linked.shape
    rows, cols, _ = heat.shape
    outs = (
        shape_of(2, strips, strip // 2, levels), shape_of(3, cols, levels), shape_of(3, cols, levels),
        shape_of(3, rows, levels), shape_of(3, rows, levels),
    )
    edge = min(8, cols)
    return pl.pallas_call(
        pack_kernel,
        grid_spec=pltpu.PrefetchScalarGridSpec(
            num_scalar_prefetch=1,
            grid=(1,),
            in_specs=[
                whole(linked),
                pl.BlockSpec((2, 1, cols, levels), lambda i, c: (0, 0, 0, 0)),
                pl.BlockSpec((2, 1, cols, levels), lambda i, c: (0, rows - 1, 0, 0)),
                pl.BlockSpec((2, rows, edge, levels), lambda i, c: (0, 0, 0, 0)),
                pl.BlockSpec((2, rows, edge, levels), lambda i, c: (0, 0, cols // edge - 1, 0)),
                pl.BlockSpec((1, cols, levels), lambda i, c: (0, 0, 0)),
                pl.BlockSpec((1, cols, levels), lambda i, c: (rows - 1, 0, 0)),
                pl.BlockSpec((rows, edge, levels), lambda i, c: (0, 0, 0)),
                pl.BlockSpec((rows, edge, levels), lambda i, c: (0, cols // edge - 1, 0)),
            ],
            out_specs=[whole(o) for o in outs],
        ),
        out_shape=outs,
        compiler_params=STREAMED,
        name="pack",
    )(comp, linked, speeds, speeds, speeds, speeds, heat, heat, heat, heat)


def ocean_kernel(
    advance, sc, coriolis_ref, speed_ref, t_ref, north_ref, south_ref, east_ref, west_ref, depth_ref,
    *rest,
):
    rest = list(rest)
    u_ref, v_ref = speed_ref.at[0], speed_ref.at[1]
    if advance == 1:
        linked_ref, got_ref = rest[:2]
        rest = rest[2:]
    next_ref, tn_ref, rise_ref = rest[:3]
    edge_refs = rest[3:7] if advance == 1 else ()
    un_ref, vn_ref = next_ref.at[0], next_ref.at[1]
    p_ref, pn_ref, ps_ref, pe_ref, pw_ref, div_ref = rest[-6:]
    rows, cols, levels = t_ref.shape
    above = level_matrix(levels, "above")
    p_ref[...] = (
        weight_pull_factor * level_sums(t_ref[...].reshape(rows * cols, levels), above)
    ).reshape(rows, cols, levels)
    for target, source in ((pn_ref, north_ref), (ps_ref, south_ref), (pe_ref, east_ref), (pw_ref, west_ref)):
        target[...] = weight_pull_factor * level_sums(source[2], above)
    lanes = min(128, levels)
    place = lax.broadcasted_iota(jnp.int32, (cols, lanes), 0)
    at_east, at_west = place == cols - 1, place == 0

    def piece(y, at, lane):
        north_in = at < rows - 1
        south_in = at > 0
        part = slice(lane, lane + lanes)
        level = lane + lax.broadcasted_iota(jnp.int32, (cols, lanes), 1)

        def around(x, e, w, n, s):
            return (
                x, jnp.where(at_east, e, pltpu.roll(x, cols - 1, 0)), jnp.where(at_west, w, pltpu.roll(x, 1, 0)), n, s
            )

        def field(ref, f):
            return around(
                ref[y, :, part],
                east_ref[f, pl.ds(y, 1)][:, part],
                west_ref[f, pl.ds(y, 1)][:, part],
                ref[y + 1, :, part] if north_in else north_ref[f, :, part],
                ref[y - 1, :, part] if south_in else south_ref[f, :, part],
            )

        wet = [jnp.where(level < depth_ref[i, y], 1.0, 0.0) for i in range(5)]
        u = field(u_ref, 0)
        v = field(v_ref, 1)
        own = 0.5 * wet[0]
        east = (u[0] + u[1]) * (own * wet[1])
        west = (u[2] + u[0]) * (own * wet[2])
        north = (v[0] + v[3]) * (own * wet[3])
        south = (v[4] + v[0]) * (own * wet[4])
        div_ref[y, :, part] = east - west + north - south
        t = field(t_ref, 2)
        p = around(
            p_ref[y, :, part],
            pe_ref[pl.ds(y, 1)][:, part],
            pw_ref[pl.ds(y, 1)][:, part],
            p_ref[y + 1, :, part] if north_in else pn_ref[:, part],
            p_ref[y - 1, :, part] if south_in else ps_ref[:, part],
        )
        wets = wet[1] + wet[2] + wet[3] + wet[4]

        def spread(x):
            return wet[1] * x[1] + wet[2] * x[2] + wet[3] * x[3] + wet[4] * x[4] - wets * x[0]

        carry_along = 0.5 * (
            east * (t[0] + t[1]) - west * (t[2] + t[0]) + north * (t[0] + t[3]) - south * (t[4] + t[0])
        )
        change = spreading * spread(t) - carry_along
        if advance == 1:
            halves = [got_ref[i, y, :, part] for i in range(2)]
            absorb = jnp.where(
                sc[0] == 0, linked_ref[0, y, :, part] + linked_ref[1, y, :, part], jnp.concatenate(halves, axis=0)
            )
            change = change + heat_gain * absorb
        zonal = 0.5 * (wet[1] * (p[1] - p[0]) + wet[2] * (p[0] - p[2]))
        merid = 0.5 * (wet[3] * (p[3] - p[0]) + wet[4] * (p[0] - p[4]))
        turn = coriolis_ref[y]
        results = (
            wet[0] * (u[0] + advance_marine * (turn * v[0] - zonal + viscosity * spread(u) - damping * u[0])),
            wet[0] * (v[0] + advance_marine * (-turn * u[0] - merid + viscosity * spread(v) - damping * v[0])),
            wet[0] * (t[0] + advance_marine * change),
        )
        for f, (ref, value) in enumerate(zip((un_ref, vn_ref, tn_ref), results)):
            ref[y, :, part] = value

    def row(y, at):
        for lane in range(0, levels, lanes):
            piece(y, at, lane)
        if edge_refs:
            for f, ref in enumerate((un_ref, vn_ref, tn_ref)):
                edge_refs[2][f, pl.ds(y, 1)] = ref[y, :1]
                edge_refs[3][f, pl.ds(y, 1)] = ref[y, cols - 1 :]

    row(0, 0)

    def inner(y, carry):
        row(y, 1)
        return carry

    lax.fori_loop(1, rows - 1, inner, 0)
    row(rows - 1, rows - 1)
    if edge_refs:
        for f, ref in enumerate((un_ref, vn_ref, tn_ref)):
            edge_refs[0][f] = ref[0]
            edge_refs[1][f] = ref[rows - 1]
    sums = level_sums(div_ref[...].reshape(rows * cols, levels), level_matrix(levels, "below"))
    rise_ref[...] = -sums.reshape(rows, cols, levels)


def ocean(advance, comp, coriolis, speeds, heat, halos, depth, linked=None, got=None):
    rows, cols, levels = heat.shape
    grid = shape_of(rows, cols, levels)
    outs = (shape_of(2, rows, cols, levels), grid, grid)
    if advance == 1:
        outs += (
            shape_of(3, cols, levels), shape_of(3, cols, levels), shape_of(3, rows, levels), shape_of(3, rows, levels),
        )
    scratch = [
        (rows, cols, levels), (cols, levels), (cols, levels), (rows, levels), (rows, levels), (rows, cols, levels),
    ]
    args = [coriolis, speeds, heat, *halos, depth] + ([linked, got] if advance == 1 else [])
    return pl.pallas_call(
        functools.partial(ocean_kernel, advance),
        grid_spec=pltpu.PrefetchScalarGridSpec(
            num_scalar_prefetch=1,
            grid=(1,),
            in_specs=[SMEM] + [whole(a) for a in args[1:]],
            out_specs=[whole(o) for o in outs],
            scratch_shapes=[pltpu.VMEM(s, jnp.float32) for s in scratch],
        ),
        out_shape=outs,
        compiler_params=STREAMED if advance == 1 else PARAMS,
        name=f"ocean{advance}",
    )(comp, *args)


def absorb_kernel(
    sc, y_ref, t_ref, speed_ref, depth_ref, t2_ref, irr_ref, row0_ref, row1_ref, col0_ref, col1_ref, chl_ref
):
    rows, cols, levels = t_ref.shape
    flat = (rows * cols, levels)

    def gather(s, carry):
        chl_ref[s] = softplus(y_ref[sc[1 + s], 0])
        return carry

    lax.fori_loop(0, rows, gather, 0, unroll=2)
    chl = chl_ref[...].reshape(flat)
    sums = level_sums(chl, level_matrix(levels, "prefix"))
    absorbed, irradiance = light(chl, sums, level_of(flat))
    wet = wet_of(depth_ref[0], t_ref.shape)
    both = (absorbed[0] + absorbed[1]).reshape(t_ref.shape)
    t2_ref[...] = t_ref[...] + advance_marine * heat_gain * (wet * both)
    irr_ref[...] = irradiance.reshape(t_ref.shape)
    for f, ref in enumerate((speed_ref.at[0], speed_ref.at[1], t2_ref)):
        row0_ref[f] = ref[0]
        row1_ref[f] = ref[rows - 1]
        for y in range(rows):
            col0_ref[f, pl.ds(y, 1)] = ref[y, :1]
            col1_ref[f, pl.ds(y, 1)] = ref[y, cols - 1 :]


def second_kernel(
    sc, y_ref, irr_ref, t1_ref, r1_ref, depth_ref, share_ref, heat_ref, a_ref, b_ref, g_ref, n_ref, chl_ref
):
    patches, _, cols, levels = y_ref.shape
    flat = (patches * cols, levels)
    whole = (patches, cols, levels)

    def one(s, carry):
        owner = sc[1 + s]
        wet = wet_of(depth_ref[0, s], (cols, levels))
        warm = jnp.exp(heating_speed * t1_ref[s])
        up = half_rise(r1_ref[s])
        y = [y_ref[owner, i] for i in range(len(KEPT))]
        g = uptake_rate * irr_ref[s] * saturation(y[3])
        for ref, i, k in ((a_ref, 0, 0), (b_ref, 1, 1), (n_ref, 3, 4)):
            change = warm * y[i + 1] + share_ref[k] * g + transport(up, y[i])
            ref[s] = wet * (y[i] + step_tracer * change)
        chl_ref[s] = softplus(a_ref[s])
        return carry

    lax.fori_loop(0, patches, one, 0, unroll=4)
    chl = chl_ref[...].reshape(flat)
    absorbed, irradiance = light(chl, level_sums(chl, level_matrix(levels, "prefix")), level_of(flat))
    wet = wet_of(depth_ref[0], whole)
    heat_ref[...] = advance_marine * heat_gain * (wet * (absorbed[0] + absorbed[1]).reshape(whole))
    g_ref[...] = uptake_rate * irradiance.reshape(whole) * saturation(n_ref[...])


def third_kernel(sc, a_ref, b_ref, g_ref, t2_ref, r2_ref, depth_ref, share_ref, band_ref, chl_ref):
    patches, cols, levels = a_ref.shape
    flat = (patches * cols, levels)
    whole = (patches, cols, levels)

    def one(s, carry):
        wet = wet_of(depth_ref[0, s], (cols, levels))
        warm = jnp.exp(heating_speed * t2_ref[s])
        a = a_ref[s]
        change = warm * b_ref[s] + share_ref[0] * g_ref[s] + transport(half_rise(r2_ref[s]), a)
        chl_ref[s] = softplus(wet * (a + step_tracer * change))
        return carry

    lax.fori_loop(0, patches, one, 0, unroll=4)
    chl = chl_ref[...].reshape(flat)
    absorbed, _ = light(chl, level_sums(chl, level_matrix(levels, "prefix")), level_of(flat))
    wet = wet_of(depth_ref[0], whole)
    for band in range(2):
        band_ref[:, band] = wet * absorbed[band].reshape(whole)


def last_ocean_kernel(
    sc, speed_ref, t_ref, north_ref, south_ref, east_ref, west_ref, depth_ref, heat_ref, out_ref, div_ref
):
    rows, cols, levels = t_ref.shape
    place = lax.broadcasted_iota(jnp.int32, (cols, levels), 0)
    sources = (speed_ref.at[0], speed_ref.at[1], t_ref)
    for y in range(rows):
        wet = [wet_of(depth_ref[i, y], (cols, levels)) for i in range(5)]

        def east_of(f):
            return jnp.where(place == cols - 1, east_ref[f, pl.ds(y, 1)], pltpu.roll(sources[f][y], cols - 1, 0))

        def west_of(f):
            return jnp.where(place == 0, west_ref[f, pl.ds(y, 1)], pltpu.roll(sources[f][y], 1, 0))

        def north_of(f):
            return sources[f][y + 1] if y < rows - 1 else north_ref[f]

        def south_of(f):
            return sources[f][y - 1] if y > 0 else south_ref[f]

        u, v, t = (ref[y] for ref in sources)
        own = 0.5 * wet[0]
        east = (u + east_of(0)) * (own * wet[1])
        west = (west_of(0) + u) * (own * wet[2])
        north = (v + north_of(1)) * (own * wet[3])
        south = (south_of(1) + v) * (own * wet[4])
        div_ref[y] = east - west + north - south
        e, w, n, s = east_of(2), west_of(2), north_of(2), south_of(2)
        spread = wet[1] * (e - t) + wet[2] * (w - t) + wet[3] * (n - t) + wet[4] * (s - t)
        carry_along = 0.5 * (east * (t + e) - west * (w + t) + north * (t + n) - south * (s + t))
        change = spreading * spread - carry_along
        out_ref[1, sc[1 + y], 1] = wet[0] * (t + advance_marine * change) + heat_ref[y]
    sums = level_sums(div_ref[...].reshape(rows * cols, levels), level_matrix(levels, "below"))
    div_ref[...] = -sums.reshape(rows, cols, levels)
    for y in range(rows):
        out_ref[1, sc[1 + y], 0] = div_ref[y]
    out_ref[0] = jnp.zeros(out_ref.shape[1:], jnp.float32)


def join_kernel(sc, absorbed_ref, flux_ref, other_ref, out_ref):
    patches, _, half, levels = absorbed_ref.shape

    @pl.when(sc[0] == 0)
    def _():
        for s in range(patches):
            for f in range(2):
                out_ref[f, s, :half] = absorbed_ref[s, f]
                out_ref[f, s, half:] = other_ref[s, f]

    @pl.when(sc[0] != 0)
    def _():
        for s in range(patches):
            for f in range(2):
                for part in range(2):
                    out_ref[f, s, part * half : (part + 1) * half] = flux_ref[part, s, f]


def call(kernel, comp, args, specs, outs, scratch=(), name=None, params=PARAMS):
    return pl.pallas_call(
        kernel,
        grid_spec=pltpu.PrefetchScalarGridSpec(
            num_scalar_prefetch=1,
            grid=(1,),
            in_specs=[spec or whole(a) for spec, a in zip(specs, args)],
            out_specs=[whole(o) for o in outs],
            scratch_shapes=[pltpu.VMEM(s, jnp.float32) for s in scratch],
        ),
        out_shape=outs,
        compiler_params=params,
        name=name,
    )(comp, *args)


def exchange_rows(low, high):
    count = lax.axis_size("py")
    north = lax.ppermute(low, "py", [((i + 1) % count, i) for i in range(count)])
    south = lax.ppermute(high, "py", [(i, (i + 1) % count) for i in range(count)])
    return north, south


def exchange_cols(low, high):
    count = lax.axis_size("px")
    east = lax.ppermute(low, "px", [((i + 1) % count, i) for i in range(count)])
    west = lax.ppermute(high, "px", [(i, (i + 1) % count) for i in range(count)])
    return east, west


def exchange_half_cols(low, high):
    count = lax.axis_size("px")
    line = [(h % 2) * count + h // 2 for h in range(2 * count)]
    ahead = [(line[h], line[(h + 1) % len(line)]) for h in range(len(line))]
    east = lax.ppermute(low, ("comp", "px"), [(b, a) for a, b in ahead])
    west = lax.ppermute(high, ("comp", "px"), ahead)
    return east, west


def to_owners(blocks):
    return lax.all_to_all(blocks, ("py", "px"), split_axis=0, concat_axis=0, tiled=True)


def swap(block):
    return lax.ppermute(block, "comp", [(0, 1), (1, 0)])


def pick(blocks, order, axis):
    return jnp.stack(
        [lax.dynamic_index_in_dim(blocks, order[k], axis, keepdims=False) for k in range(order.shape[0])], axis
    )


def table(levels, pattern):
    return level_matrix(levels, pattern).astype(jnp.float32)


def product(values, matrix):
    return jnp.einsum("...j,jk->...k", values, matrix, precision=lax.Precision.HIGHEST)


def general_light(conc, wet, loading):
    chl = jax.nn.softplus(jnp.einsum("f...,f->...", conc, loading, precision=lax.Precision.HIGHEST))
    levels = chl.shape[-1]
    absorbed, irradiance = light(chl, product(chl, table(levels, "prefix")), level_of(chl.shape))
    return wet * jnp.stack(absorbed), irradiance


def general_tracers(conc, rise, heat, irradiance, wet, matrix, share):
    none = jnp.zeros_like(conc[..., :1])
    top = jnp.concatenate([none, 0.5 * (conc[..., 1:] + conc[..., :-1]) * rise[..., 1:]], axis=-1)
    below = jnp.concatenate([top[..., 1:], none], axis=-1)
    mixed = jnp.einsum("ij,j...->i...", matrix, conc, precision=lax.Precision.HIGHEST)
    growth = uptake_rate * irradiance * saturation(conc[0])
    change = (
        jnp.exp(heating_speed * heat) * mixed
        + share.reshape((-1,) + (1,) * (conc.ndim - 1)) * growth + below - top
    )
    return wet * (conc + step_tracer * change)


def general_ocean(u, v, t, absorb, depth, coriolis):
    levels = t.shape[-1]
    fields = jnp.stack([u, v, t])
    north, south = exchange_rows(fields[:, 0], fields[:, -1])
    east, west = exchange_cols(fields[:, :, 0], fields[:, :, -1])
    tall = jnp.concatenate([south[:, None], fields, north[:, None]], axis=1)
    wide = jnp.concatenate([west[:, :, None], fields, east[:, :, None]], axis=2)
    around = (fields, wide[:, :, 2:], wide[:, :, :-2], tall[:, 2:], tall[:, :-2])
    above = table(levels, "above")
    u, v, t = ([x[f] for x in around] for f in range(3))
    p = [weight_pull_factor * product(x, above) for x in t]
    wet = [wet_of(depth[i], t[0].shape) for i in range(5)]

    def spread(x):
        return sum(wet[i] * (x[i] - x[0]) for i in range(1, 5))

    east = 0.5 * (u[0] + u[1]) * wet[0] * wet[1]
    west = 0.5 * (u[2] + u[0]) * wet[2] * wet[0]
    north = 0.5 * (v[0] + v[3]) * wet[0] * wet[3]
    south = 0.5 * (v[4] + v[0]) * wet[4] * wet[0]
    carry_along = 0.5 * (
        east * (t[0] + t[1]) - west * (t[2] + t[0]) + north * (t[0] + t[3]) - south * (t[4] + t[0])
    )
    zonal = 0.5 * (wet[1] * (p[1] - p[0]) + wet[2] * (p[0] - p[2]))
    merid = 0.5 * (wet[3] * (p[3] - p[0]) + wet[4] * (p[0] - p[4]))
    turn = coriolis[:, None, None]
    rise = -product(east - west + north - south, table(levels, "below"))
    return (
        wet[0] * (u[0] + advance_marine * (turn * v[0] - zonal + viscosity * spread(u) - damping * u[0])),
        wet[0] * (v[0] + advance_marine * (-turn * u[0] - merid + viscosity * spread(v) - damping * v[0])),
        wet[0] * (t[0] + advance_marine * (spreading * spread(t) - carry_along + heat_gain * (absorb[0] + absorb[1]))),
        rise,
    )


def general(linked, u, v, t, tracers, depth, tracer_depth, holder_rank, patch_index, coriolis, matrix, share, loading):
    comp_index = lax.axis_index("comp")
    first = comp_index == 0
    fields, patches, strip, levels = tracers.shape
    half = strip // 2
    indices = jnp.arange(patches, dtype=jnp.int32)
    owner_row = lax.dynamic_index_in_dim(holder_rank, patch_index, 0, keepdims=False)
    inverse_row = jnp.sum(jnp.where(owner_row[:, None] == indices[None], indices[:, None], 0), axis=0)

    def own_half(x):
        return lax.dynamic_slice_in_dim(x, comp_index * half, half, x.ndim - 2)

    partner = swap(linked)
    absorb = jnp.where(first, linked, partner)
    flux = own_half(jnp.where(first, partner, linked))
    conc = own_half(tracers)
    wet = wet_of(tracer_depth, conc.shape[1:])
    irradiance = general_light(conc, wet, loading)[1]
    grid = t.shape
    for _ in range(3):
        u, v, t, rise = general_ocean(u, v, t, absorb.reshape((2,) + grid), depth, coriolis)
        conc = general_tracers(conc, flux[0], flux[1], irradiance, wet, matrix, share)
        absorbed, irradiance = general_light(conc, wet, loading)
        both = own_half(pick(jnp.stack([rise, t]).reshape(2, patches, strip, levels), inverse_row, 1))
        send = jnp.concatenate([both, absorbed])
        back = lax.all_to_all(send, ("py", "px"), split_axis=1, concat_axis=1, tiled=True)
        flux = back[:2]
        mine = pick(back[2:], owner_row, 1)
        other = swap(mine)
        absorb = jnp.where(first, jnp.concatenate([mine, other], 2), jnp.concatenate([other, mine], 2))
    other = swap(flux)
    joined = jnp.where(first, jnp.concatenate([flux, other], 2), jnp.concatenate([other, flux], 2))
    return jnp.where(first, absorb, joined)


def shards(
    current_speeds,
    thermal_anomaly,
    solute_amounts,
    delayed_link_source,
    marine_indicator,
    floor_layer_index,
    holder_rank,
    biota_exchange_matrix,
    photic_absorb_share,
    chroma_loading,
):
    comp_index = lax.axis_index("comp")
    row_index = lax.axis_index("py")
    col_index = lax.axis_index("px")
    rows_mesh = lax.axis_size("py")
    cols_mesh = lax.axis_size("px")
    patches = rows_mesh * cols_mesh
    fields, _, columns, levels = solute_amounts.shape
    strip = columns // patches
    half = strip // 2
    patch_index = row_index * cols_mesh + col_index
    first = comp_index == 0

    linked = delayed_link_source.reshape(2, patches, strip, levels)
    tracers = solute_amounts.reshape(fields, patches, strip, levels)
    u0, v0 = current_speeds[0], current_speeds[1]

    column_depth = marine_indicator * floor_layer_index
    wrapped = jnp.concatenate([column_depth[:, -1:], column_depth, column_depth[:, :1]], axis=1)
    padded = jnp.pad(wrapped, ((1, 1), (0, 0)))
    local = lax.dynamic_slice(padded, (row_index * CY, col_index * CX), (CY + 2, CX + 2))
    depth = jnp.stack([local[1:-1, 1:-1], local[1:-1, 2:], local[1:-1, :-2], local[2:, 1:-1], local[:-2, 1:-1]])
    depth = depth[..., None]
    by_strip = (
        column_depth.reshape(rows_mesh, CY, cols_mesh, CX).transpose(0, 2, 1, 3).reshape(patches, patches, strip)
    )
    here = (holder_rank == patch_index)[:, :, None]
    tracer_depth = jnp.sum(jnp.where(here, by_strip, 0), axis=1)
    tracer_depth = lax.dynamic_slice_in_dim(tracer_depth, comp_index * half, half, 1)[..., None]
    owner_row = lax.dynamic_index_in_dim(holder_rank, patch_index, 0, keepdims=False)
    side_index = comp_index.astype(jnp.int32)[None]
    comp = jnp.concatenate([side_index, owner_row])
    ys = (row_index * CY + jnp.arange(CY, dtype=jnp.int32)).astype(jnp.float32)
    coriolis = coriolis_scale * (2.0 * (ys + 0.5) / (CY * rows_mesh) - 1.0)

    if half % 8:
        out = general(
            linked, u0, v0, thermal_anomaly, tracers, depth, tracer_depth, holder_rank, patch_index, coriolis,
            biota_exchange_matrix, photic_absorb_share, chroma_loading,
        )
        return out.reshape(1, 2, 1, columns, levels)

    sent, *edges = pack(side_index, linked, current_speeds, thermal_anomaly)
    got = swap(sent)
    times = functools.partial(jnp.dot, precision=lax.Precision.HIGHEST)
    unit = (jnp.arange(fields) == 0).astype(jnp.float32)
    chain = [jnp.stack([chroma_loading, unit])]
    for _ in range(3):
        chain.append(times(chain[-1], biota_exchange_matrix))
    weights = jnp.stack([c[0] for c in chain] + [c[1] for c in chain[:3]])
    shares = times(weights, photic_absorb_share)

    projected, g = project(side_index, tracers, weights, tracer_depth)
    edges, projected, g = lax.optimization_barrier((edges, projected, g))
    halos0 = exchange_rows(edges[0], edges[1]) + exchange_cols(edges[2], edges[3])
    kept = first_tracer(side_index, projected, g, got, linked, tracer_depth, shares)
    kept, halos0 = lax.optimization_barrier((kept, halos0))
    arrived = to_owners(kept)

    speeds1, t1, r1, *edges = ocean(1, comp, coriolis, current_speeds, thermal_anomaly, halos0, depth, linked, got)
    halos1 = exchange_rows(edges[0], edges[1]) + exchange_cols(edges[2], edges[3])
    speeds2, t2, r2 = ocean(2, comp, coriolis, speeds1, t1, halos1, depth)
    arrived, speeds2, t2 = lax.optimization_barrier((arrived, speeds2, t2))

    patch_half = half_spec((CY,), half, levels)
    speeds_half = half_spec((2, CY), half, levels)
    depth_half = pl.BlockSpec((5, CY, half, 1), lambda i, c: (0, 0, c[0], 0))
    piece = shape_of(CY, half, levels)
    scratch = (CY, half, levels)
    line = shape_of(3, half, levels)
    first_field = pl.BlockSpec((patches, 1, half, levels), lambda i, c: (0, 0, 0, 0))
    side = shape_of(3, CY, levels)

    t2, irr1, *edges = call(
        absorb_kernel, comp, (arrived, t2, speeds2, depth), [first_field, patch_half, speeds_half, depth_half],
        (piece, piece, line, line, side, side), [scratch], "absorb", STREAMED,
    )
    halos2 = exchange_rows(edges[0], edges[1]) + exchange_half_cols(edges[2], edges[3])
    heat, a, b, g = call(
        second_kernel, comp, (arrived, irr1, t1, r1, depth, shares),
        [None, None, patch_half, patch_half, depth_half, SMEM],
        (piece,) * 4, [scratch] * 2, "second",
    )
    [back] = call(
        last_ocean_kernel, comp, (speeds2, t2, *halos2, depth, heat),
        [speeds_half] + [None] * 5 + [depth_half, None],
        (shape_of(2, patches, 2, half, levels),), [scratch], "last_ocean",
    )
    flux = lax.all_to_all(
        back.reshape(2 * patches, 2, half, levels), ("comp", "py", "px"), split_axis=0, concat_axis=0, tiled=True
    ).reshape(2, patches, 2, half, levels)
    [absorbed] = call(
        third_kernel, comp, (a, b, g, t2, r2, depth, shares),
        [None] * 4 + [patch_half, depth_half, SMEM], (shape_of(CY, 2, half, levels),), [scratch], "third",
    )
    other = swap(absorbed)
    [out] = call(
        join_kernel, comp, (absorbed, flux, other), [None] * 3, (shape_of(2, patches, strip, levels),), (), "join"
    )
    return out.reshape(1, 2, 1, columns, levels)


def solution(mesh):
    placed = (
        P(None, "py", "px", None),
        P("py", "px", None),
        P(None, ("py", "px"), None, None),
        P("comp", None, ("py", "px"), None, None),
        P(),
        P(),
        P(),
        P(),
        P(),
        P(),
    )
    return jax.shard_map(
        shards,
        mesh=mesh,
        in_specs=placed,
        out_specs=P("comp", None, ("py", "px"), None, None),
        check_vma=False,
    )
```

```python
import functools

import jax
import jax.numpy as jnp
from jax import lax
from jax.experimental import pallas as pl
from jax.experimental.pallas import tpu as pltpu
from jax.sharding import PartitionSpec as P

advance_marine = 0.1
spreading = 0.1
viscosity = 0.1
damping = 0.05
heat_gain = 0.2
weight_pull_factor = 0.05
coriolis_scale = 1.0
step_tracer = 0.1
heating_speed = 0.06
uptake_rate = 0.01
water_absorb = (0.02, 0.003)
pigment_absorb = (0.03, 0.004)
surface_light = (40.0, 60.0)
CY = 16
CX = 32
KEPT = (0, 1, 2, 4, 5)
SMEM = pl.BlockSpec(memory_space=pltpu.SMEM)
PARAMS = pltpu.CompilerParams(vmem_limit_bytes=20 * 1024 * 1024)
HBM = pl.BlockSpec(memory_space=pltpu.HBM)
STREAMED = pltpu.CompilerParams(vmem_limit_bytes=60 * 1024 * 1024)


def whole(array):
    zeros = (0,) * len(array.shape)
    return pl.BlockSpec(array.shape, lambda i, c: zeros)


def shape_of(*dims):
    return jax.ShapeDtypeStruct(dims, jnp.float32)


def level_matrix(levels, pattern):
    row = lax.broadcasted_iota(jnp.int32, (levels, levels), 0)
    col = lax.broadcasted_iota(jnp.int32, (levels, levels), 1)
    if pattern == "above":
        m = jnp.where(row < col, 1.0, jnp.where(row == col, 0.5, 0.0))
    elif pattern == "below":
        m = jnp.where(row >= col, 1.0, 0.0)
    else:
        m = jnp.where(row < col, 1.0, 0.0)
    return m.astype(jnp.bfloat16)


def level_sums(x, matrix):
    hi = x.astype(jnp.bfloat16)
    rest = x - hi.astype(jnp.float32)
    mid = rest.astype(jnp.bfloat16)
    low = (rest - mid.astype(jnp.float32)).astype(jnp.bfloat16)
    dot = functools.partial(jnp.dot, preferred_element_type=jnp.float32)
    return dot(hi, matrix) + dot(mid, matrix) + dot(low, matrix)


def softplus(x):
    return jnp.maximum(x, 0.0) + jnp.log1p(jnp.exp(-jnp.abs(x)))


def light(chl, sums, level):
    absorbed, irradiance = [], None
    for water, pigment, surface in zip(water_absorb, pigment_absorb, surface_light):
        fade = jnp.exp(-0.5 * (water + pigment * chl))
        intensity = surface * jnp.exp(-(water * level + pigment * sums))
        absorbed.append(intensity * (1.0 - fade * fade))
        part = intensity * fade
        irradiance = part if irradiance is None else irradiance + part
    return absorbed, irradiance


def saturation(n):
    return n * n / (1.0 + n * n)


def transport(rise_half, y):
    top = rise_half * (y + pltpu.roll(y, 1, 1))
    return pltpu.roll(top, top.shape[1] - 1, 1) - top


def wet_of(depth, shape):
    level = lax.broadcasted_iota(jnp.int32, shape, len(shape) - 1)
    return jnp.where(level < depth, 1.0, 0.0)


def level_of(shape):
    return lax.broadcasted_iota(jnp.int32, shape, len(shape) - 1).astype(jnp.float32)


def half_rise(rise):
    k = lax.broadcasted_iota(jnp.int32, rise.shape, 1)
    return jnp.where(k > 0, 0.5 * rise, 0.0)


def project_kernel(sc, x_hbm, w_ref, y_ref, g_ref, x_ref, chl_ref, sems):
    pieces, fields, block, cols, levels = x_ref.shape
    own = pl.ds(pl.multiple_of(sc[0] * cols, cols), cols)
    copies = [
        pltpu.make_async_copy(x_hbm.at[:, pl.ds(i * block, block), own], x_ref.at[i], sems.at[i]) for i in range(pieces)
    ]
    for copy in copies:
        copy.start()
    mixed = [k for k in range(y_ref.shape[0]) if k != 4]
    prefix = level_matrix(levels, "prefix")
    flat = (block * cols, levels)
    for i, copy in enumerate(copies):
        copy.wait()

        def one(q, carry):
            at = i * block + q
            value = x_ref[i, 0, q]
            y_ref[4, at] = value
            totals = [w_ref[k, 0] * value for k in mixed]
            for j in range(1, fields):
                value = x_ref[i, j, q]
                totals = [t + w_ref[k, j] * value for t, k in zip(totals, mixed)]
            for k, total in zip(mixed, totals):
                y_ref[k, at] = total
            chl_ref[q] = softplus(totals[0])
            return carry

        lax.fori_loop(0, block, one, 0)
        chl = chl_ref[...].reshape(flat)
        _, irradiance = light(chl, level_sums(chl, prefix), level_of(flat))
        n = x_ref[i, 0].reshape(flat)
        g_ref[i * block : (i + 1) * block] = (uptake_rate * irradiance * saturation(n)).reshape(block, cols, levels)


def project(comp, tracers, weights):
    fields, patches, strip, levels = tracers.shape
    half = strip // 2
    pieces = 4
    block = patches // pieces
    outs = (shape_of(weights.shape[0], patches, half, levels), shape_of(patches, half, levels))
    return pl.pallas_call(
        project_kernel,
        grid_spec=pltpu.PrefetchScalarGridSpec(
            num_scalar_prefetch=1,
            grid=(1,),
            in_specs=[HBM, SMEM],
            out_specs=[whole(o) for o in outs],
            scratch_shapes=[
                pltpu.VMEM((pieces, fields, block, half, levels), jnp.float32),
                pltpu.VMEM((block, half, levels), jnp.float32),
                pltpu.SemaphoreType.DMA((pieces,)),
            ],
        ),
        out_shape=outs,
        compiler_params=PARAMS,
        name="project",
    )(comp, tracers, weights)


def first_tracer_kernel(sc, y_ref, g_ref, got_ref, own_ref, depth_ref, share_ref, out_ref):
    patches, cols, levels = g_ref.shape
    first = sc[0] == 0

    def one(q, carry):
        rise = jnp.where(first, got_ref[0, q], own_ref[0, q])
        heat = jnp.where(first, got_ref[1, q], own_ref[1, q])
        warm = jnp.exp(heating_speed * heat)
        wet = wet_of(depth_ref[q], (cols, levels))
        up = half_rise(rise)
        g = g_ref[q]
        for place, k in enumerate(KEPT):
            y = y_ref[k, q]
            change = warm * y_ref[k + 1, q] + share_ref[k] * g + transport(up, y)
            out_ref[q, place] = wet * (y + step_tracer * change)
        return carry

    lax.fori_loop(0, patches, one, 0, unroll=2)


def half_spec(lead, cols, levels):
    zeros = (0,) * len(lead)
    return pl.BlockSpec(lead + (cols, levels), lambda i, c: zeros + (c[0], 0))


def first_tracer(comp, projected, g, got, linked, depth, shares):
    kinds, patches, half, levels = projected.shape
    block = 4
    return pl.pallas_call(
        first_tracer_kernel,
        grid_spec=pltpu.PrefetchScalarGridSpec(
            num_scalar_prefetch=1,
            grid=(patches // block,),
            in_specs=[
                pl.BlockSpec((kinds, block, half, levels), lambda i, c: (0, i, 0, 0)),
                pl.BlockSpec((block, half, levels), lambda i, c: (i, 0, 0)),
                pl.BlockSpec((2, block, half, levels), lambda i, c: (0, i, 0, 0)),
                pl.BlockSpec((2, block, half, levels), lambda i, c: (0, i, c[0], 0)),
                pl.BlockSpec((block, half, 1), lambda i, c: (i, 0, 0)),
                SMEM,
            ],
            out_specs=pl.BlockSpec((block, len(KEPT), half, levels), lambda i, c: (i, 0, 0, 0)),
        ),
        out_shape=shape_of(patches, len(KEPT), half, levels),
        compiler_params=PARAMS,
        name="first_tracer",
    )(comp, projected, g, got, linked, depth, shares)


def pack_kernel(sc, linked_ref, row0_ref, row1_ref, col0_ref, col1_ref, t0_ref, t1_ref, tc0_ref, tc1_ref,
                sent_ref, low_ref, high_ref, left_ref, right_ref):
    _, strips, strip, levels = linked_ref.shape
    half = strip // 2

    @pl.when(sc[0] == 0)
    def _():
        for part in range(2):
            cols = slice(part * half, (part + 1) * half)
            sent_ref[part] = linked_ref[0, :, cols] + linked_ref[1, :, cols]

    @pl.when(sc[0] != 0)
    def _():
        sent_ref[...] = linked_ref[:, :, :half]

    last = col1_ref.shape[2] - 1
    for f in range(2):
        low_ref[f] = row0_ref[f, 0]
        high_ref[f] = row1_ref[f, 0]
        left_ref[f] = col0_ref[f, :, 0]
        right_ref[f] = col1_ref[f, :, last]
    low_ref[2] = t0_ref[0]
    high_ref[2] = t1_ref[0]
    left_ref[2] = tc0_ref[:, 0]
    right_ref[2] = tc1_ref[:, last]


def pack(comp, linked, speeds, heat):
    _, strips, strip, levels = linked.shape
    rows, cols, _ = heat.shape
    outs = (
        shape_of(2, strips, strip // 2, levels), shape_of(3, cols, levels), shape_of(3, cols, levels),
        shape_of(3, rows, levels), shape_of(3, rows, levels),
    )
    edge = min(8, cols)
    return pl.pallas_call(
        pack_kernel,
        grid_spec=pltpu.PrefetchScalarGridSpec(
            num_scalar_prefetch=1,
            grid=(1,),
            in_specs=[
                whole(linked),
                pl.BlockSpec((2, 1, cols, levels), lambda i, c: (0, 0, 0, 0)),
                pl.BlockSpec((2, 1, cols, levels), lambda i, c: (0, rows - 1, 0, 0)),
                pl.BlockSpec((2, rows, edge, levels), lambda i, c: (0, 0, 0, 0)),
                pl.BlockSpec((2, rows, edge, levels), lambda i, c: (0, 0, cols // edge - 1, 0)),
                pl.BlockSpec((1, cols, levels), lambda i, c: (0, 0, 0)),
                pl.BlockSpec((1, cols, levels), lambda i, c: (rows - 1, 0, 0)),
                pl.BlockSpec((rows, edge, levels), lambda i, c: (0, 0, 0)),
                pl.BlockSpec((rows, edge, levels), lambda i, c: (0, cols // edge - 1, 0)),
            ],
            out_specs=[whole(o) for o in outs],
        ),
        out_shape=outs,
        compiler_params=STREAMED,
        name="pack",
    )(comp, linked, speeds, speeds, speeds, speeds, heat, heat, heat, heat)


def ocean_kernel(
    advance, sc, coriolis_ref, speed_ref, t_ref, north_ref, south_ref, east_ref, west_ref, depth_ref,
    *rest,
):
    rest = list(rest)
    copies = []
    if advance == 1:
        linked_ref, got_ref = rest[:2]
        *rest, heat_in, speed_in, linked_in, sems = rest[2:]
        for i, (source, target) in enumerate(((t_ref, heat_in), (speed_ref, speed_in), (linked_ref, linked_in))):
            copies.append(pltpu.make_async_copy(source, target, sems.at[i]))
            copies[-1].start()
        t_ref, speed_ref, linked_ref = heat_in, speed_in, linked_in
        copies[0].wait()
    u_ref, v_ref = speed_ref.at[0], speed_ref.at[1]
    next_ref, tn_ref, rise_ref = rest[:3]
    edge_refs = rest[3:7] if advance == 1 else ()
    un_ref, vn_ref = next_ref.at[0], next_ref.at[1]
    p_ref, pn_ref, ps_ref, pe_ref, pw_ref, div_ref = rest[-6:]
    rows, cols, levels = t_ref.shape
    above = level_matrix(levels, "above")
    p_ref[...] = (
        weight_pull_factor * level_sums(t_ref[...].reshape(rows * cols, levels), above)
    ).reshape(rows, cols, levels)
    for target, source in ((pn_ref, north_ref), (ps_ref, south_ref), (pe_ref, east_ref), (pw_ref, west_ref)):
        target[...] = weight_pull_factor * level_sums(source[2], above)
    for copy in copies[1:]:
        copy.wait()
    lanes = min(128, levels)
    place = lax.broadcasted_iota(jnp.int32, (cols, lanes), 0)
    at_east, at_west = place == cols - 1, place == 0

    def piece(y, at, lane):
        north_in = at < rows - 1
        south_in = at > 0
        part = slice(lane, lane + lanes)
        level = lane + lax.broadcasted_iota(jnp.int32, (cols, lanes), 1)

        def around(x, e, w, n, s):
            return (
                x, jnp.where(at_east, e, pltpu.roll(x, cols - 1, 0)), jnp.where(at_west, w, pltpu.roll(x, 1, 0)), n, s
            )

        def field(ref, f):
            return around(
                ref[y, :, part],
                east_ref[f, pl.ds(y, 1)][:, part],
                west_ref[f, pl.ds(y, 1)][:, part],
                ref[y + 1, :, part] if north_in else north_ref[f, :, part],
                ref[y - 1, :, part] if south_in else south_ref[f, :, part],
            )

        wet = [jnp.where(level < depth_ref[i, y], 1.0, 0.0) for i in range(5)]
        u = field(u_ref, 0)
        v = field(v_ref, 1)
        own = 0.5 * wet[0]
        east = (u[0] + u[1]) * (own * wet[1])
        west = (u[2] + u[0]) * (own * wet[2])
        north = (v[0] + v[3]) * (own * wet[3])
        south = (v[4] + v[0]) * (own * wet[4])
        div_ref[y, :, part] = east - west + north - south
        t = field(t_ref, 2)
        p = around(
            p_ref[y, :, part],
            pe_ref[pl.ds(y, 1)][:, part],
            pw_ref[pl.ds(y, 1)][:, part],
            p_ref[y + 1, :, part] if north_in else pn_ref[:, part],
            p_ref[y - 1, :, part] if south_in else ps_ref[:, part],
        )
        wets = wet[1] + wet[2] + wet[3] + wet[4]

        def spread(x):
            return wet[1] * x[1] + wet[2] * x[2] + wet[3] * x[3] + wet[4] * x[4] - wets * x[0]

        carry_along = 0.5 * (
            east * (t[0] + t[1]) - west * (t[2] + t[0]) + north * (t[0] + t[3]) - south * (t[4] + t[0])
        )
        change = spreading * spread(t) - carry_along
        if advance == 1:
            halves = [got_ref[i, y, :, part] for i in range(2)]
            absorb = jnp.where(
                sc[0] == 0, linked_ref[0, y, :, part] + linked_ref[1, y, :, part], jnp.concatenate(halves, axis=0)
            )
            change = change + heat_gain * absorb
        zonal = 0.5 * (wet[1] * (p[1] - p[0]) + wet[2] * (p[0] - p[2]))
        merid = 0.5 * (wet[3] * (p[3] - p[0]) + wet[4] * (p[0] - p[4]))
        turn = coriolis_ref[y]
        results = (
            wet[0] * (u[0] + advance_marine * (turn * v[0] - zonal + viscosity * spread(u) - damping * u[0])),
            wet[0] * (v[0] + advance_marine * (-turn * u[0] - merid + viscosity * spread(v) - damping * v[0])),
            wet[0] * (t[0] + advance_marine * change),
        )
        for f, (ref, value) in enumerate(zip((un_ref, vn_ref, tn_ref), results)):
            ref[y, :, part] = value

    def row(y, at):
        for lane in range(0, levels, lanes):
            piece(y, at, lane)
        if edge_refs:
            for f, ref in enumerate((un_ref, vn_ref, tn_ref)):
                edge_refs[2][f, pl.ds(y, 1)] = ref[y, :1]
                edge_refs[3][f, pl.ds(y, 1)] = ref[y, cols - 1 :]

    row(0, 0)

    def inner(y, carry):
        row(y, 1)
        return carry

    lax.fori_loop(1, rows - 1, inner, 0)
    row(rows - 1, rows - 1)
    if edge_refs:
        for f, ref in enumerate((un_ref, vn_ref, tn_ref)):
            edge_refs[0][f] = ref[0]
            edge_refs[1][f] = ref[rows - 1]
    sums = level_sums(div_ref[...].reshape(rows * cols, levels), level_matrix(levels, "below"))
    rise_ref[...] = -sums.reshape(rows, cols, levels)


def ocean(advance, comp, coriolis, speeds, heat, halos, depth, linked=None, got=None):
    rows, cols, levels = heat.shape
    grid = shape_of(rows, cols, levels)
    outs = (shape_of(2, rows, cols, levels), grid, grid)
    if advance == 1:
        outs += (
            shape_of(3, cols, levels), shape_of(3, cols, levels), shape_of(3, rows, levels), shape_of(3, rows, levels),
        )
    scratch = [
        (rows, cols, levels), (cols, levels), (cols, levels), (rows, levels), (rows, levels), (rows, cols, levels),
    ]
    scratch = [pltpu.VMEM(s, jnp.float32) for s in scratch]
    if advance == 1:
        scratch += [pltpu.VMEM(x.shape, jnp.float32) for x in (heat, speeds, linked)] + [pltpu.SemaphoreType.DMA((3,))]
    args = [coriolis, speeds, heat, *halos, depth] + ([linked, got] if advance == 1 else [])
    return pl.pallas_call(
        functools.partial(ocean_kernel, advance),
        grid_spec=pltpu.PrefetchScalarGridSpec(
            num_scalar_prefetch=1,
            grid=(1,),
            in_specs=[SMEM] + [
                HBM if advance == 1 and any(x is y for y in (speeds, heat, linked)) else whole(x) for x in args[1:]
            ],
            out_specs=[whole(o) for o in outs],
            scratch_shapes=scratch,
        ),
        out_shape=outs,
        compiler_params=PARAMS,
        name=f"ocean{advance}",
    )(comp, *args)


def absorb_kernel(
    sc, y_hbm, t_ref, speed_ref, depth_ref, t2_ref, irr_ref, row0_ref, row1_ref, col0_ref, col1_ref, chl_ref, y_ref, sem
):
    rows, cols, levels = t_ref.shape
    flat = (rows * cols, levels)
    copy = pltpu.make_async_copy(y_hbm.at[:, 0], y_ref, sem)
    copy.start()
    copy.wait()

    def gather(s, carry):
        chl_ref[s] = softplus(y_ref[sc[1 + s]])
        return carry

    lax.fori_loop(0, rows, gather, 0, unroll=2)
    chl = chl_ref[...].reshape(flat)
    sums = level_sums(chl, level_matrix(levels, "prefix"))
    absorbed, irradiance = light(chl, sums, level_of(flat))
    wet = wet_of(depth_ref[0], t_ref.shape)
    both = (absorbed[0] + absorbed[1]).reshape(t_ref.shape)
    t2_ref[...] = t_ref[...] + advance_marine * heat_gain * (wet * both)
    irr_ref[...] = irradiance.reshape(t_ref.shape)
    for f, ref in enumerate((speed_ref.at[0], speed_ref.at[1], t2_ref)):
        row0_ref[f] = ref[0]
        row1_ref[f] = ref[rows - 1]
        for y in range(rows):
            col0_ref[f, pl.ds(y, 1)] = ref[y, :1]
            col1_ref[f, pl.ds(y, 1)] = ref[y, cols - 1 :]


def second_kernel(
    sc, y_ref, irr_ref, t1_ref, r1_ref, depth_ref, share_ref, heat_ref, a_ref, b_ref, g_ref, n_ref, chl_ref
):
    patches, _, cols, levels = y_ref.shape
    flat = (patches * cols, levels)
    whole = (patches, cols, levels)

    def one(s, carry):
        owner = sc[1 + s]
        wet = wet_of(depth_ref[0, s], (cols, levels))
        warm = jnp.exp(heating_speed * t1_ref[s])
        up = half_rise(r1_ref[s])
        y = [y_ref[owner, i] for i in range(len(KEPT))]
        g = uptake_rate * irr_ref[s] * saturation(y[3])
        for ref, i, k in ((a_ref, 0, 0), (b_ref, 1, 1), (n_ref, 3, 4)):
            change = warm * y[i + 1] + share_ref[k] * g + transport(up, y[i])
            ref[s] = wet * (y[i] + step_tracer * change)
        chl_ref[s] = softplus(a_ref[s])
        return carry

    lax.fori_loop(0, patches, one, 0, unroll=4)
    chl = chl_ref[...].reshape(flat)
    absorbed, irradiance = light(chl, level_sums(chl, level_matrix(levels, "prefix")), level_of(flat))
    wet = wet_of(depth_ref[0], whole)
    heat_ref[...] = advance_marine * heat_gain * (wet * (absorbed[0] + absorbed[1]).reshape(whole))
    g_ref[...] = uptake_rate * irradiance.reshape(whole) * saturation(n_ref[...])


def third_kernel(sc, a_ref, b_ref, g_ref, t2_ref, r2_ref, depth_ref, share_ref, band_ref, chl_ref):
    patches, cols, levels = a_ref.shape
    flat = (patches * cols, levels)
    whole = (patches, cols, levels)

    def one(s, carry):
        wet = wet_of(depth_ref[0, s], (cols, levels))
        warm = jnp.exp(heating_speed * t2_ref[s])
        a = a_ref[s]
        change = warm * b_ref[s] + share_ref[0] * g_ref[s] + transport(half_rise(r2_ref[s]), a)
        chl_ref[s] = softplus(wet * (a + step_tracer * change))
        return carry

    lax.fori_loop(0, patches, one, 0, unroll=4)
    chl = chl_ref[...].reshape(flat)
    absorbed, _ = light(chl, level_sums(chl, level_matrix(levels, "prefix")), level_of(flat))
    wet = wet_of(depth_ref[0], whole)
    for band in range(2):
        band_ref[:, band] = wet * absorbed[band].reshape(whole)


def last_ocean_kernel(
    sc, speed_ref, t_ref, north_ref, south_ref, east_ref, west_ref, depth_ref, heat_ref, out_ref, div_ref
):
    rows, cols, levels = t_ref.shape
    place = lax.broadcasted_iota(jnp.int32, (cols, levels), 0)
    sources = (speed_ref.at[0], speed_ref.at[1], t_ref)
    for y in range(rows):
        wet = [wet_of(depth_ref[i, y], (cols, levels)) for i in range(5)]

        def east_of(f):
            return jnp.where(place == cols - 1, east_ref[f, pl.ds(y, 1)], pltpu.roll(sources[f][y], cols - 1, 0))

        def west_of(f):
            return jnp.where(place == 0, west_ref[f, pl.ds(y, 1)], pltpu.roll(sources[f][y], 1, 0))

        def north_of(f):
            return sources[f][y + 1] if y < rows - 1 else north_ref[f]

        def south_of(f):
            return sources[f][y - 1] if y > 0 else south_ref[f]

        u, v, t = (ref[y] for ref in sources)
        own = 0.5 * wet[0]
        east = (u + east_of(0)) * (own * wet[1])
        west = (west_of(0) + u) * (own * wet[2])
        north = (v + north_of(1)) * (own * wet[3])
        south = (south_of(1) + v) * (own * wet[4])
        div_ref[y] = east - west + north - south
        e, w, n, s = east_of(2), west_of(2), north_of(2), south_of(2)
        spread = wet[1] * (e - t) + wet[2] * (w - t) + wet[3] * (n - t) + wet[4] * (s - t)
        carry_along = 0.5 * (east * (t + e) - west * (w + t) + north * (t + n) - south * (s + t))
        change = spreading * spread - carry_along
        out_ref[1, sc[1 + y], 1] = wet[0] * (t + advance_marine * change) + heat_ref[y]
    sums = level_sums(div_ref[...].reshape(rows * cols, levels), level_matrix(levels, "below"))
    div_ref[...] = -sums.reshape(rows, cols, levels)
    for y in range(rows):
        out_ref[1, sc[1 + y], 0] = div_ref[y]
    out_ref[0] = jnp.zeros(out_ref.shape[1:], jnp.float32)


def join_kernel(sc, absorbed_ref, flux_ref, other_ref, out_ref):
    patches, _, half, levels = absorbed_ref.shape

    @pl.when(sc[0] == 0)
    def _():
        for s in range(patches):
            for f in range(2):
                out_ref[f, s, :half] = absorbed_ref[s, f]
                out_ref[f, s, half:] = other_ref[s, f]

    @pl.when(sc[0] != 0)
    def _():
        for s in range(patches):
            for f in range(2):
                for part in range(2):
                    out_ref[f, s, part * half : (part + 1) * half] = flux_ref[part, s, f]


def call(kernel, comp, args, specs, outs, scratch=(), name=None, sems=()):
    return pl.pallas_call(
        kernel,
        grid_spec=pltpu.PrefetchScalarGridSpec(
            num_scalar_prefetch=1,
            grid=(1,),
            in_specs=[spec or whole(a) for spec, a in zip(specs, args)],
            out_specs=[whole(o) for o in outs],
            scratch_shapes=[pltpu.VMEM(s, jnp.float32) for s in scratch] + list(sems),
        ),
        out_shape=outs,
        compiler_params=PARAMS,
        name=name,
    )(comp, *args)


def exchange_rows(low, high):
    count = lax.axis_size("py")
    north = lax.ppermute(low, "py", [((i + 1) % count, i) for i in range(count)])
    south = lax.ppermute(high, "py", [(i, (i + 1) % count) for i in range(count)])
    return north, south


def exchange_cols(low, high):
    count = lax.axis_size("px")
    east = lax.ppermute(low, "px", [((i + 1) % count, i) for i in range(count)])
    west = lax.ppermute(high, "px", [(i, (i + 1) % count) for i in range(count)])
    return east, west


def exchange_half_cols(low, high):
    count = lax.axis_size("px")
    line = [(h % 2) * count + h // 2 for h in range(2 * count)]
    ahead = [(line[h], line[(h + 1) % len(line)]) for h in range(len(line))]
    east = lax.ppermute(low, ("comp", "px"), [(b, a) for a, b in ahead])
    west = lax.ppermute(high, ("comp", "px"), ahead)
    return east, west


def in_hbm(x):
    return pltpu.with_memory_space_constraint(x, pltpu.HBM)


def in_vmem(x):
    return pltpu.with_memory_space_constraint(x, pltpu.VMEM)


def to_owners(blocks):
    return lax.all_to_all(blocks, ("py", "px"), split_axis=0, concat_axis=0, tiled=True)


def swap(block):
    return lax.ppermute(block, "comp", [(0, 1), (1, 0)])


def pick(blocks, order, axis):
    return jnp.stack(
        [lax.dynamic_index_in_dim(blocks, order[k], axis, keepdims=False) for k in range(order.shape[0])], axis
    )


def table(levels, pattern):
    return level_matrix(levels, pattern).astype(jnp.float32)


def product(values, matrix):
    return jnp.einsum("...j,jk->...k", values, matrix, precision=lax.Precision.HIGHEST)


def general_light(conc, wet, loading):
    chl = jax.nn.softplus(jnp.einsum("f...,f->...", conc, loading, precision=lax.Precision.HIGHEST))
    levels = chl.shape[-1]
    absorbed, irradiance = light(chl, product(chl, table(levels, "prefix")), level_of(chl.shape))
    return wet * jnp.stack(absorbed), irradiance


def general_tracers(conc, rise, heat, irradiance, wet, matrix, share):
    none = jnp.zeros_like(conc[..., :1])
    top = jnp.concatenate([none, 0.5 * (conc[..., 1:] + conc[..., :-1]) * rise[..., 1:]], axis=-1)
    below = jnp.concatenate([top[..., 1:], none], axis=-1)
    mixed = jnp.einsum("ij,j...->i...", matrix, conc, precision=lax.Precision.HIGHEST)
    growth = uptake_rate * irradiance * saturation(conc[0])
    change = (
        jnp.exp(heating_speed * heat) * mixed
        + share.reshape((-1,) + (1,) * (conc.ndim - 1)) * growth + below - top
    )
    return wet * (conc + step_tracer * change)


def general_ocean(u, v, t, absorb, depth, coriolis):
    levels = t.shape[-1]
    fields = jnp.stack([u, v, t])
    north, south = exchange_rows(fields[:, 0], fields[:, -1])
    east, west = exchange_cols(fields[:, :, 0], fields[:, :, -1])
    tall = jnp.concatenate([south[:, None], fields, north[:, None]], axis=1)
    wide = jnp.concatenate([west[:, :, None], fields, east[:, :, None]], axis=2)
    around = (fields, wide[:, :, 2:], wide[:, :, :-2], tall[:, 2:], tall[:, :-2])
    above = table(levels, "above")
    u, v, t = ([x[f] for x in around] for f in range(3))
    p = [weight_pull_factor * product(x, above) for x in t]
    wet = [wet_of(depth[i], t[0].shape) for i in range(5)]

    def spread(x):
        return sum(wet[i] * (x[i] - x[0]) for i in range(1, 5))

    east = 0.5 * (u[0] + u[1]) * wet[0] * wet[1]
    west = 0.5 * (u[2] + u[0]) * wet[2] * wet[0]
    north = 0.5 * (v[0] + v[3]) * wet[0] * wet[3]
    south = 0.5 * (v[4] + v[0]) * wet[4] * wet[0]
    carry_along = 0.5 * (
        east * (t[0] + t[1]) - west * (t[2] + t[0]) + north * (t[0] + t[3]) - south * (t[4] + t[0])
    )
    zonal = 0.5 * (wet[1] * (p[1] - p[0]) + wet[2] * (p[0] - p[2]))
    merid = 0.5 * (wet[3] * (p[3] - p[0]) + wet[4] * (p[0] - p[4]))
    turn = coriolis[:, None, None]
    rise = -product(east - west + north - south, table(levels, "below"))
    return (
        wet[0] * (u[0] + advance_marine * (turn * v[0] - zonal + viscosity * spread(u) - damping * u[0])),
        wet[0] * (v[0] + advance_marine * (-turn * u[0] - merid + viscosity * spread(v) - damping * v[0])),
        wet[0] * (t[0] + advance_marine * (spreading * spread(t) - carry_along + heat_gain * (absorb[0] + absorb[1]))),
        rise,
    )


def general(linked, u, v, t, tracers, depth, tracer_depth, holder_rank, patch_index, coriolis, matrix, share, loading):
    comp_index = lax.axis_index("comp")
    first = comp_index == 0
    fields, patches, strip, levels = tracers.shape
    half = strip // 2
    indices = jnp.arange(patches, dtype=jnp.int32)
    owner_row = lax.dynamic_index_in_dim(holder_rank, patch_index, 0, keepdims=False)
    inverse_row = jnp.sum(jnp.where(owner_row[:, None] == indices[None], indices[:, None], 0), axis=0)

    def own_half(x):
        return lax.dynamic_slice_in_dim(x, comp_index * half, half, x.ndim - 2)

    partner = swap(linked)
    absorb = jnp.where(first, linked, partner)
    flux = own_half(jnp.where(first, partner, linked))
    conc = own_half(tracers)
    wet = wet_of(tracer_depth, conc.shape[1:])
    irradiance = general_light(conc, wet, loading)[1]
    grid = t.shape
    for _ in range(3):
        u, v, t, rise = general_ocean(u, v, t, absorb.reshape((2,) + grid), depth, coriolis)
        conc = general_tracers(conc, flux[0], flux[1], irradiance, wet, matrix, share)
        absorbed, irradiance = general_light(conc, wet, loading)
        both = own_half(pick(jnp.stack([rise, t]).reshape(2, patches, strip, levels), inverse_row, 1))
        send = jnp.concatenate([both, absorbed])
        back = lax.all_to_all(send, ("py", "px"), split_axis=1, concat_axis=1, tiled=True)
        flux = back[:2]
        mine = pick(back[2:], owner_row, 1)
        other = swap(mine)
        absorb = jnp.where(first, jnp.concatenate([mine, other], 2), jnp.concatenate([other, mine], 2))
    other = swap(flux)
    joined = jnp.where(first, jnp.concatenate([flux, other], 2), jnp.concatenate([other, flux], 2))
    return jnp.where(first, absorb, joined)


def shards(
    current_speeds,
    thermal_anomaly,
    solute_amounts,
    delayed_link_source,
    marine_indicator,
    floor_layer_index,
    holder_rank,
    biota_exchange_matrix,
    photic_absorb_share,
    chroma_loading,
):
    comp_index = lax.axis_index("comp")
    row_index = lax.axis_index("py")
    col_index = lax.axis_index("px")
    rows_mesh = lax.axis_size("py")
    cols_mesh = lax.axis_size("px")
    patches = rows_mesh * cols_mesh
    fields, _, columns, levels = solute_amounts.shape
    strip = columns // patches
    half = strip // 2
    patch_index = row_index * cols_mesh + col_index
    first = comp_index == 0

    linked = delayed_link_source.reshape(2, patches, strip, levels)
    tracers = solute_amounts.reshape(fields, patches, strip, levels)
    u0, v0 = current_speeds[0], current_speeds[1]

    column_depth = marine_indicator * floor_layer_index
    wrapped = jnp.concatenate([column_depth[:, -1:], column_depth, column_depth[:, :1]], axis=1)
    padded = jnp.pad(wrapped, ((1, 1), (0, 0)))
    local = lax.dynamic_slice(padded, (row_index * CY, col_index * CX), (CY + 2, CX + 2))
    depth = jnp.stack([local[1:-1, 1:-1], local[1:-1, 2:], local[1:-1, :-2], local[2:, 1:-1], local[:-2, 1:-1]])
    depth = depth[..., None]
    by_strip = (
        column_depth.reshape(rows_mesh, CY, cols_mesh, CX).transpose(0, 2, 1, 3).reshape(patches, patches, strip)
    )
    here = (holder_rank == patch_index)[:, :, None]
    tracer_depth = jnp.sum(jnp.where(here, by_strip, 0), axis=1)
    tracer_depth = lax.dynamic_slice_in_dim(tracer_depth, comp_index * half, half, 1)[..., None]
    owner_row = lax.dynamic_index_in_dim(holder_rank, patch_index, 0, keepdims=False)
    side_index = comp_index.astype(jnp.int32)[None]
    comp = jnp.concatenate([side_index, owner_row])
    ys = (row_index * CY + jnp.arange(CY, dtype=jnp.int32)).astype(jnp.float32)
    coriolis = coriolis_scale * (2.0 * (ys + 0.5) / (CY * rows_mesh) - 1.0)

    if half % 8:
        out = general(
            linked, u0, v0, thermal_anomaly, tracers, depth, tracer_depth, holder_rank, patch_index, coriolis,
            biota_exchange_matrix, photic_absorb_share, chroma_loading,
        )
        return out.reshape(1, 2, 1, columns, levels)

    linked, tracers, current_speeds, thermal_anomaly = (
        in_hbm(x) for x in (linked, tracers, current_speeds, thermal_anomaly)
    )
    sent, *edges = pack(side_index, linked, current_speeds, thermal_anomaly)
    got = swap(sent)
    times = functools.partial(jnp.dot, precision=lax.Precision.HIGHEST)
    unit = (jnp.arange(fields) == 0).astype(jnp.float32)
    chain = [jnp.stack([chroma_loading, unit])]
    for _ in range(3):
        chain.append(times(chain[-1], biota_exchange_matrix))
    weights = jnp.stack([c[0] for c in chain] + [c[1] for c in chain[:3]])
    shares = times(weights, photic_absorb_share)

    projected, g = project(side_index, tracers, weights)
    edges, projected, g = lax.optimization_barrier((edges, projected, g))
    projected, g = in_vmem(projected), in_vmem(g)
    halos0 = exchange_rows(edges[0], edges[1]) + exchange_cols(edges[2], edges[3])
    kept = first_tracer(side_index, projected, g, got, linked, tracer_depth, shares)
    kept, halos0 = lax.optimization_barrier((kept, halos0))
    arrived = to_owners(kept)

    speeds1, t1, r1, *edges = ocean(1, comp, coriolis, current_speeds, thermal_anomaly, halos0, depth, linked, got)
    halos1 = exchange_rows(edges[0], edges[1]) + exchange_cols(edges[2], edges[3])
    speeds1, t1, r1 = in_vmem(speeds1), in_vmem(t1), in_hbm(r1)
    speeds2, t2, r2 = ocean(2, comp, coriolis, speeds1, t1, halos1, depth)
    arrived, speeds2, t2 = lax.optimization_barrier((arrived, speeds2, t2))
    speeds2, t2, r2 = in_hbm(speeds2), in_hbm(t2), in_hbm(r2)

    patch_half = half_spec((CY,), half, levels)
    speeds_half = half_spec((2, CY), half, levels)
    depth_half = pl.BlockSpec((5, CY, half, 1), lambda i, c: (0, 0, c[0], 0))
    piece = shape_of(CY, half, levels)
    scratch = (CY, half, levels)
    line = shape_of(3, half, levels)
    side = shape_of(3, CY, levels)

    t2, irr1, *edges = call(
        absorb_kernel, comp, (arrived, t2, speeds2, depth), [HBM, patch_half, speeds_half, depth_half],
        (piece, piece, line, line, side, side), [scratch] * 2, "absorb", [pltpu.SemaphoreType.DMA],
    )
    halos2 = exchange_rows(edges[0], edges[1]) + exchange_half_cols(edges[2], edges[3])
    heat, a, b, g = call(
        second_kernel, comp, (arrived, irr1, t1, r1, depth, shares),
        [None, None, patch_half, patch_half, depth_half, SMEM],
        (piece,) * 4, [scratch] * 2, "second",
    )
    [back] = call(
        last_ocean_kernel, comp, (speeds2, t2, *halos2, depth, heat),
        [speeds_half] + [None] * 5 + [depth_half, None],
        (shape_of(2, patches, 2, half, levels),), [scratch], "last_ocean",
    )
    flux = lax.all_to_all(
        back.reshape(2 * patches, 2, half, levels), ("comp", "py", "px"), split_axis=0, concat_axis=0, tiled=True
    ).reshape(2, patches, 2, half, levels)
    [absorbed] = call(
        third_kernel, comp, (a, b, g, t2, r2, depth, shares),
        [None] * 4 + [patch_half, depth_half, SMEM], (shape_of(CY, 2, half, levels),), [scratch], "third",
    )
    other = swap(absorbed)
    [out] = call(
        join_kernel, comp, (absorbed, flux, other), [None] * 3, (shape_of(2, patches, strip, levels),), (), "join"
    )
    return out.reshape(1, 2, 1, columns, levels)


def solution(mesh):
    placed = (
        P(None, "py", "px", None),
        P("py", "px", None),
        P(None, ("py", "px"), None, None),
        P("comp", None, ("py", "px"), None, None),
        P(),
        P(),
        P(),
        P(),
        P(),
        P(),
    )
    return jax.shard_map(
        shards,
        mesh=mesh,
        in_specs=placed,
        out_specs=P("comp", None, ("py", "px"), None, None),
        check_vma=False,
    )
```

```python
import functools

import jax
import jax.numpy as jnp
from jax import lax
from jax.experimental import pallas as pl
from jax.experimental.pallas import tpu as pltpu
from jax.sharding import PartitionSpec as P

advance_marine = 0.1
spreading = 0.1
viscosity = 0.1
damping = 0.05
heat_gain = 0.2
weight_pull_factor = 0.05
coriolis_scale = 1.0
step_tracer = 0.1
heating_speed = 0.06
uptake_rate = 0.01
water_absorb = (0.02, 0.003)
pigment_absorb = (0.03, 0.004)
surface_light = (40.0, 60.0)
CY = 16
CX = 32
KEPT = (0, 1, 2, 4, 5)
SMEM = pl.BlockSpec(memory_space=pltpu.SMEM)
PARAMS = pltpu.CompilerParams(vmem_limit_bytes=28 * 1024 * 1024)
HBM = pl.BlockSpec(memory_space=pltpu.HBM)
STREAMED = pltpu.CompilerParams(vmem_limit_bytes=60 * 1024 * 1024)


def whole(array):
    zeros = (0,) * len(array.shape)
    return pl.BlockSpec(array.shape, lambda i, c: zeros)


def shape_of(*dims):
    return jax.ShapeDtypeStruct(dims, jnp.float32)


def level_matrix(levels, pattern):
    row = lax.broadcasted_iota(jnp.int32, (levels, levels), 0)
    col = lax.broadcasted_iota(jnp.int32, (levels, levels), 1)
    if pattern == "above":
        m = jnp.where(row < col, 1.0, jnp.where(row == col, 0.5, 0.0))
    elif pattern == "below":
        m = jnp.where(row >= col, 1.0, 0.0)
    else:
        m = jnp.where(row < col, 1.0, 0.0)
    return m.astype(jnp.bfloat16)


def level_sums(x, matrix):
    hi = x.astype(jnp.bfloat16)
    rest = x - hi.astype(jnp.float32)
    mid = rest.astype(jnp.bfloat16)
    low = (rest - mid.astype(jnp.float32)).astype(jnp.bfloat16)
    dot = functools.partial(jnp.dot, preferred_element_type=jnp.float32)
    return dot(hi, matrix) + dot(mid, matrix) + dot(low, matrix)


def softplus(x):
    return jnp.maximum(x, 0.0) + jnp.log1p(jnp.exp(-jnp.abs(x)))


def light(chl, sums, level):
    absorbed, irradiance = [], None
    for water, pigment, surface in zip(water_absorb, pigment_absorb, surface_light):
        fade = jnp.exp(-0.5 * (water + pigment * chl))
        intensity = surface * jnp.exp(-(water * level + pigment * sums))
        absorbed.append(intensity * (1.0 - fade * fade))
        part = intensity * fade
        irradiance = part if irradiance is None else irradiance + part
    return absorbed, irradiance


def saturation(n):
    return n * n / (1.0 + n * n)


def transport(rise_half, y):
    top = rise_half * (y + pltpu.roll(y, 1, 1))
    return pltpu.roll(top, top.shape[1] - 1, 1) - top


def wet_of(depth, shape):
    level = lax.broadcasted_iota(jnp.int32, shape, len(shape) - 1)
    return jnp.where(level < depth, 1.0, 0.0)


def level_of(shape):
    return lax.broadcasted_iota(jnp.int32, shape, len(shape) - 1).astype(jnp.float32)


def half_rise(rise):
    k = lax.broadcasted_iota(jnp.int32, rise.shape, 1)
    return jnp.where(k > 0, 0.5 * rise, 0.0)


def project_kernel(sc, x_hbm, w_ref, y_ref, g_ref, x_ref, chl_ref, sems):
    pieces, fields, block, cols, levels = x_ref.shape
    own = pl.ds(pl.multiple_of(sc[0] * cols, cols), cols)
    copies = [
        pltpu.make_async_copy(x_hbm.at[:, pl.ds(i * block, block), own], x_ref.at[i], sems.at[i]) for i in range(pieces)
    ]
    for copy in copies:
        copy.start()
    mixed = [k for k in range(y_ref.shape[0]) if k != 4]
    prefix = level_matrix(levels, "prefix")
    flat = (block * cols, levels)
    for i, copy in enumerate(copies):
        copy.wait()

        def one(q, carry):
            at = i * block + q
            value = x_ref[i, 0, q]
            y_ref[4, at] = value
            totals = [w_ref[k, 0] * value for k in mixed]
            for j in range(1, fields):
                value = x_ref[i, j, q]
                totals = [t + w_ref[k, j] * value for t, k in zip(totals, mixed)]
            for k, total in zip(mixed, totals):
                y_ref[k, at] = total
            chl_ref[q] = softplus(totals[0])
            return carry

        lax.fori_loop(0, block, one, 0)
        chl = chl_ref[...].reshape(flat)
        _, irradiance = light(chl, level_sums(chl, prefix), level_of(flat))
        n = x_ref[i, 0].reshape(flat)
        g_ref[i * block : (i + 1) * block] = (uptake_rate * irradiance * saturation(n)).reshape(block, cols, levels)


def project(comp, tracers, weights):
    fields, patches, strip, levels = tracers.shape
    half = strip // 2
    pieces = 4
    block = patches // pieces
    outs = (shape_of(weights.shape[0], patches, half, levels), shape_of(patches, half, levels))
    return pl.pallas_call(
        project_kernel,
        grid_spec=pltpu.PrefetchScalarGridSpec(
            num_scalar_prefetch=1,
            grid=(1,),
            in_specs=[HBM, SMEM],
            out_specs=[whole(o) for o in outs],
            scratch_shapes=[
                pltpu.VMEM((pieces, fields, block, half, levels), jnp.float32),
                pltpu.VMEM((block, half, levels), jnp.float32),
                pltpu.SemaphoreType.DMA((pieces,)),
            ],
        ),
        out_shape=outs,
        compiler_params=PARAMS,
        name="project",
    )(comp, tracers, weights)


def first_tracer_kernel(sc, y_ref, g_ref, got_ref, own_ref, depth_ref, share_ref, out_ref):
    patches, cols, levels = g_ref.shape
    first = sc[0] == 0

    def one(q, carry):
        rise = jnp.where(first, got_ref[0, q], own_ref[0, q])
        heat = jnp.where(first, got_ref[1, q], own_ref[1, q])
        warm = jnp.exp(heating_speed * heat)
        wet = wet_of(depth_ref[q], (cols, levels))
        up = half_rise(rise)
        g = g_ref[q]
        for place, k in enumerate(KEPT):
            y = y_ref[k, q]
            change = warm * y_ref[k + 1, q] + share_ref[k] * g + transport(up, y)
            out_ref[q, place] = wet * (y + step_tracer * change)
        return carry

    lax.fori_loop(0, patches, one, 0, unroll=2)


def half_spec(lead, cols, levels):
    zeros = (0,) * len(lead)
    return pl.BlockSpec(lead + (cols, levels), lambda i, c: zeros + (c[0], 0))


def first_tracer(comp, projected, g, got, linked, depth, shares):
    kinds, patches, half, levels = projected.shape
    block = 4
    return pl.pallas_call(
        first_tracer_kernel,
        grid_spec=pltpu.PrefetchScalarGridSpec(
            num_scalar_prefetch=1,
            grid=(patches // block,),
            in_specs=[
                pl.BlockSpec((kinds, block, half, levels), lambda i, c: (0, i, 0, 0)),
                pl.BlockSpec((block, half, levels), lambda i, c: (i, 0, 0)),
                pl.BlockSpec((2, block, half, levels), lambda i, c: (0, i, 0, 0)),
                pl.BlockSpec((2, block, half, levels), lambda i, c: (0, i, c[0], 0)),
                pl.BlockSpec((block, half, 1), lambda i, c: (i, 0, 0)),
                SMEM,
            ],
            out_specs=pl.BlockSpec((block, len(KEPT), half, levels), lambda i, c: (i, 0, 0, 0)),
        ),
        out_shape=shape_of(patches, len(KEPT), half, levels),
        compiler_params=PARAMS,
        name="first_tracer",
    )(comp, projected, g, got, linked, depth, shares)


def pack_kernel(sc, linked_ref, row0_ref, row1_ref, col0_ref, col1_ref, t0_ref, t1_ref, tc0_ref, tc1_ref,
                sent_ref, low_ref, high_ref, left_ref, right_ref):
    _, strips, strip, levels = linked_ref.shape
    half = strip // 2

    @pl.when(sc[0] == 0)
    def _():
        for part in range(2):
            cols = slice(part * half, (part + 1) * half)
            sent_ref[part] = linked_ref[0, :, cols] + linked_ref[1, :, cols]

    @pl.when(sc[0] != 0)
    def _():
        sent_ref[...] = linked_ref[:, :, :half]

    last = col1_ref.shape[2]
    tall = strips - 2
    for i in range(2):
        for f in range(2):
            left_ref[f, i] = col0_ref[f, :, i]
            right_ref[f, i] = col1_ref[f, :, last - 2 + i]
        left_ref[2, i] = tc0_ref[:, i]
        right_ref[2, i] = tc1_ref[:, last - 2 + i]
        left_ref[3, i] = linked_ref[0, :, i] + linked_ref[1, :, i]
        right_ref[3, i] = linked_ref[0, :, strip - 2 + i] + linked_ref[1, :, strip - 2 + i]
    for f in range(2):
        low_ref[f] = row0_ref[f]
        high_ref[f] = row1_ref[f]
    low_ref[2] = t0_ref[...]
    high_ref[2] = t1_ref[...]
    low_ref[3] = linked_ref[0, :2] + linked_ref[1, :2]
    high_ref[3] = linked_ref[0, tall:] + linked_ref[1, tall:]


def corner_kernel(sc, left_ref, right_ref, north_ref, south_ref, low_ref, high_ref):
    rows = left_ref.shape[2]
    cols = north_ref.shape[2]
    for source, target, at in ((left_ref, low_ref, 0), (right_ref, high_ref, cols - 2)):
        for f in range(source.shape[0]):
            for i in range(2):
                target[f, i, :rows] = source[f, i]
                target[f, i, rows : rows + 1] = south_ref[f, 1, at + i : at + i + 1]
                target[f, i, rows + 1 :] = north_ref[f, 0, at + i : at + i + 1]


def ring_places(rows, cols):
    tall = -(-(rows + 2) // 8) * 8
    return 2 * cols, 2 * cols + tall, 2 * cols + 2 * tall


def ring_kernel(sc, north_ref, south_ref, east_ref, west_ref, ring_ref):
    cols = north_ref.shape[2]
    tall = east_ref.shape[2]
    at_east, at_west, _ = ring_places(tall - 2, cols)
    ring_ref[...] = jnp.zeros(ring_ref.shape, jnp.float32)
    ring_ref[:cols] = south_ref[3, 1]
    ring_ref[cols : 2 * cols] = north_ref[3, 0]
    ring_ref[at_east : at_east + tall] = east_ref[3, 0]
    ring_ref[at_west : at_west + tall] = west_ref[3, 1]


def pack(comp, linked, speeds, heat):
    _, strips, strip, levels = linked.shape
    rows, cols, _ = heat.shape
    outs = (
        shape_of(2, strips, strip // 2, levels), shape_of(4, 2, cols, levels), shape_of(4, 2, cols, levels),
        shape_of(4, 2, rows, levels), shape_of(4, 2, rows, levels),
    )
    edge = min(8, cols)
    return pl.pallas_call(
        pack_kernel,
        grid_spec=pltpu.PrefetchScalarGridSpec(
            num_scalar_prefetch=1,
            grid=(1,),
            in_specs=[
                whole(linked),
                pl.BlockSpec((2, 2, cols, levels), lambda i, c: (0, 0, 0, 0)),
                pl.BlockSpec((2, 2, cols, levels), lambda i, c: (0, rows // 2 - 1, 0, 0)),
                pl.BlockSpec((2, rows, edge, levels), lambda i, c: (0, 0, 0, 0)),
                pl.BlockSpec((2, rows, edge, levels), lambda i, c: (0, 0, cols // edge - 1, 0)),
                pl.BlockSpec((2, cols, levels), lambda i, c: (0, 0, 0)),
                pl.BlockSpec((2, cols, levels), lambda i, c: (rows // 2 - 1, 0, 0)),
                pl.BlockSpec((rows, edge, levels), lambda i, c: (0, 0, 0)),
                pl.BlockSpec((rows, edge, levels), lambda i, c: (0, cols // edge - 1, 0)),
            ],
            out_specs=[whole(o) for o in outs],
        ),
        out_shape=outs,
        compiler_params=STREAMED,
        name="pack",
    )(comp, linked, speeds, speeds, speeds, speeds, heat, heat, heat, heat)


def wide_rows(speed_hbm, heat_hbm, linked_hbm, got_ref, north_ref, south_ref, east_ref, west_ref, own_ref, other_ref,
              first, x_ref, absorb_ref, ring_absorb_ref, linked_ref, sems):
    rows, cols, levels = heat_hbm.shape
    width = x_ref.shape[2]
    inner = (pl.ds(2, rows), pl.ds(0, cols))
    copies = [
        pltpu.make_async_copy(linked_hbm, linked_ref, sems.at[0]),
        pltpu.make_async_copy(heat_hbm, x_ref.at[2, *inner], sems.at[1]),
        pltpu.make_async_copy(speed_hbm.at[0], x_ref.at[0, *inner], sems.at[2]),
        pltpu.make_async_copy(speed_hbm.at[1], x_ref.at[1, *inner], sems.at[3]),
    ]
    for copy in copies:
        copy.start()
    place = lax.broadcasted_iota(jnp.int32, (width - cols, levels), 0)
    none = jnp.zeros((width - cols, levels), jnp.float32)
    line = [rows, *range(rows), rows + 1]
    for f in range(3):
        x_ref[f, :2, :cols] = south_ref[f]
        x_ref[f, rows + 2 :, :cols] = north_ref[f]
        x_ref[f, 0, cols:] = none
        x_ref[f, rows + 3, cols:] = none
        for o, r in enumerate(line):
            cells = none
            for i in range(2):
                cells = jnp.where(place == i, east_ref[f, i, r : r + 1], cells)
                cells = jnp.where(place == width - cols - 2 + i, west_ref[f, i, r : r + 1], cells)
            x_ref[f, o + 1, cols:] = cells
    ring_absorb_ref[...] = jnp.where(first, own_ref[...], other_ref[...])
    absorb_ref[0, :cols] = ring_absorb_ref[:cols]
    absorb_ref[rows + 1, :cols] = ring_absorb_ref[cols : 2 * cols]
    at_east, at_west, _ = ring_places(rows, cols)
    for o, r in enumerate(line):
        e = ring_absorb_ref[at_east + r : at_east + r + 1]
        w = ring_absorb_ref[at_west + r : at_west + r + 1]
        absorb_ref[o, cols:] = jnp.where(place == 0, e, jnp.where(place == width - cols - 1, w, 0.0))
    copies[0].wait()
    for y in range(rows):
        absorb_ref[y + 1, :cols] = jnp.where(
            first, linked_ref[0, y] + linked_ref[1, y], jnp.concatenate([got_ref[0, y], got_ref[1, y]], axis=0)
        )
    for copy in copies[1:]:
        copy.wait()


def ocean_kernel(advance, sc, coriolis_ref, *refs):
    if advance == 1:
        *sources, depth_ref, next_ref, tn_ref, inner_ref, rise_ref, x_ref, absorb_ref = refs[: -5]
        ring_absorb_ref, linked_ref, sems, p_ref, div_ref = refs[-5:]
        wide_rows(*sources, sc[0] == 0, x_ref, absorb_ref, ring_absorb_ref, linked_ref, sems)
        fields = [x_ref.at[f] for f in range(3)]
    else:
        speed_ref, t_ref, depth_ref, next_ref, tn_ref, rise_ref, p_ref, div_ref = refs
        fields = [speed_ref.at[0], speed_ref.at[1], t_ref]
    tall, width, levels = p_ref.shape
    rows, cols = rise_ref.shape[:2]
    out_width = tn_ref.shape[1]
    p_ref[...] = (
        weight_pull_factor * level_sums(fields[2][...].reshape(tall * width, levels), level_matrix(levels, "above"))
    ).reshape(tall, width, levels)
    lanes = min(128, levels)

    def piece(o, lane):
        part = slice(lane, lane + lanes)
        level = lane + lax.broadcasted_iota(jnp.int32, (width, lanes), 1)

        def beside(x):
            return pltpu.roll(x, width - 1, 0), pltpu.roll(x, 1, 0)

        def field(ref):
            x = ref[o + 1, :, part]
            return (x, *beside(x), ref[o + 2, :, part], ref[o, :, part])

        def wet_at(d):
            return jnp.where(level < depth_ref[d], 1.0, 0.0)

        here = wet_at(o + advance)
        wet = (here, *beside(here), wet_at(o + advance + 1), wet_at(o + advance - 1))
        u, v, t, p = (field(ref) for ref in (*fields, p_ref))
        own = 0.5 * wet[0]
        east = (u[0] + u[1]) * (own * wet[1])
        west = (u[2] + u[0]) * (own * wet[2])
        north = (v[0] + v[3]) * (own * wet[3])
        south = (v[4] + v[0]) * (own * wet[4])
        div_ref[o, :, part] = east - west + north - south
        wets = wet[1] + wet[2] + wet[3] + wet[4]

        def spread(x):
            return wet[1] * x[1] + wet[2] * x[2] + wet[3] * x[3] + wet[4] * x[4] - wets * x[0]

        carry_along = 0.5 * (
            east * (t[0] + t[1]) - west * (t[2] + t[0]) + north * (t[0] + t[3]) - south * (t[4] + t[0])
        )
        change = spreading * spread(t) - carry_along
        if advance == 1:
            change = change + heat_gain * absorb_ref[o, :, part]
        zonal = 0.5 * (wet[1] * (p[1] - p[0]) + wet[2] * (p[0] - p[2]))
        merid = 0.5 * (wet[3] * (p[3] - p[0]) + wet[4] * (p[0] - p[4]))
        turn = coriolis_ref[o + advance - 1]
        results = (
            wet[0] * (u[0] + advance_marine * (turn * v[0] - zonal + viscosity * spread(u) - damping * u[0])),
            wet[0] * (v[0] + advance_marine * (-turn * u[0] - merid + viscosity * spread(v) - damping * v[0])),
            wet[0] * (t[0] + advance_marine * change),
        )
        for ref, value in zip((next_ref.at[0], next_ref.at[1], tn_ref), results):
            ref[o, :, part] = value[:out_width]

    def row(o, carry):
        for lane in range(0, levels, lanes):
            piece(o, lane)
        return carry

    lax.fori_loop(0, tall - 2, row, 0)
    rim = (tall - 2 - rows) // 2
    div = div_ref[rim : rim + rows, :cols].reshape(rows * cols, levels)
    rise_ref[...] = -level_sums(div, level_matrix(levels, "below")).reshape(rows, cols, levels)
    if advance == 1:
        inner_ref[...] = tn_ref[rim : rim + rows, :cols]


def ocean(advance, comp, coriolis, args, depth, rows, cols):
    width, levels = depth.shape[1], args[1].shape[-1]
    patch = shape_of(rows, cols, levels)
    if advance == 1:
        tall = rows + 4
        outs = (shape_of(2, rows + 2, width, levels), shape_of(rows + 2, width, levels), patch, patch)
        scratch = [
            pltpu.VMEM((3, tall, width, levels), jnp.float32),
            pltpu.VMEM((rows + 2, width, levels), jnp.float32),
            pltpu.VMEM(args[-1].shape, jnp.float32),
            pltpu.VMEM(args[2].shape, jnp.float32),
            pltpu.SemaphoreType.DMA((4,)),
        ]
    else:
        tall = rows + 2
        outs = (shape_of(2, rows, cols, levels), patch, patch)
        scratch = []
    scratch += [
        pltpu.VMEM((tall, width, levels), jnp.float32), pltpu.VMEM((tall - 2, width, levels), jnp.float32)
    ]
    args = [coriolis, *args, depth]
    own_copies = 3 if advance == 1 else 0
    return pl.pallas_call(
        functools.partial(ocean_kernel, advance),
        grid_spec=pltpu.PrefetchScalarGridSpec(
            num_scalar_prefetch=1,
            grid=(1,),
            in_specs=[SMEM] + [HBM] * own_copies + [whole(x) for x in args[1 + own_copies :]],
            out_specs=[whole(o) for o in outs],
            scratch_shapes=scratch,
        ),
        out_shape=outs,
        compiler_params=PARAMS,
        name=f"ocean{advance}",
    )(comp, *args)


def absorb_kernel(
    sc, y_hbm, t_ref, speed_ref, depth_ref, t2_ref, irr_ref, row0_ref, row1_ref, col0_ref, col1_ref, chl_ref, y_ref, sem
):
    rows, cols, levels = t_ref.shape
    flat = (rows * cols, levels)
    copy = pltpu.make_async_copy(y_hbm.at[:, 0], y_ref, sem)
    copy.start()
    copy.wait()

    def gather(s, carry):
        chl_ref[s] = softplus(y_ref[sc[1 + s]])
        return carry

    lax.fori_loop(0, rows, gather, 0, unroll=2)
    chl = chl_ref[...].reshape(flat)
    sums = level_sums(chl, level_matrix(levels, "prefix"))
    absorbed, irradiance = light(chl, sums, level_of(flat))
    wet = wet_of(depth_ref[0], t_ref.shape)
    both = (absorbed[0] + absorbed[1]).reshape(t_ref.shape)
    t2_ref[...] = t_ref[...] + advance_marine * heat_gain * (wet * both)
    irr_ref[...] = irradiance.reshape(t_ref.shape)
    for f, ref in enumerate((speed_ref.at[0], speed_ref.at[1], t2_ref)):
        row0_ref[f] = ref[0]
        row1_ref[f] = ref[rows - 1]
        for y in range(rows):
            col0_ref[f, pl.ds(y, 1)] = ref[y, :1]
            col1_ref[f, pl.ds(y, 1)] = ref[y, cols - 1 :]


def second_kernel(
    sc, y_ref, irr_ref, t1_ref, r1_ref, depth_ref, share_ref, heat_ref, a_ref, b_ref, g_ref, n_ref, chl_ref
):
    patches, _, cols, levels = y_ref.shape
    flat = (patches * cols, levels)
    whole = (patches, cols, levels)

    def one(s, carry):
        owner = sc[1 + s]
        wet = wet_of(depth_ref[0, s], (cols, levels))
        warm = jnp.exp(heating_speed * t1_ref[s])
        up = half_rise(r1_ref[s])
        y = [y_ref[owner, i] for i in range(len(KEPT))]
        g = uptake_rate * irr_ref[s] * saturation(y[3])
        for ref, i, k in ((a_ref, 0, 0), (b_ref, 1, 1), (n_ref, 3, 4)):
            change = warm * y[i + 1] + share_ref[k] * g + transport(up, y[i])
            ref[s] = wet * (y[i] + step_tracer * change)
        chl_ref[s] = softplus(a_ref[s])
        return carry

    lax.fori_loop(0, patches, one, 0, unroll=4)
    chl = chl_ref[...].reshape(flat)
    absorbed, irradiance = light(chl, level_sums(chl, level_matrix(levels, "prefix")), level_of(flat))
    wet = wet_of(depth_ref[0], whole)
    heat_ref[...] = advance_marine * heat_gain * (wet * (absorbed[0] + absorbed[1]).reshape(whole))
    g_ref[...] = uptake_rate * irradiance.reshape(whole) * saturation(n_ref[...])


def third_kernel(sc, a_ref, b_ref, g_ref, t2_ref, r2_ref, depth_ref, share_ref, band_ref, chl_ref):
    patches, cols, levels = a_ref.shape
    flat = (patches * cols, levels)
    whole = (patches, cols, levels)

    def one(s, carry):
        wet = wet_of(depth_ref[0, s], (cols, levels))
        warm = jnp.exp(heating_speed * t2_ref[s])
        a = a_ref[s]
        change = warm * b_ref[s] + share_ref[0] * g_ref[s] + transport(half_rise(r2_ref[s]), a)
        chl_ref[s] = softplus(wet * (a + step_tracer * change))
        return carry

    lax.fori_loop(0, patches, one, 0, unroll=4)
    chl = chl_ref[...].reshape(flat)
    absorbed, _ = light(chl, level_sums(chl, level_matrix(levels, "prefix")), level_of(flat))
    wet = wet_of(depth_ref[0], whole)
    for band in range(2):
        band_ref[:, band] = wet * absorbed[band].reshape(whole)


def last_ocean_kernel(
    sc, speed_ref, t_ref, north_ref, south_ref, east_ref, west_ref, depth_ref, heat_ref, out_ref, div_ref
):
    rows, cols, levels = t_ref.shape
    place = lax.broadcasted_iota(jnp.int32, (cols, levels), 0)
    sources = (speed_ref.at[0], speed_ref.at[1], t_ref)
    for y in range(rows):
        wet = [wet_of(depth_ref[i, y], (cols, levels)) for i in range(5)]

        def east_of(f):
            return jnp.where(place == cols - 1, east_ref[f, pl.ds(y, 1)], pltpu.roll(sources[f][y], cols - 1, 0))

        def west_of(f):
            return jnp.where(place == 0, west_ref[f, pl.ds(y, 1)], pltpu.roll(sources[f][y], 1, 0))

        def north_of(f):
            return sources[f][y + 1] if y < rows - 1 else north_ref[f]

        def south_of(f):
            return sources[f][y - 1] if y > 0 else south_ref[f]

        u, v, t = (ref[y] for ref in sources)
        own = 0.5 * wet[0]
        east = (u + east_of(0)) * (own * wet[1])
        west = (west_of(0) + u) * (own * wet[2])
        north = (v + north_of(1)) * (own * wet[3])
        south = (south_of(1) + v) * (own * wet[4])
        div_ref[y] = east - west + north - south
        e, w, n, s = east_of(2), west_of(2), north_of(2), south_of(2)
        spread = wet[1] * (e - t) + wet[2] * (w - t) + wet[3] * (n - t) + wet[4] * (s - t)
        carry_along = 0.5 * (east * (t + e) - west * (w + t) + north * (t + n) - south * (s + t))
        change = spreading * spread - carry_along
        out_ref[1, sc[1 + y], 1] = wet[0] * (t + advance_marine * change) + heat_ref[y]
    sums = level_sums(div_ref[...].reshape(rows * cols, levels), level_matrix(levels, "below"))
    div_ref[...] = -sums.reshape(rows, cols, levels)
    for y in range(rows):
        out_ref[1, sc[1 + y], 0] = div_ref[y]
    out_ref[0] = jnp.zeros(out_ref.shape[1:], jnp.float32)


def join_kernel(sc, absorbed_ref, flux_ref, other_ref, out_ref):
    patches, _, half, levels = absorbed_ref.shape

    @pl.when(sc[0] == 0)
    def _():
        for s in range(patches):
            for f in range(2):
                out_ref[f, s, :half] = absorbed_ref[s, f]
                out_ref[f, s, half:] = other_ref[s, f]

    @pl.when(sc[0] != 0)
    def _():
        for s in range(patches):
            for f in range(2):
                for part in range(2):
                    out_ref[f, s, part * half : (part + 1) * half] = flux_ref[part, s, f]


def call(kernel, comp, args, specs, outs, scratch=(), name=None, sems=()):
    return pl.pallas_call(
        kernel,
        grid_spec=pltpu.PrefetchScalarGridSpec(
            num_scalar_prefetch=1,
            grid=(1,),
            in_specs=[spec or whole(a) for spec, a in zip(specs, args)],
            out_specs=[whole(o) for o in outs],
            scratch_shapes=[pltpu.VMEM(s, jnp.float32) for s in scratch] + list(sems),
        ),
        out_shape=outs,
        compiler_params=PARAMS,
        name=name,
    )(comp, *args)


def exchange_rows(low, high):
    count = lax.axis_size("py")
    north = lax.ppermute(low, "py", [((i + 1) % count, i) for i in range(count)])
    south = lax.ppermute(high, "py", [(i, (i + 1) % count) for i in range(count)])
    return north, south


def exchange_cols(low, high):
    count = lax.axis_size("px")
    east = lax.ppermute(low, "px", [((i + 1) % count, i) for i in range(count)])
    west = lax.ppermute(high, "px", [(i, (i + 1) % count) for i in range(count)])
    return east, west


def exchange_half_cols(low, high):
    count = lax.axis_size("px")
    line = [(h % 2) * count + h // 2 for h in range(2 * count)]
    ahead = [(line[h], line[(h + 1) % len(line)]) for h in range(len(line))]
    east = lax.ppermute(low, ("comp", "px"), [(b, a) for a, b in ahead])
    west = lax.ppermute(high, ("comp", "px"), ahead)
    return east, west


def in_hbm(x):
    return pltpu.with_memory_space_constraint(x, pltpu.HBM)


def in_vmem(x):
    return pltpu.with_memory_space_constraint(x, pltpu.VMEM)


def to_owners(blocks):
    return lax.all_to_all(blocks, ("py", "px"), split_axis=0, concat_axis=0, tiled=True)


def swap(block):
    return lax.ppermute(block, "comp", [(0, 1), (1, 0)])


def pick(blocks, order, axis):
    return jnp.stack(
        [lax.dynamic_index_in_dim(blocks, order[k], axis, keepdims=False) for k in range(order.shape[0])], axis
    )


def table(levels, pattern):
    return level_matrix(levels, pattern).astype(jnp.float32)


def product(values, matrix):
    return jnp.einsum("...j,jk->...k", values, matrix, precision=lax.Precision.HIGHEST)


def general_light(conc, wet, loading):
    chl = jax.nn.softplus(jnp.einsum("f...,f->...", conc, loading, precision=lax.Precision.HIGHEST))
    levels = chl.shape[-1]
    absorbed, irradiance = light(chl, product(chl, table(levels, "prefix")), level_of(chl.shape))
    return wet * jnp.stack(absorbed), irradiance


def general_tracers(conc, rise, heat, irradiance, wet, matrix, share):
    none = jnp.zeros_like(conc[..., :1])
    top = jnp.concatenate([none, 0.5 * (conc[..., 1:] + conc[..., :-1]) * rise[..., 1:]], axis=-1)
    below = jnp.concatenate([top[..., 1:], none], axis=-1)
    mixed = jnp.einsum("ij,j...->i...", matrix, conc, precision=lax.Precision.HIGHEST)
    growth = uptake_rate * irradiance * saturation(conc[0])
    change = (
        jnp.exp(heating_speed * heat) * mixed
        + share.reshape((-1,) + (1,) * (conc.ndim - 1)) * growth + below - top
    )
    return wet * (conc + step_tracer * change)


def general_ocean(u, v, t, absorb, depth, coriolis):
    levels = t.shape[-1]
    fields = jnp.stack([u, v, t])
    north, south = exchange_rows(fields[:, 0], fields[:, -1])
    east, west = exchange_cols(fields[:, :, 0], fields[:, :, -1])
    tall = jnp.concatenate([south[:, None], fields, north[:, None]], axis=1)
    wide = jnp.concatenate([west[:, :, None], fields, east[:, :, None]], axis=2)
    around = (fields, wide[:, :, 2:], wide[:, :, :-2], tall[:, 2:], tall[:, :-2])
    above = table(levels, "above")
    u, v, t = ([x[f] for x in around] for f in range(3))
    p = [weight_pull_factor * product(x, above) for x in t]
    wet = [wet_of(depth[i], t[0].shape) for i in range(5)]

    def spread(x):
        return sum(wet[i] * (x[i] - x[0]) for i in range(1, 5))

    east = 0.5 * (u[0] + u[1]) * wet[0] * wet[1]
    west = 0.5 * (u[2] + u[0]) * wet[2] * wet[0]
    north = 0.5 * (v[0] + v[3]) * wet[0] * wet[3]
    south = 0.5 * (v[4] + v[0]) * wet[4] * wet[0]
    carry_along = 0.5 * (
        east * (t[0] + t[1]) - west * (t[2] + t[0]) + north * (t[0] + t[3]) - south * (t[4] + t[0])
    )
    zonal = 0.5 * (wet[1] * (p[1] - p[0]) + wet[2] * (p[0] - p[2]))
    merid = 0.5 * (wet[3] * (p[3] - p[0]) + wet[4] * (p[0] - p[4]))
    turn = coriolis[:, None, None]
    rise = -product(east - west + north - south, table(levels, "below"))
    return (
        wet[0] * (u[0] + advance_marine * (turn * v[0] - zonal + viscosity * spread(u) - damping * u[0])),
        wet[0] * (v[0] + advance_marine * (-turn * u[0] - merid + viscosity * spread(v) - damping * v[0])),
        wet[0] * (t[0] + advance_marine * (spreading * spread(t) - carry_along + heat_gain * (absorb[0] + absorb[1]))),
        rise,
    )


def general(linked, u, v, t, tracers, depth, tracer_depth, holder_rank, patch_index, coriolis, matrix, share, loading):
    comp_index = lax.axis_index("comp")
    first = comp_index == 0
    fields, patches, strip, levels = tracers.shape
    half = strip // 2
    indices = jnp.arange(patches, dtype=jnp.int32)
    owner_row = lax.dynamic_index_in_dim(holder_rank, patch_index, 0, keepdims=False)
    inverse_row = jnp.sum(jnp.where(owner_row[:, None] == indices[None], indices[:, None], 0), axis=0)

    def own_half(x):
        return lax.dynamic_slice_in_dim(x, comp_index * half, half, x.ndim - 2)

    partner = swap(linked)
    absorb = jnp.where(first, linked, partner)
    flux = own_half(jnp.where(first, partner, linked))
    conc = own_half(tracers)
    wet = wet_of(tracer_depth, conc.shape[1:])
    irradiance = general_light(conc, wet, loading)[1]
    grid = t.shape
    for _ in range(3):
        u, v, t, rise = general_ocean(u, v, t, absorb.reshape((2,) + grid), depth, coriolis)
        conc = general_tracers(conc, flux[0], flux[1], irradiance, wet, matrix, share)
        absorbed, irradiance = general_light(conc, wet, loading)
        both = own_half(pick(jnp.stack([rise, t]).reshape(2, patches, strip, levels), inverse_row, 1))
        send = jnp.concatenate([both, absorbed])
        back = lax.all_to_all(send, ("py", "px"), split_axis=1, concat_axis=1, tiled=True)
        flux = back[:2]
        mine = pick(back[2:], owner_row, 1)
        other = swap(mine)
        absorb = jnp.where(first, jnp.concatenate([mine, other], 2), jnp.concatenate([other, mine], 2))
    other = swap(flux)
    joined = jnp.where(first, jnp.concatenate([flux, other], 2), jnp.concatenate([other, flux], 2))
    return jnp.where(first, absorb, joined)


def shards(
    current_speeds,
    thermal_anomaly,
    solute_amounts,
    delayed_link_source,
    marine_indicator,
    floor_layer_index,
    holder_rank,
    biota_exchange_matrix,
    photic_absorb_share,
    chroma_loading,
):
    comp_index = lax.axis_index("comp")
    row_index = lax.axis_index("py")
    col_index = lax.axis_index("px")
    rows_mesh = lax.axis_size("py")
    cols_mesh = lax.axis_size("px")
    patches = rows_mesh * cols_mesh
    fields, _, columns, levels = solute_amounts.shape
    strip = columns // patches
    half = strip // 2
    patch_index = row_index * cols_mesh + col_index
    first = comp_index == 0

    linked = delayed_link_source.reshape(2, patches, strip, levels)
    tracers = solute_amounts.reshape(fields, patches, strip, levels)
    u0, v0 = current_speeds[0], current_speeds[1]

    column_depth = marine_indicator * floor_layer_index
    wrapped = jnp.concatenate([column_depth[:, -2:], column_depth, column_depth[:, :2]], axis=1)
    padded = jnp.pad(wrapped, ((2, 2), (0, 0)))
    far = lax.dynamic_slice(padded, (row_index * CY, col_index * CX), (CY + 4, CX + 4))
    local = far[1:-1, 1:-1]
    gap = 4
    wide_depth = jnp.concatenate(
        [far[:, 2:], jnp.zeros((CY + 4, gap), jnp.int32), far[:, :2]], axis=1
    )[..., None]
    depth = jnp.stack([local[1:-1, 1:-1], local[1:-1, 2:], local[1:-1, :-2], local[2:, 1:-1], local[:-2, 1:-1]])
    depth = depth[..., None]
    by_strip = (
        column_depth.reshape(rows_mesh, CY, cols_mesh, CX).transpose(0, 2, 1, 3).reshape(patches, patches, strip)
    )
    here = (holder_rank == patch_index)[:, :, None]
    tracer_depth = jnp.sum(jnp.where(here, by_strip, 0), axis=1)
    tracer_depth = lax.dynamic_slice_in_dim(tracer_depth, comp_index * half, half, 1)[..., None]
    owner_row = lax.dynamic_index_in_dim(holder_rank, patch_index, 0, keepdims=False)
    side_index = comp_index.astype(jnp.int32)[None]
    comp = jnp.concatenate([side_index, owner_row])
    ys = (row_index * CY - 1 + jnp.arange(CY + 2, dtype=jnp.int32)).astype(jnp.float32)
    coriolis = coriolis_scale * (2.0 * (ys + 0.5) / (CY * rows_mesh) - 1.0)

    if half % 8 or strip != CX:
        out = general(
            linked, u0, v0, thermal_anomaly, tracers, depth, tracer_depth, holder_rank, patch_index, coriolis[1:-1],
            biota_exchange_matrix, photic_absorb_share, chroma_loading,
        )
        return out.reshape(1, 2, 1, columns, levels)

    linked, tracers, current_speeds, thermal_anomaly = (
        in_hbm(x) for x in (linked, tracers, current_speeds, thermal_anomaly)
    )
    sent, *edges = pack(side_index, linked, current_speeds, thermal_anomaly)
    got = swap(sent)
    times = functools.partial(jnp.dot, precision=lax.Precision.HIGHEST)
    unit = (jnp.arange(fields) == 0).astype(jnp.float32)
    chain = [jnp.stack([chroma_loading, unit])]
    for _ in range(3):
        chain.append(times(chain[-1], biota_exchange_matrix))
    weights = jnp.stack([c[0] for c in chain] + [c[1] for c in chain[:3]])
    shares = times(weights, photic_absorb_share)

    projected, g = project(side_index, tracers, weights)
    low, high, left, right = edges
    north, south = exchange_rows(low, high)
    left, right, projected, g = lax.optimization_barrier((left, right, projected, g))
    projected, g = in_vmem(projected), in_vmem(g)

    outer = shape_of(4, 2, CY + 2, levels)
    left, right = call(corner_kernel, side_index, (left, right, north, south), [None] * 4, (outer, outer), (), "corner")
    east, west = exchange_cols(left, right)
    kept = first_tracer(side_index, projected, g, got, linked, tracer_depth, shares)
    kept, north, south, east, west = lax.optimization_barrier((kept, north, south, east, west))
    arrived = to_owners(kept)

    rim = shape_of(ring_places(CY, CX)[2], levels)
    [own_ring] = call(ring_kernel, side_index, (north, south, east, west), [None] * 4, (rim,), (), "ring")
    other_ring = swap(own_ring)
    args = (current_speeds, thermal_anomaly, linked, got, north, south, east, west, own_ring, other_ring)
    speeds1, wide_t1, t1, r1 = ocean(1, comp, coriolis, args, wide_depth, CY, CX)
    r1 = in_hbm(r1)
    speeds2, t2, r2 = ocean(2, comp, coriolis, (speeds1, wide_t1), wide_depth, CY, CX)
    arrived, speeds2, t2 = lax.optimization_barrier((arrived, speeds2, t2))
    speeds2, t2, r2 = in_hbm(speeds2), in_hbm(t2), in_hbm(r2)

    patch_half = half_spec((CY,), half, levels)
    speeds_half = half_spec((2, CY), half, levels)
    depth_half = pl.BlockSpec((5, CY, half, 1), lambda i, c: (0, 0, c[0], 0))
    piece = shape_of(CY, half, levels)
    scratch = (CY, half, levels)
    line = shape_of(3, half, levels)
    side = shape_of(3, CY, levels)

    t2, irr1, *edges = call(
        absorb_kernel, comp, (arrived, t2, speeds2, depth), [HBM, patch_half, speeds_half, depth_half],
        (piece, piece, line, line, side, side), [scratch] * 2, "absorb", [pltpu.SemaphoreType.DMA],
    )
    halos2 = exchange_rows(edges[0], edges[1]) + exchange_half_cols(edges[2], edges[3])
    heat, a, b, g = call(
        second_kernel, comp, (arrived, irr1, t1, r1, depth, shares),
        [None, None, patch_half, patch_half, depth_half, SMEM],
        (piece,) * 4, [scratch] * 2, "second",
    )
    [back] = call(
        last_ocean_kernel, comp, (speeds2, t2, *halos2, depth, heat),
        [speeds_half] + [None] * 5 + [depth_half, None],
        (shape_of(2, patches, 2, half, levels),), [scratch], "last_ocean",
    )
    flux = lax.all_to_all(
        back.reshape(2 * patches, 2, half, levels), ("comp", "py", "px"), split_axis=0, concat_axis=0, tiled=True
    ).reshape(2, patches, 2, half, levels)
    [absorbed] = call(
        third_kernel, comp, (a, b, g, t2, r2, depth, shares),
        [None] * 4 + [patch_half, depth_half, SMEM], (shape_of(CY, 2, half, levels),), [scratch], "third",
    )
    other = swap(absorbed)
    [out] = call(
        join_kernel, comp, (absorbed, flux, other), [None] * 3, (shape_of(2, patches, strip, levels),), (), "join"
    )
    return out.reshape(1, 2, 1, columns, levels)


def solution(mesh):
    placed = (
        P(None, "py", "px", None),
        P("py", "px", None),
        P(None, ("py", "px"), None, None),
        P("comp", None, ("py", "px"), None, None),
        P(),
        P(),
        P(),
        P(),
        P(),
        P(),
    )
    return jax.shard_map(
        shards,
        mesh=mesh,
        in_specs=placed,
        out_specs=P("comp", None, ("py", "px"), None, None),
        check_vma=False,
    )
```

```python
import functools

import jax
import jax.numpy as jnp
from jax import lax
from jax.experimental import pallas as pl
from jax.experimental.pallas import tpu as pltpu
from jax.sharding import PartitionSpec as P

advance_marine = 0.1
spreading = 0.1
viscosity = 0.1
damping = 0.05
heat_gain = 0.2
weight_pull_factor = 0.05
coriolis_scale = 1.0
step_tracer = 0.1
heating_speed = 0.06
uptake_rate = 0.01
water_absorb = (0.02, 0.003)
pigment_absorb = (0.03, 0.004)
surface_light = (40.0, 60.0)
CY = 16
CX = 32
KEPT = (0, 1, 2, 4, 5)
SMEM = pl.BlockSpec(memory_space=pltpu.SMEM)
PARAMS = pltpu.CompilerParams(vmem_limit_bytes=28 * 1024 * 1024)
HBM = pl.BlockSpec(memory_space=pltpu.HBM)
STREAMED = pltpu.CompilerParams(vmem_limit_bytes=60 * 1024 * 1024)


def whole(array):
    zeros = (0,) * len(array.shape)
    return pl.BlockSpec(array.shape, lambda i, c: zeros)


def shape_of(*dims):
    return jax.ShapeDtypeStruct(dims, jnp.float32)


def level_matrix(levels, pattern):
    row = lax.broadcasted_iota(jnp.int32, (levels, levels), 0)
    col = lax.broadcasted_iota(jnp.int32, (levels, levels), 1)
    if pattern == "above":
        m = jnp.where(row < col, 1.0, jnp.where(row == col, 0.5, 0.0))
    elif pattern == "below":
        m = jnp.where(row >= col, 1.0, 0.0)
    else:
        m = jnp.where(row < col, 1.0, 0.0)
    return m.astype(jnp.bfloat16)


def level_sums(x, matrix):
    hi = x.astype(jnp.bfloat16)
    rest = x - hi.astype(jnp.float32)
    mid = rest.astype(jnp.bfloat16)
    low = (rest - mid.astype(jnp.float32)).astype(jnp.bfloat16)
    dot = functools.partial(jnp.dot, preferred_element_type=jnp.float32)
    return dot(hi, matrix) + dot(mid, matrix) + dot(low, matrix)


def softplus(x):
    return jnp.maximum(x, 0.0) + jnp.log1p(jnp.exp(-jnp.abs(x)))


def light(chl, sums, level):
    absorbed, irradiance = [], None
    for water, pigment, surface in zip(water_absorb, pigment_absorb, surface_light):
        fade = jnp.exp(-0.5 * (water + pigment * chl))
        intensity = surface * jnp.exp(-(water * level + pigment * sums))
        absorbed.append(intensity * (1.0 - fade * fade))
        part = intensity * fade
        irradiance = part if irradiance is None else irradiance + part
    return absorbed, irradiance


def saturation(n):
    return n * n / (1.0 + n * n)


def transport(rise_half, y):
    top = rise_half * (y + pltpu.roll(y, 1, 1))
    return pltpu.roll(top, top.shape[1] - 1, 1) - top


def wet_of(depth, shape):
    level = lax.broadcasted_iota(jnp.int32, shape, len(shape) - 1)
    return jnp.where(level < depth, 1.0, 0.0)


def level_of(shape):
    return lax.broadcasted_iota(jnp.int32, shape, len(shape) - 1).astype(jnp.float32)


def half_rise(rise):
    k = lax.broadcasted_iota(jnp.int32, rise.shape, 1)
    return jnp.where(k > 0, 0.5 * rise, 0.0)


def project_kernel(sc, x_hbm, w_ref, y_ref, g_ref, x_ref, chl_ref, sems):
    pieces, fields, block, cols, levels = x_ref.shape
    own = pl.ds(pl.multiple_of(sc[0] * cols, cols), cols)
    copies = [
        pltpu.make_async_copy(x_hbm.at[:, pl.ds(i * block, block), own], x_ref.at[i], sems.at[i]) for i in range(pieces)
    ]
    for copy in copies:
        copy.start()
    mixed = [k for k in range(y_ref.shape[0]) if k != 4]
    prefix = level_matrix(levels, "prefix")
    flat = (block * cols, levels)
    for i, copy in enumerate(copies):
        copy.wait()

        def one(q, carry):
            at = i * block + q
            value = x_ref[i, 0, q]
            y_ref[4, at] = value
            totals = [w_ref[k, 0] * value for k in mixed]
            for j in range(1, fields):
                value = x_ref[i, j, q]
                totals = [t + w_ref[k, j] * value for t, k in zip(totals, mixed)]
            for k, total in zip(mixed, totals):
                y_ref[k, at] = total
            chl_ref[q] = softplus(totals[0])
            return carry

        lax.fori_loop(0, block, one, 0)
        chl = chl_ref[...].reshape(flat)
        _, irradiance = light(chl, level_sums(chl, prefix), level_of(flat))
        n = x_ref[i, 0].reshape(flat)
        g_ref[i * block : (i + 1) * block] = (uptake_rate * irradiance * saturation(n)).reshape(block, cols, levels)


def project(comp, tracers, weights):
    fields, patches, strip, levels = tracers.shape
    half = strip // 2
    pieces = 4
    block = patches // pieces
    outs = (shape_of(weights.shape[0], patches, half, levels), shape_of(patches, half, levels))
    return pl.pallas_call(
        project_kernel,
        grid_spec=pltpu.PrefetchScalarGridSpec(
            num_scalar_prefetch=1,
            grid=(1,),
            in_specs=[HBM, SMEM],
            out_specs=[whole(o) for o in outs],
            scratch_shapes=[
                pltpu.VMEM((pieces, fields, block, half, levels), jnp.float32),
                pltpu.VMEM((block, half, levels), jnp.float32),
                pltpu.SemaphoreType.DMA((pieces,)),
            ],
        ),
        out_shape=outs,
        compiler_params=PARAMS,
        name="project",
    )(comp, tracers, weights)


def first_tracer_kernel(sc, y_ref, g_ref, got_ref, own_ref, depth_ref, share_ref, out_ref):
    patches, cols, levels = g_ref.shape
    first = sc[0] == 0

    def one(q, carry):
        rise = jnp.where(first, got_ref[0, q], own_ref[0, q])
        heat = jnp.where(first, got_ref[1, q], own_ref[1, q])
        warm = jnp.exp(heating_speed * heat)
        wet = wet_of(depth_ref[q], (cols, levels))
        up = half_rise(rise)
        g = g_ref[q]
        for place, k in enumerate(KEPT):
            y = y_ref[k, q]
            change = warm * y_ref[k + 1, q] + share_ref[k] * g + transport(up, y)
            out_ref[q, place] = wet * (y + step_tracer * change)
        return carry

    lax.fori_loop(0, patches, one, 0, unroll=2)


def half_spec(lead, cols, levels):
    zeros = (0,) * len(lead)
    return pl.BlockSpec(lead + (cols, levels), lambda i, c: zeros + (c[0], 0))


def first_tracer(comp, projected, g, got, linked, depth, shares):
    kinds, patches, half, levels = projected.shape
    block = 4
    return pl.pallas_call(
        first_tracer_kernel,
        grid_spec=pltpu.PrefetchScalarGridSpec(
            num_scalar_prefetch=1,
            grid=(patches // block,),
            in_specs=[
                pl.BlockSpec((kinds, block, half, levels), lambda i, c: (0, i, 0, 0)),
                pl.BlockSpec((block, half, levels), lambda i, c: (i, 0, 0)),
                pl.BlockSpec((2, block, half, levels), lambda i, c: (0, i, 0, 0)),
                pl.BlockSpec((2, block, half, levels), lambda i, c: (0, i, c[0], 0)),
                pl.BlockSpec((block, half, 1), lambda i, c: (i, 0, 0)),
                SMEM,
            ],
            out_specs=pl.BlockSpec((block, len(KEPT), half, levels), lambda i, c: (i, 0, 0, 0)),
        ),
        out_shape=shape_of(patches, len(KEPT), half, levels),
        compiler_params=PARAMS,
        name="first_tracer",
    )(comp, projected, g, got, linked, depth, shares)


def pack_kernel(sc, linked_ref, row0_ref, row1_ref, col0_ref, col1_ref, t0_ref, t1_ref, tc0_ref, tc1_ref,
                sent_ref, low_ref, high_ref, left_ref, right_ref, first_ref):
    _, strips, strip, levels = linked_ref.shape
    half = strip // 2

    @pl.when(sc[0] == 0)
    def _():
        for part in range(2):
            cols = slice(part * half, (part + 1) * half)
            sent_ref[part] = linked_ref[0, :, cols] + linked_ref[1, :, cols]

    @pl.when(sc[0] != 0)
    def _():
        sent_ref[...] = linked_ref[:, :, :half]

    last = col1_ref.shape[2]
    tall = strips - 2
    for i in range(2):
        for f in range(2):
            left_ref[f, i] = col0_ref[f, :, i]
            right_ref[f, i] = col1_ref[f, :, last - 2 + i]
        left_ref[2, i] = tc0_ref[:, i]
        right_ref[2, i] = tc1_ref[:, last - 2 + i]
        left_ref[3, i] = linked_ref[0, :, i] + linked_ref[1, :, i]
        right_ref[3, i] = linked_ref[0, :, strip - 2 + i] + linked_ref[1, :, strip - 2 + i]
    first_ref[...] = left_ref[3, 0]
    for f in range(2):
        low_ref[f] = row0_ref[f]
        high_ref[f] = row1_ref[f]
    low_ref[2] = t0_ref[...]
    high_ref[2] = t1_ref[...]
    low_ref[3] = linked_ref[0, :2] + linked_ref[1, :2]
    high_ref[3] = linked_ref[0, tall:] + linked_ref[1, tall:]


def corner_kernel(sc, left_ref, right_ref, north_ref, south_ref, out_ref):
    rows = left_ref.shape[2]
    cols = north_ref.shape[2]

    def fill(source, at):
        for f in range(source.shape[0]):
            for i in range(2):
                out_ref[f, i, :rows] = source[f, i]
                out_ref[f, i, rows : rows + 1] = south_ref[f, 1, at + i : at + i + 1]
                out_ref[f, i, rows + 1 :] = north_ref[f, 0, at + i : at + i + 1]

    @pl.when(sc[0] == 0)
    def _():
        fill(right_ref, cols - 2)

    @pl.when(sc[0] != 0)
    def _():
        fill(left_ref, 0)


def ring_kernel(sc, north_ref, south_ref, ring_ref):
    ring_ref[0] = south_ref[3, 1]
    ring_ref[1] = north_ref[3, 0]


def pack(comp, linked, speeds, heat):
    _, strips, strip, levels = linked.shape
    rows, cols, _ = heat.shape
    outs = (
        shape_of(2, strips, strip // 2, levels), shape_of(4, 2, cols, levels), shape_of(4, 2, cols, levels),
        shape_of(4, 2, rows, levels), shape_of(4, 2, rows, levels), shape_of(rows, levels),
    )
    edge = min(8, cols)
    return pl.pallas_call(
        pack_kernel,
        grid_spec=pltpu.PrefetchScalarGridSpec(
            num_scalar_prefetch=1,
            grid=(1,),
            in_specs=[
                whole(linked),
                pl.BlockSpec((2, 2, cols, levels), lambda i, c: (0, 0, 0, 0)),
                pl.BlockSpec((2, 2, cols, levels), lambda i, c: (0, rows // 2 - 1, 0, 0)),
                pl.BlockSpec((2, rows, edge, levels), lambda i, c: (0, 0, 0, 0)),
                pl.BlockSpec((2, rows, edge, levels), lambda i, c: (0, 0, cols // edge - 1, 0)),
                pl.BlockSpec((2, cols, levels), lambda i, c: (0, 0, 0)),
                pl.BlockSpec((2, cols, levels), lambda i, c: (rows // 2 - 1, 0, 0)),
                pl.BlockSpec((rows, edge, levels), lambda i, c: (0, 0, 0)),
                pl.BlockSpec((rows, edge, levels), lambda i, c: (0, cols // edge - 1, 0)),
            ],
            out_specs=[whole(o) for o in outs],
        ),
        out_shape=outs,
        compiler_params=STREAMED,
        name="pack",
    )(comp, linked, speeds, speeds, speeds, speeds, heat, heat, heat, heat)


def wide_rows(sc, speed_hbm, heat_hbm, linked_hbm, got_ref, north_ref, south_ref, side_ref, edge_ref, ring_ref,
              x_ref, near_ref, absorb_ref, linked_ref, sems):
    rows, cols, levels = heat_hbm.shape
    half = cols // 2
    comp = sc[0]
    first = comp == 0
    width = x_ref.shape[2]
    rim = width - half
    own = pl.ds(pl.multiple_of(comp * half, half), half)
    near = pl.ds(pl.multiple_of(half - rim * comp, 8), rim)
    copies = [pltpu.make_async_copy(linked_hbm, linked_ref, sems.at[0])]
    for f, source in enumerate((speed_hbm.at[0], speed_hbm.at[1], heat_hbm)):
        copies.append(
            pltpu.make_async_copy(source.at[:, own], x_ref.at[f, pl.ds(2, rows), pl.ds(0, half)], sems.at[1 + f])
        )
        copies.append(pltpu.make_async_copy(source.at[:, near], near_ref.at[f], sems.at[4 + f]))
    for copy in copies:
        copy.start()
    place = lax.broadcasted_iota(jnp.int32, (rim, levels), 0)
    none = jnp.zeros((rim, levels), jnp.float32)
    far_place = (1 - comp) * (rim - 2)
    for copy in copies:
        copy.wait()
    for f in range(3):
        x_ref[f, :2, :half] = south_ref[f, :, own]
        x_ref[f, rows + 2 :, :half] = north_ref[f, :, own]
        x_ref[f, 0, half:] = none
        x_ref[f, rows + 3, half:] = none
        for o in range(rows + 2):
            if o == 0:
                r, cells = rows, south_ref[f, 1, near]
            elif o == rows + 1:
                r, cells = rows + 1, north_ref[f, 0, near]
            else:
                r, cells = o - 1, near_ref[f, o - 1]
            for i in range(2):
                cells = jnp.where(place == far_place + i, side_ref[f, i, r : r + 1], cells)
            x_ref[f, o + 1, half:] = cells
    for o, side in ((0, 0), (rows + 1, 1)):
        here = (south_ref[3, 1] if side == 0 else north_ref[3, 0])[:half]
        absorb_ref[o, :half] = jnp.where(first, here, ring_ref[side, half:])
        absorb_ref[o, half:] = none
    for y in range(rows):
        both = linked_ref[0, y] + linked_ref[1, y]
        absorb_ref[y + 1, :half] = jnp.where(first, both[:half], got_ref[1, y])
        cells = jnp.where(first, both[half : half + rim], got_ref[0, y, half - rim :])
        far = jnp.where(first, side_ref[3, 1, y : y + 1], edge_ref[y : y + 1])
        absorb_ref[y + 1, half:] = jnp.where(place == (1 - comp) * (rim - 1), far, cells)


def ocean_kernel(advance, sc, coriolis_ref, *refs):
    if advance == 1:
        *sources, depth_ref, next_ref, tn_ref, inner_ref, rise_ref, x_ref, near_ref, absorb_ref = refs[:-4]
        linked_ref, sems, p_ref, div_ref = refs[-4:]
        wide_rows(sc, *sources, x_ref, near_ref, absorb_ref, linked_ref, sems)
        fields = [x_ref.at[f] for f in range(3)]
    else:
        speed_ref, t_ref, depth_ref, next_ref, tn_ref, rise_ref, p_ref, div_ref = refs
        fields = [speed_ref.at[0], speed_ref.at[1], t_ref]
    tall, width, levels = p_ref.shape
    rows, cols = rise_ref.shape[:2]
    out_width = tn_ref.shape[1]
    p_ref[...] = (
        weight_pull_factor * level_sums(fields[2][...].reshape(tall * width, levels), level_matrix(levels, "above"))
    ).reshape(tall, width, levels)
    lanes = min(128, levels)

    def piece(o, lane):
        part = slice(lane, lane + lanes)
        level = lane + lax.broadcasted_iota(jnp.int32, (width, lanes), 1)

        def beside(x):
            return pltpu.roll(x, width - 1, 0), pltpu.roll(x, 1, 0)

        def field(ref):
            x = ref[o + 1, :, part]
            return (x, *beside(x), ref[o + 2, :, part], ref[o, :, part])

        def wet_at(d):
            return jnp.where(level < depth_ref[d], 1.0, 0.0)

        here = wet_at(o + advance)
        wet = (here, *beside(here), wet_at(o + advance + 1), wet_at(o + advance - 1))
        u, v, t, p = (field(ref) for ref in (*fields, p_ref))
        own = 0.5 * wet[0]
        east = (u[0] + u[1]) * (own * wet[1])
        west = (u[2] + u[0]) * (own * wet[2])
        north = (v[0] + v[3]) * (own * wet[3])
        south = (v[4] + v[0]) * (own * wet[4])
        div_ref[o, :, part] = east - west + north - south
        wets = wet[1] + wet[2] + wet[3] + wet[4]

        def spread(x):
            return wet[1] * x[1] + wet[2] * x[2] + wet[3] * x[3] + wet[4] * x[4] - wets * x[0]

        carry_along = 0.5 * (
            east * (t[0] + t[1]) - west * (t[2] + t[0]) + north * (t[0] + t[3]) - south * (t[4] + t[0])
        )
        change = spreading * spread(t) - carry_along
        if advance == 1:
            change = change + heat_gain * absorb_ref[o, :, part]
        zonal = 0.5 * (wet[1] * (p[1] - p[0]) + wet[2] * (p[0] - p[2]))
        merid = 0.5 * (wet[3] * (p[3] - p[0]) + wet[4] * (p[0] - p[4]))
        turn = coriolis_ref[o + advance - 1]
        results = (
            wet[0] * (u[0] + advance_marine * (turn * v[0] - zonal + viscosity * spread(u) - damping * u[0])),
            wet[0] * (v[0] + advance_marine * (-turn * u[0] - merid + viscosity * spread(v) - damping * v[0])),
            wet[0] * (t[0] + advance_marine * change),
        )
        for ref, value in zip((next_ref.at[0], next_ref.at[1], tn_ref), results):
            ref[o, :, part] = value[:out_width]

    def row(o, carry):
        for lane in range(0, levels, lanes):
            piece(o, lane)
        return carry

    lax.fori_loop(0, tall - 2, row, 0)
    rim = (tall - 2 - rows) // 2
    div = div_ref[rim : rim + rows, :cols].reshape(rows * cols, levels)
    rise_ref[...] = -level_sums(div, level_matrix(levels, "below")).reshape(rows, cols, levels)
    if advance == 1:
        inner_ref[...] = tn_ref[rim : rim + rows, :cols]


def ocean(advance, comp, coriolis, args, depth, rows, cols):
    width, levels = depth.shape[1], args[1].shape[-1]
    patch = shape_of(rows, cols, levels)
    if advance == 1:
        tall = rows + 4
        outs = (shape_of(2, rows + 2, width, levels), shape_of(rows + 2, width, levels), patch, patch)
        scratch = [
            pltpu.VMEM((3, tall, width, levels), jnp.float32),
            pltpu.VMEM((3, rows, width - cols, levels), jnp.float32),
            pltpu.VMEM((rows + 2, width, levels), jnp.float32),
            pltpu.VMEM(args[2].shape, jnp.float32),
            pltpu.SemaphoreType.DMA((7,)),
        ]
    else:
        tall = rows + 2
        outs = (shape_of(2, rows, cols, levels), patch, patch)
        scratch = []
    scratch += [
        pltpu.VMEM((tall, width, levels), jnp.float32), pltpu.VMEM((tall - 2, width, levels), jnp.float32)
    ]
    args = [coriolis, *args, depth]
    own_copies = 3 if advance == 1 else 0
    return pl.pallas_call(
        functools.partial(ocean_kernel, advance),
        grid_spec=pltpu.PrefetchScalarGridSpec(
            num_scalar_prefetch=1,
            grid=(1,),
            in_specs=[SMEM] + [HBM] * own_copies + [whole(x) for x in args[1 + own_copies :]],
            out_specs=[whole(o) for o in outs],
            scratch_shapes=scratch,
        ),
        out_shape=outs,
        compiler_params=PARAMS,
        name=f"ocean{advance}",
    )(comp, *args)


def absorb_kernel(
    sc, y_hbm, t_ref, speed_ref, depth_ref, t2_ref, irr_ref, row0_ref, row1_ref, col0_ref, col1_ref, chl_ref, y_ref, sem
):
    rows, cols, levels = t_ref.shape
    flat = (rows * cols, levels)
    copy = pltpu.make_async_copy(y_hbm.at[:, 0], y_ref, sem)
    copy.start()
    copy.wait()

    def gather(s, carry):
        chl_ref[s] = softplus(y_ref[sc[1 + s]])
        return carry

    lax.fori_loop(0, rows, gather, 0, unroll=2)
    chl = chl_ref[...].reshape(flat)
    sums = level_sums(chl, level_matrix(levels, "prefix"))
    absorbed, irradiance = light(chl, sums, level_of(flat))
    wet = wet_of(depth_ref[0], t_ref.shape)
    both = (absorbed[0] + absorbed[1]).reshape(t_ref.shape)
    t2_ref[...] = t_ref[...] + advance_marine * heat_gain * (wet * both)
    irr_ref[...] = irradiance.reshape(t_ref.shape)
    for f, ref in enumerate((speed_ref.at[0], speed_ref.at[1], t2_ref)):
        row0_ref[f] = ref[0]
        row1_ref[f] = ref[rows - 1]
        for y in range(rows):
            col0_ref[f, pl.ds(y, 1)] = ref[y, :1]
            col1_ref[f, pl.ds(y, 1)] = ref[y, cols - 1 :]


def second_kernel(
    sc, y_ref, irr_ref, t1_ref, r1_ref, depth_ref, share_ref, heat_ref, a_ref, b_ref, g_ref, n_ref, chl_ref
):
    patches, _, cols, levels = y_ref.shape
    flat = (patches * cols, levels)
    whole = (patches, cols, levels)

    def one(s, carry):
        owner = sc[1 + s]
        wet = wet_of(depth_ref[0, s], (cols, levels))
        warm = jnp.exp(heating_speed * t1_ref[s])
        up = half_rise(r1_ref[s])
        y = [y_ref[owner, i] for i in range(len(KEPT))]
        g = uptake_rate * irr_ref[s] * saturation(y[3])
        for ref, i, k in ((a_ref, 0, 0), (b_ref, 1, 1), (n_ref, 3, 4)):
            change = warm * y[i + 1] + share_ref[k] * g + transport(up, y[i])
            ref[s] = wet * (y[i] + step_tracer * change)
        chl_ref[s] = softplus(a_ref[s])
        return carry

    lax.fori_loop(0, patches, one, 0, unroll=4)
    chl = chl_ref[...].reshape(flat)
    absorbed, irradiance = light(chl, level_sums(chl, level_matrix(levels, "prefix")), level_of(flat))
    wet = wet_of(depth_ref[0], whole)
    heat_ref[...] = advance_marine * heat_gain * (wet * (absorbed[0] + absorbed[1]).reshape(whole))
    g_ref[...] = uptake_rate * irradiance.reshape(whole) * saturation(n_ref[...])


def third_kernel(sc, a_ref, b_ref, g_ref, t2_ref, r2_ref, depth_ref, share_ref, band_ref, chl_ref):
    patches, cols, levels = a_ref.shape
    flat = (patches * cols, levels)
    whole = (patches, cols, levels)

    def one(s, carry):
        wet = wet_of(depth_ref[0, s], (cols, levels))
        warm = jnp.exp(heating_speed * t2_ref[s])
        a = a_ref[s]
        change = warm * b_ref[s] + share_ref[0] * g_ref[s] + transport(half_rise(r2_ref[s]), a)
        chl_ref[s] = softplus(wet * (a + step_tracer * change))
        return carry

    lax.fori_loop(0, patches, one, 0, unroll=4)
    chl = chl_ref[...].reshape(flat)
    absorbed, _ = light(chl, level_sums(chl, level_matrix(levels, "prefix")), level_of(flat))
    wet = wet_of(depth_ref[0], whole)
    for band in range(2):
        band_ref[:, band] = wet * absorbed[band].reshape(whole)


def last_ocean_kernel(
    sc, speed_ref, t_ref, north_ref, south_ref, east_ref, west_ref, depth_ref, heat_ref, out_ref, div_ref
):
    rows, cols, levels = t_ref.shape
    place = lax.broadcasted_iota(jnp.int32, (cols, levels), 0)
    sources = (speed_ref.at[0], speed_ref.at[1], t_ref)
    for y in range(rows):
        wet = [wet_of(depth_ref[i, y], (cols, levels)) for i in range(5)]

        def east_of(f):
            return jnp.where(place == cols - 1, east_ref[f, pl.ds(y, 1)], pltpu.roll(sources[f][y], cols - 1, 0))

        def west_of(f):
            return jnp.where(place == 0, west_ref[f, pl.ds(y, 1)], pltpu.roll(sources[f][y], 1, 0))

        def north_of(f):
            return sources[f][y + 1] if y < rows - 1 else north_ref[f]

        def south_of(f):
            return sources[f][y - 1] if y > 0 else south_ref[f]

        u, v, t = (ref[y] for ref in sources)
        own = 0.5 * wet[0]
        east = (u + east_of(0)) * (own * wet[1])
        west = (west_of(0) + u) * (own * wet[2])
        north = (v + north_of(1)) * (own * wet[3])
        south = (south_of(1) + v) * (own * wet[4])
        div_ref[y] = east - west + north - south
        e, w, n, s = east_of(2), west_of(2), north_of(2), south_of(2)
        spread = wet[1] * (e - t) + wet[2] * (w - t) + wet[3] * (n - t) + wet[4] * (s - t)
        carry_along = 0.5 * (east * (t + e) - west * (w + t) + north * (t + n) - south * (s + t))
        change = spreading * spread - carry_along
        out_ref[1, sc[1 + y], 1] = wet[0] * (t + advance_marine * change) + heat_ref[y]
    sums = level_sums(div_ref[...].reshape(rows * cols, levels), level_matrix(levels, "below"))
    div_ref[...] = -sums.reshape(rows, cols, levels)
    for y in range(rows):
        out_ref[1, sc[1 + y], 0] = div_ref[y]
    out_ref[0] = jnp.zeros(out_ref.shape[1:], jnp.float32)


def join_kernel(sc, absorbed_ref, flux_ref, other_ref, out_ref):
    patches, _, half, levels = absorbed_ref.shape

    @pl.when(sc[0] == 0)
    def _():
        for s in range(patches):
            for f in range(2):
                out_ref[f, s, :half] = absorbed_ref[s, f]
                out_ref[f, s, half:] = other_ref[s, f]

    @pl.when(sc[0] != 0)
    def _():
        for s in range(patches):
            for f in range(2):
                for part in range(2):
                    out_ref[f, s, part * half : (part + 1) * half] = flux_ref[part, s, f]


def call(kernel, comp, args, specs, outs, scratch=(), name=None, sems=()):
    return pl.pallas_call(
        kernel,
        grid_spec=pltpu.PrefetchScalarGridSpec(
            num_scalar_prefetch=1,
            grid=(1,),
            in_specs=[spec or whole(a) for spec, a in zip(specs, args)],
            out_specs=[whole(o) for o in outs],
            scratch_shapes=[pltpu.VMEM(s, jnp.float32) for s in scratch] + list(sems),
        ),
        out_shape=outs,
        compiler_params=PARAMS,
        name=name,
    )(comp, *args)


def exchange_rows(low, high):
    count = lax.axis_size("py")
    north = lax.ppermute(low, "py", [((i + 1) % count, i) for i in range(count)])
    south = lax.ppermute(high, "py", [(i, (i + 1) % count) for i in range(count)])
    return north, south


def exchange_cols(low, high):
    count = lax.axis_size("px")
    east = lax.ppermute(low, "px", [((i + 1) % count, i) for i in range(count)])
    west = lax.ppermute(high, "px", [(i, (i + 1) % count) for i in range(count)])
    return east, west


def far_columns(block):
    count = lax.axis_size("px")
    east = [(i, (i + 1) % count) for i in range(count)]
    west = [(count + (i + 1) % count, count + i) for i in range(count)]
    return lax.ppermute(block, ("comp", "px"), east + west)


def east_column(block):
    count = lax.axis_size("px")
    return lax.ppermute(block, ("comp", "px"), [((i + 1) % count, count + i) for i in range(count)])


def exchange_half_cols(low, high):
    count = lax.axis_size("px")
    line = [(h % 2) * count + h // 2 for h in range(2 * count)]
    ahead = [(line[h], line[(h + 1) % len(line)]) for h in range(len(line))]
    east = lax.ppermute(low, ("comp", "px"), [(b, a) for a, b in ahead])
    west = lax.ppermute(high, ("comp", "px"), ahead)
    return east, west


def in_hbm(x):
    return pltpu.with_memory_space_constraint(x, pltpu.HBM)


def in_vmem(x):
    return pltpu.with_memory_space_constraint(x, pltpu.VMEM)


def to_owners(blocks):
    return lax.all_to_all(blocks, ("py", "px"), split_axis=0, concat_axis=0, tiled=True)


def swap(block):
    return lax.ppermute(block, "comp", [(0, 1), (1, 0)])


def pick(blocks, order, axis):
    return jnp.stack(
        [lax.dynamic_index_in_dim(blocks, order[k], axis, keepdims=False) for k in range(order.shape[0])], axis
    )


def table(levels, pattern):
    return level_matrix(levels, pattern).astype(jnp.float32)


def product(values, matrix):
    return jnp.einsum("...j,jk->...k", values, matrix, precision=lax.Precision.HIGHEST)


def general_light(conc, wet, loading):
    chl = jax.nn.softplus(jnp.einsum("f...,f->...", conc, loading, precision=lax.Precision.HIGHEST))
    levels = chl.shape[-1]
    absorbed, irradiance = light(chl, product(chl, table(levels, "prefix")), level_of(chl.shape))
    return wet * jnp.stack(absorbed), irradiance


def general_tracers(conc, rise, heat, irradiance, wet, matrix, share):
    none = jnp.zeros_like(conc[..., :1])
    top = jnp.concatenate([none, 0.5 * (conc[..., 1:] + conc[..., :-1]) * rise[..., 1:]], axis=-1)
    below = jnp.concatenate([top[..., 1:], none], axis=-1)
    mixed = jnp.einsum("ij,j...->i...", matrix, conc, precision=lax.Precision.HIGHEST)
    growth = uptake_rate * irradiance * saturation(conc[0])
    change = (
        jnp.exp(heating_speed * heat) * mixed
        + share.reshape((-1,) + (1,) * (conc.ndim - 1)) * growth + below - top
    )
    return wet * (conc + step_tracer * change)


def general_ocean(u, v, t, absorb, depth, coriolis):
    levels = t.shape[-1]
    fields = jnp.stack([u, v, t])
    north, south = exchange_rows(fields[:, 0], fields[:, -1])
    east, west = exchange_cols(fields[:, :, 0], fields[:, :, -1])
    tall = jnp.concatenate([south[:, None], fields, north[:, None]], axis=1)
    wide = jnp.concatenate([west[:, :, None], fields, east[:, :, None]], axis=2)
    around = (fields, wide[:, :, 2:], wide[:, :, :-2], tall[:, 2:], tall[:, :-2])
    above = table(levels, "above")
    u, v, t = ([x[f] for x in around] for f in range(3))
    p = [weight_pull_factor * product(x, above) for x in t]
    wet = [wet_of(depth[i], t[0].shape) for i in range(5)]

    def spread(x):
        return sum(wet[i] * (x[i] - x[0]) for i in range(1, 5))

    east = 0.5 * (u[0] + u[1]) * wet[0] * wet[1]
    west = 0.5 * (u[2] + u[0]) * wet[2] * wet[0]
    north = 0.5 * (v[0] + v[3]) * wet[0] * wet[3]
    south = 0.5 * (v[4] + v[0]) * wet[4] * wet[0]
    carry_along = 0.5 * (
        east * (t[0] + t[1]) - west * (t[2] + t[0]) + north * (t[0] + t[3]) - south * (t[4] + t[0])
    )
    zonal = 0.5 * (wet[1] * (p[1] - p[0]) + wet[2] * (p[0] - p[2]))
    merid = 0.5 * (wet[3] * (p[3] - p[0]) + wet[4] * (p[0] - p[4]))
    turn = coriolis[:, None, None]
    rise = -product(east - west + north - south, table(levels, "below"))
    return (
        wet[0] * (u[0] + advance_marine * (turn * v[0] - zonal + viscosity * spread(u) - damping * u[0])),
        wet[0] * (v[0] + advance_marine * (-turn * u[0] - merid + viscosity * spread(v) - damping * v[0])),
        wet[0] * (t[0] + advance_marine * (spreading * spread(t) - carry_along + heat_gain * (absorb[0] + absorb[1]))),
        rise,
    )


def general(linked, u, v, t, tracers, depth, tracer_depth, holder_rank, patch_index, coriolis, matrix, share, loading):
    comp_index = lax.axis_index("comp")
    first = comp_index == 0
    fields, patches, strip, levels = tracers.shape
    half = strip // 2
    indices = jnp.arange(patches, dtype=jnp.int32)
    owner_row = lax.dynamic_index_in_dim(holder_rank, patch_index, 0, keepdims=False)
    inverse_row = jnp.sum(jnp.where(owner_row[:, None] == indices[None], indices[:, None], 0), axis=0)

    def own_half(x):
        return lax.dynamic_slice_in_dim(x, comp_index * half, half, x.ndim - 2)

    partner = swap(linked)
    absorb = jnp.where(first, linked, partner)
    flux = own_half(jnp.where(first, partner, linked))
    conc = own_half(tracers)
    wet = wet_of(tracer_depth, conc.shape[1:])
    irradiance = general_light(conc, wet, loading)[1]
    grid = t.shape
    for _ in range(3):
        u, v, t, rise = general_ocean(u, v, t, absorb.reshape((2,) + grid), depth, coriolis)
        conc = general_tracers(conc, flux[0], flux[1], irradiance, wet, matrix, share)
        absorbed, irradiance = general_light(conc, wet, loading)
        both = own_half(pick(jnp.stack([rise, t]).reshape(2, patches, strip, levels), inverse_row, 1))
        send = jnp.concatenate([both, absorbed])
        back = lax.all_to_all(send, ("py", "px"), split_axis=1, concat_axis=1, tiled=True)
        flux = back[:2]
        mine = pick(back[2:], owner_row, 1)
        other = swap(mine)
        absorb = jnp.where(first, jnp.concatenate([mine, other], 2), jnp.concatenate([other, mine], 2))
    other = swap(flux)
    joined = jnp.where(first, jnp.concatenate([flux, other], 2), jnp.concatenate([other, flux], 2))
    return jnp.where(first, absorb, joined)


def shards(
    current_speeds,
    thermal_anomaly,
    solute_amounts,
    delayed_link_source,
    marine_indicator,
    floor_layer_index,
    holder_rank,
    biota_exchange_matrix,
    photic_absorb_share,
    chroma_loading,
):
    comp_index = lax.axis_index("comp")
    row_index = lax.axis_index("py")
    col_index = lax.axis_index("px")
    rows_mesh = lax.axis_size("py")
    cols_mesh = lax.axis_size("px")
    patches = rows_mesh * cols_mesh
    fields, _, columns, levels = solute_amounts.shape
    strip = columns // patches
    half = strip // 2
    patch_index = row_index * cols_mesh + col_index
    first = comp_index == 0

    linked = delayed_link_source.reshape(2, patches, strip, levels)
    tracers = solute_amounts.reshape(fields, patches, strip, levels)
    u0, v0 = current_speeds[0], current_speeds[1]

    column_depth = marine_indicator * floor_layer_index
    wrapped = jnp.concatenate([column_depth[:, -2:], column_depth, column_depth[:, :2]], axis=1)
    padded = jnp.pad(wrapped, ((2, 2), (0, 0)))
    far = lax.dynamic_slice(padded, (row_index * CY, col_index * CX), (CY + 4, CX + 4))
    local = far[1:-1, 1:-1]
    gap = 4
    near = lax.dynamic_slice_in_dim(far, comp_index * half, half + 4, 1)
    wide_depth = jnp.concatenate(
        [near[:, 2:], jnp.zeros((CY + 4, gap), jnp.int32), near[:, :2]], axis=1
    )[..., None]
    depth = jnp.stack([local[1:-1, 1:-1], local[1:-1, 2:], local[1:-1, :-2], local[2:, 1:-1], local[:-2, 1:-1]])
    depth = depth[..., None]
    by_strip = (
        column_depth.reshape(rows_mesh, CY, cols_mesh, CX).transpose(0, 2, 1, 3).reshape(patches, patches, strip)
    )
    here = (holder_rank == patch_index)[:, :, None]
    tracer_depth = jnp.sum(jnp.where(here, by_strip, 0), axis=1)
    tracer_depth = lax.dynamic_slice_in_dim(tracer_depth, comp_index * half, half, 1)[..., None]
    owner_row = lax.dynamic_index_in_dim(holder_rank, patch_index, 0, keepdims=False)
    side_index = comp_index.astype(jnp.int32)[None]
    comp = jnp.concatenate([side_index, owner_row])
    ys = (row_index * CY - 1 + jnp.arange(CY + 2, dtype=jnp.int32)).astype(jnp.float32)
    coriolis = coriolis_scale * (2.0 * (ys + 0.5) / (CY * rows_mesh) - 1.0)

    if half % 8 or strip != CX:
        out = general(
            linked, u0, v0, thermal_anomaly, tracers, depth, tracer_depth, holder_rank, patch_index, coriolis[1:-1],
            biota_exchange_matrix, photic_absorb_share, chroma_loading,
        )
        return out.reshape(1, 2, 1, columns, levels)

    linked, tracers, current_speeds, thermal_anomaly = (
        in_hbm(x) for x in (linked, tracers, current_speeds, thermal_anomaly)
    )
    sent, *edges = pack(side_index, linked, current_speeds, thermal_anomaly)
    got = swap(sent)
    times = functools.partial(jnp.dot, precision=lax.Precision.HIGHEST)
    unit = (jnp.arange(fields) == 0).astype(jnp.float32)
    chain = [jnp.stack([chroma_loading, unit])]
    for _ in range(3):
        chain.append(times(chain[-1], biota_exchange_matrix))
    weights = jnp.stack([c[0] for c in chain] + [c[1] for c in chain[:3]])
    shares = times(weights, photic_absorb_share)

    projected, g = project(side_index, tracers, weights)
    low, high, left, right, first_column = edges
    north, south = exchange_rows(low, high)
    edge = east_column(first_column)
    left, right, projected, g = lax.optimization_barrier((left, right, projected, g))
    projected, g = in_vmem(projected), in_vmem(g)
    outer = shape_of(4, 2, CY + 2, levels)
    [sides] = call(corner_kernel, side_index, (left, right, north, south), [None] * 4, (outer,), (), "corner")
    sides = far_columns(sides)
    kept = first_tracer(side_index, projected, g, got, linked, tracer_depth, shares)
    kept, north, south, sides, edge = lax.optimization_barrier((kept, north, south, sides, edge))
    arrived = to_owners(kept)

    [ring] = call(ring_kernel, side_index, (north, south), [None] * 2, (shape_of(2, CX, levels),), (), "ring")
    args = (current_speeds, thermal_anomaly, linked, got, north, south, sides, edge, swap(ring))
    speeds1, wide_t1, t1, r1 = ocean(1, comp, coriolis, args, wide_depth, CY, half)
    r1 = in_hbm(r1)
    speeds2, t2, r2 = ocean(2, comp, coriolis, (speeds1, wide_t1), wide_depth, CY, half)
    arrived, speeds2, t2 = lax.optimization_barrier((arrived, speeds2, t2))
    speeds2, t2, r2 = in_vmem(speeds2), in_vmem(t2), in_hbm(r2)

    depth_half = pl.BlockSpec((5, CY, half, 1), lambda i, c: (0, 0, c[0], 0))
    piece = shape_of(CY, half, levels)
    scratch = (CY, half, levels)
    line = shape_of(3, half, levels)
    side = shape_of(3, CY, levels)

    t2, irr1, *edges = call(
        absorb_kernel, comp, (arrived, t2, speeds2, depth), [HBM, None, None, depth_half],
        (piece, piece, line, line, side, side), [scratch] * 2, "absorb", [pltpu.SemaphoreType.DMA],
    )
    halos2 = exchange_rows(edges[0], edges[1]) + exchange_half_cols(edges[2], edges[3])
    heat, a, b, g = call(
        second_kernel, comp, (arrived, irr1, t1, r1, depth, shares),
        [None] * 4 + [depth_half, SMEM],
        (piece,) * 4, [scratch] * 2, "second",
    )
    [back] = call(
        last_ocean_kernel, comp, (speeds2, t2, *halos2, depth, heat),
        [None] * 6 + [depth_half, None],
        (shape_of(2, patches, 2, half, levels),), [scratch], "last_ocean",
    )
    flux = lax.all_to_all(
        back.reshape(2 * patches, 2, half, levels), ("comp", "py", "px"), split_axis=0, concat_axis=0, tiled=True
    ).reshape(2, patches, 2, half, levels)
    [absorbed] = call(
        third_kernel, comp, (a, b, g, t2, r2, depth, shares),
        [None] * 5 + [depth_half, SMEM], (shape_of(CY, 2, half, levels),), [scratch], "third",
    )
    other = swap(absorbed)
    [out] = call(
        join_kernel, comp, (absorbed, flux, other), [None] * 3, (shape_of(2, patches, strip, levels),), (), "join"
    )
    return out.reshape(1, 2, 1, columns, levels)


def solution(mesh):
    placed = (
        P(None, "py", "px", None),
        P("py", "px", None),
        P(None, ("py", "px"), None, None),
        P("comp", None, ("py", "px"), None, None),
        P(),
        P(),
        P(),
        P(),
        P(),
        P(),
    )
    return jax.shard_map(
        shards,
        mesh=mesh,
        in_specs=placed,
        out_specs=P("comp", None, ("py", "px"), None, None),
        check_vma=False,
    )
```

```python
import functools

import jax
import jax.numpy as jnp
from jax import lax
from jax.experimental import pallas as pl
from jax.experimental.pallas import tpu as pltpu
from jax.sharding import PartitionSpec as P

advance_marine = 0.1
spreading = 0.1
viscosity = 0.1
damping = 0.05
heat_gain = 0.2
weight_pull_factor = 0.05
coriolis_scale = 1.0
step_tracer = 0.1
heating_speed = 0.06
uptake_rate = 0.01
water_absorb = (0.02, 0.003)
pigment_absorb = (0.03, 0.004)
surface_light = (40.0, 60.0)
CY = 16
CX = 32
KEPT = (0, 1, 2, 4, 5)
SMEM = pl.BlockSpec(memory_space=pltpu.SMEM)
PARAMS = pltpu.CompilerParams(vmem_limit_bytes=28 * 1024 * 1024)
HBM = pl.BlockSpec(memory_space=pltpu.HBM)
STREAMED = pltpu.CompilerParams(vmem_limit_bytes=60 * 1024 * 1024)


def whole(array):
    zeros = (0,) * len(array.shape)
    return pl.BlockSpec(array.shape, lambda i, c: zeros)


def shape_of(*dims):
    return jax.ShapeDtypeStruct(dims, jnp.float32)


def level_matrix(levels, pattern):
    row = lax.broadcasted_iota(jnp.int32, (levels, levels), 0)
    col = lax.broadcasted_iota(jnp.int32, (levels, levels), 1)
    if pattern == "above":
        m = jnp.where(row < col, 1.0, jnp.where(row == col, 0.5, 0.0))
    elif pattern == "below":
        m = jnp.where(row >= col, 1.0, 0.0)
    else:
        m = jnp.where(row < col, 1.0, 0.0)
    return m.astype(jnp.bfloat16)


def level_sums(x, matrix):
    hi = x.astype(jnp.bfloat16)
    rest = x - hi.astype(jnp.float32)
    mid = rest.astype(jnp.bfloat16)
    low = (rest - mid.astype(jnp.float32)).astype(jnp.bfloat16)
    dot = functools.partial(jnp.dot, preferred_element_type=jnp.float32)
    return dot(hi, matrix) + dot(mid, matrix) + dot(low, matrix)


def softplus(x):
    return jnp.maximum(x, 0.0) + jnp.log1p(jnp.exp(-jnp.abs(x)))


def light(chl, sums, level):
    absorbed, irradiance = [], None
    for water, pigment, surface in zip(water_absorb, pigment_absorb, surface_light):
        fade = jnp.exp(-0.5 * (water + pigment * chl))
        intensity = surface * jnp.exp(-(water * level + pigment * sums))
        absorbed.append(intensity * (1.0 - fade * fade))
        part = intensity * fade
        irradiance = part if irradiance is None else irradiance + part
    return absorbed, irradiance


def saturation(n):
    return n * n / (1.0 + n * n)


def transport(rise_half, y):
    top = rise_half * (y + pltpu.roll(y, 1, 1))
    return pltpu.roll(top, top.shape[1] - 1, 1) - top


def wet_of(depth, shape):
    level = lax.broadcasted_iota(jnp.int32, shape, len(shape) - 1)
    return jnp.where(level < depth, 1.0, 0.0)


def level_of(shape):
    return lax.broadcasted_iota(jnp.int32, shape, len(shape) - 1).astype(jnp.float32)


def half_rise(rise):
    k = lax.broadcasted_iota(jnp.int32, rise.shape, 1)
    return jnp.where(k > 0, 0.5 * rise, 0.0)


def project_kernel(sc, x_hbm, w_ref, y_ref, g_ref, x_ref, chl_ref, sems):
    pieces, fields, block, cols, levels = x_ref.shape
    own = pl.ds(pl.multiple_of(sc[0] * cols, cols), cols)
    copies = [
        pltpu.make_async_copy(x_hbm.at[:, pl.ds(i * block, block), own], x_ref.at[i], sems.at[i]) for i in range(pieces)
    ]
    for copy in copies:
        copy.start()
    mixed = [k for k in range(y_ref.shape[0]) if k != 4]
    prefix = level_matrix(levels, "prefix")
    flat = (block * cols, levels)
    for i, copy in enumerate(copies):
        copy.wait()

        def one(q, carry):
            at = i * block + q
            value = x_ref[i, 0, q]
            y_ref[4, at] = value
            totals = [w_ref[k, 0] * value for k in mixed]
            for j in range(1, fields):
                value = x_ref[i, j, q]
                totals = [t + w_ref[k, j] * value for t, k in zip(totals, mixed)]
            for k, total in zip(mixed, totals):
                y_ref[k, at] = total
            chl_ref[q] = softplus(totals[0])
            return carry

        lax.fori_loop(0, block, one, 0)
        chl = chl_ref[...].reshape(flat)
        _, irradiance = light(chl, level_sums(chl, prefix), level_of(flat))
        n = x_ref[i, 0].reshape(flat)
        g_ref[i * block : (i + 1) * block] = (uptake_rate * irradiance * saturation(n)).reshape(block, cols, levels)


def project(comp, tracers, weights):
    fields, patches, strip, levels = tracers.shape
    half = strip // 2
    pieces = 4
    block = patches // pieces
    outs = (shape_of(weights.shape[0], patches, half, levels), shape_of(patches, half, levels))
    return pl.pallas_call(
        project_kernel,
        grid_spec=pltpu.PrefetchScalarGridSpec(
            num_scalar_prefetch=1,
            grid=(1,),
            in_specs=[HBM, SMEM],
            out_specs=[whole(o) for o in outs],
            scratch_shapes=[
                pltpu.VMEM((pieces, fields, block, half, levels), jnp.float32),
                pltpu.VMEM((block, half, levels), jnp.float32),
                pltpu.SemaphoreType.DMA((pieces,)),
            ],
        ),
        out_shape=outs,
        compiler_params=PARAMS,
        name="project",
    )(comp, tracers, weights)


def first_tracer_kernel(sc, y_ref, g_ref, got_ref, own_ref, depth_ref, share_ref, out_ref):
    patches, cols, levels = g_ref.shape
    first = sc[0] == 0

    def one(q, carry):
        rise = jnp.where(first, got_ref[0, q], own_ref[0, q])
        heat = jnp.where(first, got_ref[1, q], own_ref[1, q])
        warm = jnp.exp(heating_speed * heat)
        wet = wet_of(depth_ref[q], (cols, levels))
        up = half_rise(rise)
        g = g_ref[q]
        for place, k in enumerate(KEPT):
            y = y_ref[k, q]
            change = warm * y_ref[k + 1, q] + share_ref[k] * g + transport(up, y)
            out_ref[q, place] = wet * (y + step_tracer * change)
        return carry

    lax.fori_loop(0, patches, one, 0, unroll=2)


def half_spec(lead, cols, levels):
    zeros = (0,) * len(lead)
    return pl.BlockSpec(lead + (cols, levels), lambda i, c: zeros + (c[0], 0))


def first_tracer(comp, projected, g, got, linked, depth, shares):
    kinds, patches, half, levels = projected.shape
    block = 4
    return pl.pallas_call(
        first_tracer_kernel,
        grid_spec=pltpu.PrefetchScalarGridSpec(
            num_scalar_prefetch=1,
            grid=(patches // block,),
            in_specs=[
                pl.BlockSpec((kinds, block, half, levels), lambda i, c: (0, i, 0, 0)),
                pl.BlockSpec((block, half, levels), lambda i, c: (i, 0, 0)),
                pl.BlockSpec((2, block, half, levels), lambda i, c: (0, i, 0, 0)),
                pl.BlockSpec((2, block, half, levels), lambda i, c: (0, i, c[0], 0)),
                pl.BlockSpec((block, half, 1), lambda i, c: (i, 0, 0)),
                SMEM,
            ],
            out_specs=pl.BlockSpec((block, len(KEPT), half, levels), lambda i, c: (i, 0, 0, 0)),
        ),
        out_shape=shape_of(patches, len(KEPT), half, levels),
        compiler_params=PARAMS,
        name="first_tracer",
    )(comp, projected, g, got, linked, depth, shares)


def pack_kernel(sc, linked_ref, row0_ref, row1_ref, col0_ref, col1_ref, t0_ref, t1_ref, tc0_ref, tc1_ref,
                sent_ref, low_ref, high_ref, left_ref, right_ref, first_ref):
    _, strips, strip, levels = linked_ref.shape
    half = strip // 2

    @pl.when(sc[0] == 0)
    def _():
        for part in range(2):
            cols = slice(part * half, (part + 1) * half)
            sent_ref[part] = linked_ref[0, :, cols] + linked_ref[1, :, cols]

    @pl.when(sc[0] != 0)
    def _():
        sent_ref[...] = linked_ref[:, :, :half]

    last = col1_ref.shape[2]
    tall = strips - 2
    for i in range(2):
        for f in range(2):
            left_ref[f, i] = col0_ref[f, :, i]
            right_ref[f, i] = col1_ref[f, :, last - 2 + i]
        left_ref[2, i] = tc0_ref[:, i]
        right_ref[2, i] = tc1_ref[:, last - 2 + i]
        left_ref[3, i] = linked_ref[0, :, i] + linked_ref[1, :, i]
        right_ref[3, i] = linked_ref[0, :, strip - 2 + i] + linked_ref[1, :, strip - 2 + i]
    first_ref[...] = left_ref[3, 0]
    for f in range(2):
        low_ref[f] = row0_ref[f]
        high_ref[f] = row1_ref[f]
    low_ref[2] = t0_ref[...]
    high_ref[2] = t1_ref[...]
    low_ref[3] = linked_ref[0, :2] + linked_ref[1, :2]
    high_ref[3] = linked_ref[0, tall:] + linked_ref[1, tall:]


def corner_kernel(sc, left_ref, right_ref, north_ref, south_ref, out_ref):
    rows = left_ref.shape[2]
    cols = north_ref.shape[2]

    def fill(source, at):
        for f in range(source.shape[0]):
            for i in range(2):
                out_ref[f, i, :rows] = source[f, i]
                out_ref[f, i, rows : rows + 1] = south_ref[f, 1, at + i : at + i + 1]
                out_ref[f, i, rows + 1 :] = north_ref[f, 0, at + i : at + i + 1]

    @pl.when(sc[0] == 0)
    def _():
        fill(right_ref, cols - 2)

    @pl.when(sc[0] != 0)
    def _():
        fill(left_ref, 0)


def ring_kernel(sc, north_ref, south_ref, ring_ref):
    ring_ref[0] = south_ref[3, 1]
    ring_ref[1] = north_ref[3, 0]


def pack(comp, linked, speeds, heat):
    _, strips, strip, levels = linked.shape
    rows, cols, _ = heat.shape
    outs = (
        shape_of(2, strips, strip // 2, levels), shape_of(4, 2, cols, levels), shape_of(4, 2, cols, levels),
        shape_of(4, 2, rows, levels), shape_of(4, 2, rows, levels), shape_of(rows, levels),
    )
    edge = min(8, cols)
    return pl.pallas_call(
        pack_kernel,
        grid_spec=pltpu.PrefetchScalarGridSpec(
            num_scalar_prefetch=1,
            grid=(1,),
            in_specs=[
                whole(linked),
                pl.BlockSpec((2, 2, cols, levels), lambda i, c: (0, 0, 0, 0)),
                pl.BlockSpec((2, 2, cols, levels), lambda i, c: (0, rows // 2 - 1, 0, 0)),
                pl.BlockSpec((2, rows, edge, levels), lambda i, c: (0, 0, 0, 0)),
                pl.BlockSpec((2, rows, edge, levels), lambda i, c: (0, 0, cols // edge - 1, 0)),
                pl.BlockSpec((2, cols, levels), lambda i, c: (0, 0, 0)),
                pl.BlockSpec((2, cols, levels), lambda i, c: (rows // 2 - 1, 0, 0)),
                pl.BlockSpec((rows, edge, levels), lambda i, c: (0, 0, 0)),
                pl.BlockSpec((rows, edge, levels), lambda i, c: (0, cols // edge - 1, 0)),
            ],
            out_specs=[whole(o) for o in outs],
        ),
        out_shape=outs,
        compiler_params=STREAMED,
        name="pack",
    )(comp, linked, speeds, speeds, speeds, speeds, heat, heat, heat, heat)


def wide_rows(sc, speed_hbm, heat_hbm, linked_hbm, got_ref, north_ref, south_ref, side_ref, edge_ref, ring_ref,
              x_ref, near_ref, absorb_ref, linked_ref, sems):
    rows, cols, levels = heat_hbm.shape
    half = cols // 2
    comp = sc[0]
    first = comp == 0
    width = x_ref.shape[2]
    rim = width - half
    own = pl.ds(pl.multiple_of(comp * half, half), half)
    near = pl.ds(pl.multiple_of(half - rim * comp, 8), rim)
    copies = [pltpu.make_async_copy(linked_hbm, linked_ref, sems.at[0])]
    for f, source in enumerate((speed_hbm.at[0], speed_hbm.at[1], heat_hbm)):
        copies.append(
            pltpu.make_async_copy(source.at[:, own], x_ref.at[f, pl.ds(2, rows), pl.ds(0, half)], sems.at[1 + f])
        )
        copies.append(pltpu.make_async_copy(source.at[:, near], near_ref.at[f], sems.at[4 + f]))
    for copy in copies:
        copy.start()
    place = lax.broadcasted_iota(jnp.int32, (rim, levels), 0)
    none = jnp.zeros((rim, levels), jnp.float32)
    far_place = (1 - comp) * (rim - 2)
    for copy in copies:
        copy.wait()
    for f in range(3):
        x_ref[f, :2, :half] = south_ref[f, :, own]
        x_ref[f, rows + 2 :, :half] = north_ref[f, :, own]
        x_ref[f, 0, half:] = none
        x_ref[f, rows + 3, half:] = none
        for o in range(rows + 2):
            if o == 0:
                r, cells = rows, south_ref[f, 1, near]
            elif o == rows + 1:
                r, cells = rows + 1, north_ref[f, 0, near]
            else:
                r, cells = o - 1, near_ref[f, o - 1]
            for i in range(2):
                cells = jnp.where(place == far_place + i, side_ref[f, i, r : r + 1], cells)
            x_ref[f, o + 1, half:] = cells
    for o, side in ((0, 0), (rows + 1, 1)):
        here = (south_ref[3, 1] if side == 0 else north_ref[3, 0])[:half]
        absorb_ref[o, :half] = jnp.where(first, here, ring_ref[side, half:])
        absorb_ref[o, half:] = none
    for y in range(rows):
        both = linked_ref[0, y] + linked_ref[1, y]
        absorb_ref[y + 1, :half] = jnp.where(first, both[:half], got_ref[1, y])
        cells = jnp.where(first, both[half : half + rim], got_ref[0, y, half - rim :])
        far = jnp.where(first, side_ref[3, 1, y : y + 1], edge_ref[y : y + 1])
        absorb_ref[y + 1, half:] = jnp.where(place == (1 - comp) * (rim - 1), far, cells)


def ocean_kernel(advance, sc, coriolis_ref, *refs):
    if advance == 1:
        *sources, depth_ref, next_ref, tn_ref, inner_ref, rise_ref, x_ref, near_ref, absorb_ref = refs[:-4]
        linked_ref, sems, p_ref, div_ref = refs[-4:]
        wide_rows(sc, *sources, x_ref, near_ref, absorb_ref, linked_ref, sems)
        fields = [x_ref.at[f] for f in range(3)]
    else:
        speed_ref, t_ref, depth_ref, next_ref, tn_ref, rise_ref, p_ref, div_ref = refs
        fields = [speed_ref.at[0], speed_ref.at[1], t_ref]
    tall, width, levels = p_ref.shape
    rows, cols = rise_ref.shape[:2]
    out_width = tn_ref.shape[1]
    p_ref[...] = (
        weight_pull_factor * level_sums(fields[2][...].reshape(tall * width, levels), level_matrix(levels, "above"))
    ).reshape(tall, width, levels)
    lanes = min(128, levels)

    def piece(o, lane):
        part = slice(lane, lane + lanes)
        level = lane + lax.broadcasted_iota(jnp.int32, (width, lanes), 1)

        def beside(x):
            return pltpu.roll(x, width - 1, 0), pltpu.roll(x, 1, 0)

        def field(ref):
            x = ref[o + 1, :, part]
            return (x, *beside(x), ref[o + 2, :, part], ref[o, :, part])

        def wet_at(d):
            return jnp.where(level < depth_ref[d], 1.0, 0.0)

        here = wet_at(o + advance)
        wet = (here, *beside(here), wet_at(o + advance + 1), wet_at(o + advance - 1))
        u, v, t, p = (field(ref) for ref in (*fields, p_ref))
        own = 0.5 * wet[0]
        east = (u[0] + u[1]) * (own * wet[1])
        west = (u[2] + u[0]) * (own * wet[2])
        north = (v[0] + v[3]) * (own * wet[3])
        south = (v[4] + v[0]) * (own * wet[4])
        div_ref[o, :, part] = east - west + north - south
        wets = wet[1] + wet[2] + wet[3] + wet[4]

        def spread(x):
            return wet[1] * x[1] + wet[2] * x[2] + wet[3] * x[3] + wet[4] * x[4] - wets * x[0]

        carry_along = 0.5 * (
            east * (t[0] + t[1]) - west * (t[2] + t[0]) + north * (t[0] + t[3]) - south * (t[4] + t[0])
        )
        change = spreading * spread(t) - carry_along
        if advance == 1:
            change = change + heat_gain * absorb_ref[o, :, part]
        zonal = 0.5 * (wet[1] * (p[1] - p[0]) + wet[2] * (p[0] - p[2]))
        merid = 0.5 * (wet[3] * (p[3] - p[0]) + wet[4] * (p[0] - p[4]))
        turn = coriolis_ref[o + advance - 1]
        results = (
            wet[0] * (u[0] + advance_marine * (turn * v[0] - zonal + viscosity * spread(u) - damping * u[0])),
            wet[0] * (v[0] + advance_marine * (-turn * u[0] - merid + viscosity * spread(v) - damping * v[0])),
            wet[0] * (t[0] + advance_marine * change),
        )
        for ref, value in zip((next_ref.at[0], next_ref.at[1], tn_ref), results):
            ref[o, :, part] = value[:out_width]

    def row(o, carry):
        for lane in range(0, levels, lanes):
            piece(o, lane)
        return carry

    lax.fori_loop(0, tall - 2, row, 0)
    rim = (tall - 2 - rows) // 2
    div = div_ref[rim : rim + rows, :cols].reshape(rows * cols, levels)
    rise_ref[...] = -level_sums(div, level_matrix(levels, "below")).reshape(rows, cols, levels)
    if advance == 1:
        inner_ref[...] = tn_ref[rim : rim + rows, :cols]


def ocean(advance, comp, coriolis, args, depth, rows, cols):
    width, levels = depth.shape[1], args[1].shape[-1]
    patch = shape_of(rows, cols, levels)
    if advance == 1:
        tall = rows + 4
        outs = (shape_of(2, rows + 2, width, levels), shape_of(rows + 2, width, levels), patch, patch)
        scratch = [
            pltpu.VMEM((3, tall, width, levels), jnp.float32),
            pltpu.VMEM((3, rows, width - cols, levels), jnp.float32),
            pltpu.VMEM((rows + 2, width, levels), jnp.float32),
            pltpu.VMEM(args[2].shape, jnp.float32),
            pltpu.SemaphoreType.DMA((7,)),
        ]
    else:
        tall = rows + 2
        outs = (shape_of(2, rows, cols, levels), patch, patch)
        scratch = []
    scratch += [
        pltpu.VMEM((tall, width, levels), jnp.float32), pltpu.VMEM((tall - 2, width, levels), jnp.float32)
    ]
    args = [coriolis, *args, depth]
    own_copies = 3 if advance == 1 else 0
    return pl.pallas_call(
        functools.partial(ocean_kernel, advance),
        grid_spec=pltpu.PrefetchScalarGridSpec(
            num_scalar_prefetch=1,
            grid=(1,),
            in_specs=[SMEM] + [HBM] * own_copies + [whole(x) for x in args[1 + own_copies :]],
            out_specs=[whole(o) for o in outs],
            scratch_shapes=scratch,
        ),
        out_shape=outs,
        compiler_params=PARAMS,
        name=f"ocean{advance}",
    )(comp, *args)


def absorb_kernel(
    sc, y_hbm, t_ref, speed_ref, depth_ref, t2_ref, irr_ref, row0_ref, row1_ref, col0_ref, col1_ref, chl_ref, y_ref, sem
):
    rows, cols, levels = t_ref.shape
    flat = (rows * cols, levels)
    copy = pltpu.make_async_copy(y_hbm.at[:, 0], y_ref, sem)
    copy.start()
    copy.wait()

    def gather(s, carry):
        chl_ref[s] = softplus(y_ref[sc[1 + s]])
        return carry

    lax.fori_loop(0, rows, gather, 0, unroll=2)
    chl = chl_ref[...].reshape(flat)
    sums = level_sums(chl, level_matrix(levels, "prefix"))
    absorbed, irradiance = light(chl, sums, level_of(flat))
    wet = wet_of(depth_ref[0], t_ref.shape)
    both = (absorbed[0] + absorbed[1]).reshape(t_ref.shape)
    t2_ref[...] = t_ref[...] + advance_marine * heat_gain * (wet * both)
    irr_ref[...] = irradiance.reshape(t_ref.shape)
    for f, ref in enumerate((speed_ref.at[0], speed_ref.at[1], t2_ref)):
        row0_ref[f] = ref[0]
        row1_ref[f] = ref[rows - 1]
        for y in range(rows):
            col0_ref[f, pl.ds(y, 1)] = ref[y, :1]
            col1_ref[f, pl.ds(y, 1)] = ref[y, cols - 1 :]


def second_kernel(
    sc, y_ref, irr_ref, t1_ref, r1_ref, depth_ref, share_ref, heat_ref, a_ref, b_ref, g_ref, n_ref, chl_ref
):
    patches, _, cols, levels = y_ref.shape
    flat = (patches * cols, levels)
    whole = (patches, cols, levels)

    def one(s, carry):
        owner = sc[1 + s]
        wet = wet_of(depth_ref[0, s], (cols, levels))
        warm = jnp.exp(heating_speed * t1_ref[s])
        up = half_rise(r1_ref[s])
        y = [y_ref[owner, i] for i in range(len(KEPT))]
        g = uptake_rate * irr_ref[s] * saturation(y[3])
        for ref, i, k in ((a_ref, 0, 0), (b_ref, 1, 1), (n_ref, 3, 4)):
            change = warm * y[i + 1] + share_ref[k] * g + transport(up, y[i])
            ref[s] = wet * (y[i] + step_tracer * change)
        chl_ref[s] = softplus(a_ref[s])
        return carry

    lax.fori_loop(0, patches, one, 0, unroll=4)
    chl = chl_ref[...].reshape(flat)
    absorbed, irradiance = light(chl, level_sums(chl, level_matrix(levels, "prefix")), level_of(flat))
    wet = wet_of(depth_ref[0], whole)
    heat_ref[...] = advance_marine * heat_gain * (wet * (absorbed[0] + absorbed[1]).reshape(whole))
    g_ref[...] = uptake_rate * irradiance.reshape(whole) * saturation(n_ref[...])


def third_kernel(sc, a_ref, b_ref, g_ref, t2_ref, r2_ref, depth_ref, share_ref, band_ref, chl_ref):
    patches, cols, levels = a_ref.shape
    flat = (patches * cols, levels)
    whole = (patches, cols, levels)

    def one(s, carry):
        wet = wet_of(depth_ref[0, s], (cols, levels))
        warm = jnp.exp(heating_speed * t2_ref[s])
        a = a_ref[s]
        change = warm * b_ref[s] + share_ref[0] * g_ref[s] + transport(half_rise(r2_ref[s]), a)
        chl_ref[s] = softplus(wet * (a + step_tracer * change))
        return carry

    lax.fori_loop(0, patches, one, 0, unroll=4)
    chl = chl_ref[...].reshape(flat)
    absorbed, _ = light(chl, level_sums(chl, level_matrix(levels, "prefix")), level_of(flat))
    wet = wet_of(depth_ref[0], whole)
    for band in range(2):
        band_ref[:, band] = wet * absorbed[band].reshape(whole)


def last_ocean_kernel(
    sc, speed_ref, t_ref, north_ref, south_ref, east_ref, west_ref, depth_ref, heat_ref, out_ref, div_ref
):
    rows, cols, levels = t_ref.shape
    place = lax.broadcasted_iota(jnp.int32, (cols, levels), 0)
    sources = (speed_ref.at[0], speed_ref.at[1], t_ref)
    for y in range(rows):
        wet = [wet_of(depth_ref[i, y], (cols, levels)) for i in range(5)]

        def east_of(f):
            return jnp.where(place == cols - 1, east_ref[f, pl.ds(y, 1)], pltpu.roll(sources[f][y], cols - 1, 0))

        def west_of(f):
            return jnp.where(place == 0, west_ref[f, pl.ds(y, 1)], pltpu.roll(sources[f][y], 1, 0))

        def north_of(f):
            return sources[f][y + 1] if y < rows - 1 else north_ref[f]

        def south_of(f):
            return sources[f][y - 1] if y > 0 else south_ref[f]

        u, v, t = (ref[y] for ref in sources)
        own = 0.5 * wet[0]
        east = (u + east_of(0)) * (own * wet[1])
        west = (west_of(0) + u) * (own * wet[2])
        north = (v + north_of(1)) * (own * wet[3])
        south = (south_of(1) + v) * (own * wet[4])
        div_ref[y] = east - west + north - south
        e, w, n, s = east_of(2), west_of(2), north_of(2), south_of(2)
        spread = wet[1] * (e - t) + wet[2] * (w - t) + wet[3] * (n - t) + wet[4] * (s - t)
        carry_along = 0.5 * (east * (t + e) - west * (w + t) + north * (t + n) - south * (s + t))
        change = spreading * spread - carry_along
        out_ref[1, sc[1 + y], 1] = wet[0] * (t + advance_marine * change) + heat_ref[y]
    sums = level_sums(div_ref[...].reshape(rows * cols, levels), level_matrix(levels, "below"))
    div_ref[...] = -sums.reshape(rows, cols, levels)
    for y in range(rows):
        out_ref[1, sc[1 + y], 0] = div_ref[y]
    out_ref[0] = jnp.zeros(out_ref.shape[1:], jnp.float32)


def join_kernel(sc, absorbed_ref, flux_ref, other_ref, out_ref):
    patches, _, half, levels = absorbed_ref.shape

    @pl.when(sc[0] == 0)
    def _():
        for s in range(patches):
            for f in range(2):
                out_ref[f, s, :half] = absorbed_ref[s, f]
                out_ref[f, s, half:] = other_ref[s, f]

    @pl.when(sc[0] != 0)
    def _():
        for s in range(patches):
            for f in range(2):
                for part in range(2):
                    out_ref[f, s, part * half : (part + 1) * half] = flux_ref[part, s, f]


def call(kernel, comp, args, specs, outs, scratch=(), name=None, sems=()):
    return pl.pallas_call(
        kernel,
        grid_spec=pltpu.PrefetchScalarGridSpec(
            num_scalar_prefetch=1,
            grid=(1,),
            in_specs=[spec or whole(a) for spec, a in zip(specs, args)],
            out_specs=[whole(o) for o in outs],
            scratch_shapes=[pltpu.VMEM(s, jnp.float32) for s in scratch] + list(sems),
        ),
        out_shape=outs,
        compiler_params=PARAMS,
        name=name,
    )(comp, *args)


def exchange_rows(low, high):
    count = lax.axis_size("py")
    north = lax.ppermute(low, "py", [((i + 1) % count, i) for i in range(count)])
    south = lax.ppermute(high, "py", [(i, (i + 1) % count) for i in range(count)])
    return north, south


def exchange_cols(low, high):
    count = lax.axis_size("px")
    east = lax.ppermute(low, "px", [((i + 1) % count, i) for i in range(count)])
    west = lax.ppermute(high, "px", [(i, (i + 1) % count) for i in range(count)])
    return east, west


def far_columns(block):
    count = lax.axis_size("px")
    east = [(i, (i + 1) % count) for i in range(count)]
    west = [(count + (i + 1) % count, count + i) for i in range(count)]
    return lax.ppermute(block, ("comp", "px"), east + west)


def east_column(block):
    count = lax.axis_size("px")
    return lax.ppermute(block, ("comp", "px"), [((i + 1) % count, count + i) for i in range(count)])


def exchange_half_cols(low, high):
    count = lax.axis_size("px")
    line = [(h % 2) * count + h // 2 for h in range(2 * count)]
    ahead = [(line[h], line[(h + 1) % len(line)]) for h in range(len(line))]
    east = lax.ppermute(low, ("comp", "px"), [(b, a) for a, b in ahead])
    west = lax.ppermute(high, ("comp", "px"), ahead)
    return east, west


def in_hbm(x):
    return pltpu.with_memory_space_constraint(x, pltpu.HBM)


def in_vmem(x):
    return pltpu.with_memory_space_constraint(x, pltpu.VMEM)


def to_owners(blocks):
    return lax.all_to_all(blocks, ("py", "px"), split_axis=0, concat_axis=0, tiled=True)


def swap(block):
    return lax.ppermute(block, "comp", [(0, 1), (1, 0)])


def pick(blocks, order, axis):
    return jnp.stack(
        [lax.dynamic_index_in_dim(blocks, order[k], axis, keepdims=False) for k in range(order.shape[0])], axis
    )


def table(levels, pattern):
    return level_matrix(levels, pattern).astype(jnp.float32)


def product(values, matrix):
    return jnp.einsum("...j,jk->...k", values, matrix, precision=lax.Precision.HIGHEST)


def general_light(conc, wet, loading):
    chl = jax.nn.softplus(jnp.einsum("f...,f->...", conc, loading, precision=lax.Precision.HIGHEST))
    levels = chl.shape[-1]
    absorbed, irradiance = light(chl, product(chl, table(levels, "prefix")), level_of(chl.shape))
    return wet * jnp.stack(absorbed), irradiance


def general_tracers(conc, rise, heat, irradiance, wet, matrix, share):
    none = jnp.zeros_like(conc[..., :1])
    top = jnp.concatenate([none, 0.5 * (conc[..., 1:] + conc[..., :-1]) * rise[..., 1:]], axis=-1)
    below = jnp.concatenate([top[..., 1:], none], axis=-1)
    mixed = jnp.einsum("ij,j...->i...", matrix, conc, precision=lax.Precision.HIGHEST)
    growth = uptake_rate * irradiance * saturation(conc[0])
    change = (
        jnp.exp(heating_speed * heat) * mixed
        + share.reshape((-1,) + (1,) * (conc.ndim - 1)) * growth + below - top
    )
    return wet * (conc + step_tracer * change)


def general_ocean(u, v, t, absorb, depth, coriolis):
    levels = t.shape[-1]
    fields = jnp.stack([u, v, t])
    north, south = exchange_rows(fields[:, 0], fields[:, -1])
    east, west = exchange_cols(fields[:, :, 0], fields[:, :, -1])
    tall = jnp.concatenate([south[:, None], fields, north[:, None]], axis=1)
    wide = jnp.concatenate([west[:, :, None], fields, east[:, :, None]], axis=2)
    around = (fields, wide[:, :, 2:], wide[:, :, :-2], tall[:, 2:], tall[:, :-2])
    above = table(levels, "above")
    u, v, t = ([x[f] for x in around] for f in range(3))
    p = [weight_pull_factor * product(x, above) for x in t]
    wet = [wet_of(depth[i], t[0].shape) for i in range(5)]

    def spread(x):
        return sum(wet[i] * (x[i] - x[0]) for i in range(1, 5))

    east = 0.5 * (u[0] + u[1]) * wet[0] * wet[1]
    west = 0.5 * (u[2] + u[0]) * wet[2] * wet[0]
    north = 0.5 * (v[0] + v[3]) * wet[0] * wet[3]
    south = 0.5 * (v[4] + v[0]) * wet[4] * wet[0]
    carry_along = 0.5 * (
        east * (t[0] + t[1]) - west * (t[2] + t[0]) + north * (t[0] + t[3]) - south * (t[4] + t[0])
    )
    zonal = 0.5 * (wet[1] * (p[1] - p[0]) + wet[2] * (p[0] - p[2]))
    merid = 0.5 * (wet[3] * (p[3] - p[0]) + wet[4] * (p[0] - p[4]))
    turn = coriolis[:, None, None]
    rise = -product(east - west + north - south, table(levels, "below"))
    return (
        wet[0] * (u[0] + advance_marine * (turn * v[0] - zonal + viscosity * spread(u) - damping * u[0])),
        wet[0] * (v[0] + advance_marine * (-turn * u[0] - merid + viscosity * spread(v) - damping * v[0])),
        wet[0] * (t[0] + advance_marine * (spreading * spread(t) - carry_along + heat_gain * (absorb[0] + absorb[1]))),
        rise,
    )


def general(linked, u, v, t, tracers, depth, tracer_depth, holder_rank, patch_index, coriolis, matrix, share, loading):
    comp_index = lax.axis_index("comp")
    first = comp_index == 0
    fields, patches, strip, levels = tracers.shape
    half = strip // 2
    indices = jnp.arange(patches, dtype=jnp.int32)
    owner_row = lax.dynamic_index_in_dim(holder_rank, patch_index, 0, keepdims=False)
    inverse_row = jnp.sum(jnp.where(owner_row[:, None] == indices[None], indices[:, None], 0), axis=0)

    def own_half(x):
        return lax.dynamic_slice_in_dim(x, comp_index * half, half, x.ndim - 2)

    partner = swap(linked)
    absorb = jnp.where(first, linked, partner)
    flux = own_half(jnp.where(first, partner, linked))
    conc = own_half(tracers)
    wet = wet_of(tracer_depth, conc.shape[1:])
    irradiance = general_light(conc, wet, loading)[1]
    grid = t.shape
    for _ in range(3):
        u, v, t, rise = general_ocean(u, v, t, absorb.reshape((2,) + grid), depth, coriolis)
        conc = general_tracers(conc, flux[0], flux[1], irradiance, wet, matrix, share)
        absorbed, irradiance = general_light(conc, wet, loading)
        both = own_half(pick(jnp.stack([rise, t]).reshape(2, patches, strip, levels), inverse_row, 1))
        send = jnp.concatenate([both, absorbed])
        back = lax.all_to_all(send, ("py", "px"), split_axis=1, concat_axis=1, tiled=True)
        flux = back[:2]
        mine = pick(back[2:], owner_row, 1)
        other = swap(mine)
        absorb = jnp.where(first, jnp.concatenate([mine, other], 2), jnp.concatenate([other, mine], 2))
    other = swap(flux)
    joined = jnp.where(first, jnp.concatenate([flux, other], 2), jnp.concatenate([other, flux], 2))
    return jnp.where(first, absorb, joined)


def shards(
    current_speeds,
    thermal_anomaly,
    solute_amounts,
    delayed_link_source,
    marine_indicator,
    floor_layer_index,
    holder_rank,
    biota_exchange_matrix,
    photic_absorb_share,
    chroma_loading,
):
    comp_index = lax.axis_index("comp")
    row_index = lax.axis_index("py")
    col_index = lax.axis_index("px")
    rows_mesh = lax.axis_size("py")
    cols_mesh = lax.axis_size("px")
    patches = rows_mesh * cols_mesh
    fields, _, columns, levels = solute_amounts.shape
    strip = columns // patches
    half = strip // 2
    patch_index = row_index * cols_mesh + col_index
    first = comp_index == 0

    linked = delayed_link_source.reshape(2, patches, strip, levels)
    tracers = solute_amounts.reshape(fields, patches, strip, levels)
    u0, v0 = current_speeds[0], current_speeds[1]

    column_depth = marine_indicator * floor_layer_index
    wrapped = jnp.concatenate([column_depth[:, -2:], column_depth, column_depth[:, :2]], axis=1)
    padded = jnp.pad(wrapped, ((2, 2), (0, 0)))
    far = lax.dynamic_slice(padded, (row_index * CY, col_index * CX), (CY + 4, CX + 4))
    local = far[1:-1, 1:-1]
    gap = 4
    near = lax.dynamic_slice_in_dim(far, comp_index * half, half + 4, 1)
    wide_depth = jnp.concatenate(
        [near[:, 2:], jnp.zeros((CY + 4, gap), jnp.int32), near[:, :2]], axis=1
    )[..., None]
    depth = jnp.stack([local[1:-1, 1:-1], local[1:-1, 2:], local[1:-1, :-2], local[2:, 1:-1], local[:-2, 1:-1]])
    depth = depth[..., None]
    def depth_of_tracers(column_depth):
        by_strip = (
            column_depth.reshape(rows_mesh, CY, cols_mesh, CX).transpose(0, 2, 1, 3).reshape(patches, patches, strip)
        )
        here = (holder_rank == patch_index)[:, :, None]
        tracer_depth = jnp.sum(jnp.where(here, by_strip, 0), axis=1)
        return lax.dynamic_slice_in_dim(tracer_depth, comp_index * half, half, 1)[..., None]

    owner_row = lax.dynamic_index_in_dim(holder_rank, patch_index, 0, keepdims=False)
    side_index = comp_index.astype(jnp.int32)[None]
    comp = jnp.concatenate([side_index, owner_row])
    ys = (row_index * CY - 1 + jnp.arange(CY + 2, dtype=jnp.int32)).astype(jnp.float32)
    coriolis = coriolis_scale * (2.0 * (ys + 0.5) / (CY * rows_mesh) - 1.0)

    if half % 8 or strip != CX:
        out = general(
            linked, u0, v0, thermal_anomaly, tracers, depth, depth_of_tracers(column_depth), holder_rank, patch_index, coriolis[1:-1],
            biota_exchange_matrix, photic_absorb_share, chroma_loading,
        )
        return out.reshape(1, 2, 1, columns, levels)

    linked, tracers, current_speeds, thermal_anomaly = (
        in_hbm(x) for x in (linked, tracers, current_speeds, thermal_anomaly)
    )
    sent, *edges = pack(side_index, linked, current_speeds, thermal_anomaly)
    got = swap(sent)
    times = functools.partial(jnp.dot, precision=lax.Precision.HIGHEST)
    unit = (jnp.arange(fields) == 0).astype(jnp.float32)
    chain = [jnp.stack([chroma_loading, unit])]
    for _ in range(3):
        chain.append(times(chain[-1], biota_exchange_matrix))
    weights = jnp.stack([c[0] for c in chain] + [c[1] for c in chain[:3]])

    projected, g = project(side_index, tracers, weights)
    low, high, left, right, first_column = edges
    north, south = exchange_rows(low, high)
    edge = east_column(first_column)
    left, right, projected, g = lax.optimization_barrier((left, right, projected, g))
    projected, g = in_vmem(projected), in_vmem(g)
    outer = shape_of(4, 2, CY + 2, levels)
    [sides] = call(corner_kernel, side_index, (left, right, north, south), [None] * 4, (outer,), (), "corner")
    column_depth, photic_absorb_share, sides = lax.optimization_barrier((column_depth, photic_absorb_share, sides))
    sides = far_columns(sides)
    tracer_depth = depth_of_tracers(column_depth)
    shares = times(weights, photic_absorb_share)
    kept = first_tracer(side_index, projected, g, got, linked, tracer_depth, shares)
    kept, north, south, sides, edge = lax.optimization_barrier((kept, north, south, sides, edge))
    arrived = to_owners(kept)

    [ring] = call(ring_kernel, side_index, (north, south), [None] * 2, (shape_of(2, CX, levels),), (), "ring")
    args = (current_speeds, thermal_anomaly, linked, got, north, south, sides, edge, swap(ring))
    speeds1, wide_t1, t1, r1 = ocean(1, comp, coriolis, args, wide_depth, CY, half)
    r1 = in_hbm(r1)
    speeds2, t2, r2 = ocean(2, comp, coriolis, (speeds1, wide_t1), wide_depth, CY, half)
    arrived, speeds2, t2 = lax.optimization_barrier((arrived, speeds2, t2))
    speeds2, t2, r2 = in_vmem(speeds2), in_vmem(t2), in_hbm(r2)

    depth_half = pl.BlockSpec((5, CY, half, 1), lambda i, c: (0, 0, c[0], 0))
    piece = shape_of(CY, half, levels)
    scratch = (CY, half, levels)
    line = shape_of(3, half, levels)
    side = shape_of(3, CY, levels)

    t2, irr1, *edges = call(
        absorb_kernel, comp, (arrived, t2, speeds2, depth), [HBM, None, None, depth_half],
        (piece, piece, line, line, side, side), [scratch] * 2, "absorb", [pltpu.SemaphoreType.DMA],
    )
    halos2 = exchange_rows(edges[0], edges[1]) + exchange_half_cols(edges[2], edges[3])
    heat, a, b, g = call(
        second_kernel, comp, (arrived, irr1, t1, r1, depth, shares),
        [None] * 4 + [depth_half, SMEM],
        (piece,) * 4, [scratch] * 2, "second",
    )
    [back] = call(
        last_ocean_kernel, comp, (speeds2, t2, *halos2, depth, heat),
        [None] * 6 + [depth_half, None],
        (shape_of(2, patches, 2, half, levels),), [scratch], "last_ocean",
    )
    flux = lax.all_to_all(
        back.reshape(2 * patches, 2, half, levels), ("comp", "py", "px"), split_axis=0, concat_axis=0, tiled=True
    ).reshape(2, patches, 2, half, levels)
    [absorbed] = call(
        third_kernel, comp, (a, b, g, t2, r2, depth, shares),
        [None] * 5 + [depth_half, SMEM], (shape_of(CY, 2, half, levels),), [scratch], "third",
    )
    other = swap(absorbed)
    [out] = call(
        join_kernel, comp, (absorbed, flux, other), [None] * 3, (shape_of(2, patches, strip, levels),), (), "join"
    )
    return out.reshape(1, 2, 1, columns, levels)


def solution(mesh):
    placed = (
        P(None, "py", "px", None),
        P("py", "px", None),
        P(None, ("py", "px"), None, None),
        P("comp", None, ("py", "px"), None, None),
        P(),
        P(),
        P(),
        P(),
        P(),
        P(),
    )
    return jax.shard_map(
        shards,
        mesh=mesh,
        in_specs=placed,
        out_specs=P("comp", None, ("py", "px"), None, None),
        check_vma=False,
    )
```

```python
import functools

import jax
import jax.numpy as jnp
from jax import lax
from jax.experimental import pallas as pl
from jax.experimental.pallas import tpu as pltpu
from jax.sharding import PartitionSpec as P

advance_marine = 0.1
spreading = 0.1
viscosity = 0.1
damping = 0.05
heat_gain = 0.2
weight_pull_factor = 0.05
coriolis_scale = 1.0
step_tracer = 0.1
heating_speed = 0.06
uptake_rate = 0.01
water_absorb = (0.02, 0.003)
pigment_absorb = (0.03, 0.004)
surface_light = (40.0, 60.0)
CY = 16
CX = 32
KEPT = (0, 1, 2, 4, 5)
SMEM = pl.BlockSpec(memory_space=pltpu.SMEM)
PARAMS = pltpu.CompilerParams(vmem_limit_bytes=28 * 1024 * 1024)
HBM = pl.BlockSpec(memory_space=pltpu.HBM)
STREAMED = pltpu.CompilerParams(vmem_limit_bytes=60 * 1024 * 1024)


def whole(array):
    zeros = (0,) * len(array.shape)
    return pl.BlockSpec(array.shape, lambda i, c: zeros)


def shape_of(*dims):
    return jax.ShapeDtypeStruct(dims, jnp.float32)


def level_matrix(levels, pattern):
    row = lax.broadcasted_iota(jnp.int32, (levels, levels), 0)
    col = lax.broadcasted_iota(jnp.int32, (levels, levels), 1)
    if pattern == "above":
        m = jnp.where(row < col, 1.0, jnp.where(row == col, 0.5, 0.0))
    elif pattern == "below":
        m = jnp.where(row >= col, 1.0, 0.0)
    else:
        m = jnp.where(row < col, 1.0, 0.0)
    return m.astype(jnp.bfloat16)


def level_sums(x, matrix):
    hi = x.astype(jnp.bfloat16)
    rest = x - hi.astype(jnp.float32)
    mid = rest.astype(jnp.bfloat16)
    low = (rest - mid.astype(jnp.float32)).astype(jnp.bfloat16)
    dot = functools.partial(jnp.dot, preferred_element_type=jnp.float32)
    return dot(hi, matrix) + dot(mid, matrix) + dot(low, matrix)


def softplus(x):
    return jnp.maximum(x, 0.0) + jnp.log1p(jnp.exp(-jnp.abs(x)))


def light(chl, sums, level):
    absorbed, irradiance = [], None
    for water, pigment, surface in zip(water_absorb, pigment_absorb, surface_light):
        fade = jnp.exp(-0.5 * (water + pigment * chl))
        intensity = surface * jnp.exp(-(water * level + pigment * sums))
        absorbed.append(intensity * (1.0 - fade * fade))
        part = intensity * fade
        irradiance = part if irradiance is None else irradiance + part
    return absorbed, irradiance


def saturation(n):
    return n * n / (1.0 + n * n)


def transport(rise_half, y):
    top = rise_half * (y + pltpu.roll(y, 1, 1))
    return pltpu.roll(top, top.shape[1] - 1, 1) - top


def wet_of(depth, shape):
    level = lax.broadcasted_iota(jnp.int32, shape, len(shape) - 1)
    return jnp.where(level < depth, 1.0, 0.0)


def level_of(shape):
    return lax.broadcasted_iota(jnp.int32, shape, len(shape) - 1).astype(jnp.float32)


def half_rise(rise):
    k = lax.broadcasted_iota(jnp.int32, rise.shape, 1)
    return jnp.where(k > 0, 0.5 * rise, 0.0)


def project_kernel(sc, x_hbm, w_ref, y_ref, g_ref, x_ref, chl_ref, sems):
    pieces, fields, block, cols, levels = x_ref.shape
    own = pl.ds(pl.multiple_of(sc[0] * cols, cols), cols)
    copies = [
        pltpu.make_async_copy(x_hbm.at[:, pl.ds(i * block, block), own], x_ref.at[i], sems.at[i]) for i in range(pieces)
    ]
    for copy in copies:
        copy.start()
    mixed = [k for k in range(y_ref.shape[0]) if k != 4]
    prefix = level_matrix(levels, "prefix")
    flat = (block * cols, levels)
    for i, copy in enumerate(copies):
        copy.wait()

        def one(q, carry):
            at = i * block + q
            value = x_ref[i, 0, q]
            y_ref[4, at] = value
            totals = [w_ref[k, 0] * value for k in mixed]
            for j in range(1, fields):
                value = x_ref[i, j, q]
                totals = [t + w_ref[k, j] * value for t, k in zip(totals, mixed)]
            for k, total in zip(mixed, totals):
                y_ref[k, at] = total
            chl_ref[q] = softplus(totals[0])
            return carry

        lax.fori_loop(0, block, one, 0)
        chl = chl_ref[...].reshape(flat)
        _, irradiance = light(chl, level_sums(chl, prefix), level_of(flat))
        n = x_ref[i, 0].reshape(flat)
        g_ref[i * block : (i + 1) * block] = (uptake_rate * irradiance * saturation(n)).reshape(block, cols, levels)


def project(comp, tracers, weights):
    fields, patches, strip, levels = tracers.shape
    half = strip // 2
    pieces = 4
    block = patches // pieces
    outs = (shape_of(weights.shape[0], patches, half, levels), shape_of(patches, half, levels))
    return pl.pallas_call(
        project_kernel,
        grid_spec=pltpu.PrefetchScalarGridSpec(
            num_scalar_prefetch=1,
            grid=(1,),
            in_specs=[HBM, SMEM],
            out_specs=[whole(o) for o in outs],
            scratch_shapes=[
                pltpu.VMEM((pieces, fields, block, half, levels), jnp.float32),
                pltpu.VMEM((block, half, levels), jnp.float32),
                pltpu.SemaphoreType.DMA((pieces,)),
            ],
        ),
        out_shape=outs,
        compiler_params=PARAMS,
        name="project",
    )(comp, tracers, weights)


def first_tracer_kernel(sc, y_ref, g_ref, got_ref, own_ref, depth_ref, share_ref, out_ref):
    patches, cols, levels = g_ref.shape
    first = sc[0] == 0

    def one(q, carry):
        rise = jnp.where(first, got_ref[0, q], own_ref[0, q])
        heat = jnp.where(first, got_ref[1, q], own_ref[1, q])
        warm = jnp.exp(heating_speed * heat)
        wet = wet_of(depth_ref[q], (cols, levels))
        up = half_rise(rise)
        g = g_ref[q]
        for place, k in enumerate(KEPT):
            y = y_ref[k, q]
            change = warm * y_ref[k + 1, q] + share_ref[k] * g + transport(up, y)
            out_ref[q, place] = wet * (y + step_tracer * change)
        return carry

    lax.fori_loop(0, patches, one, 0, unroll=2)


def half_spec(lead, cols, levels):
    zeros = (0,) * len(lead)
    return pl.BlockSpec(lead + (cols, levels), lambda i, c: zeros + (c[0], 0))


def first_tracer(comp, projected, g, got, linked, depth, shares):
    kinds, patches, half, levels = projected.shape
    block = 4
    return pl.pallas_call(
        first_tracer_kernel,
        grid_spec=pltpu.PrefetchScalarGridSpec(
            num_scalar_prefetch=1,
            grid=(patches // block,),
            in_specs=[
                pl.BlockSpec((kinds, block, half, levels), lambda i, c: (0, i, 0, 0)),
                pl.BlockSpec((block, half, levels), lambda i, c: (i, 0, 0)),
                pl.BlockSpec((2, block, half, levels), lambda i, c: (0, i, 0, 0)),
                pl.BlockSpec((2, block, half, levels), lambda i, c: (0, i, c[0], 0)),
                pl.BlockSpec((block, half, 1), lambda i, c: (i, 0, 0)),
                SMEM,
            ],
            out_specs=pl.BlockSpec((block, len(KEPT), half, levels), lambda i, c: (i, 0, 0, 0)),
        ),
        out_shape=shape_of(patches, len(KEPT), half, levels),
        compiler_params=PARAMS,
        name="first_tracer",
    )(comp, projected, g, got, linked, depth, shares)


def pack_kernel(sc, linked_ref, row0_ref, row1_ref, col0_ref, col1_ref, t0_ref, t1_ref, tc0_ref, tc1_ref,
                sent_ref, low_ref, high_ref, left_ref, right_ref, first_ref):
    _, strips, strip, levels = linked_ref.shape
    half = strip // 2

    @pl.when(sc[0] == 0)
    def _():
        for part in range(2):
            cols = slice(part * half, (part + 1) * half)
            sent_ref[part] = linked_ref[0, :, cols] + linked_ref[1, :, cols]

    @pl.when(sc[0] != 0)
    def _():
        sent_ref[...] = linked_ref[:, :, :half]

    last = col1_ref.shape[2]
    tall = strips - 2
    for i in range(2):
        for f in range(2):
            left_ref[f, i] = col0_ref[f, :, i]
            right_ref[f, i] = col1_ref[f, :, last - 2 + i]
        left_ref[2, i] = tc0_ref[:, i]
        right_ref[2, i] = tc1_ref[:, last - 2 + i]
        left_ref[3, i] = linked_ref[0, :, i] + linked_ref[1, :, i]
        right_ref[3, i] = linked_ref[0, :, strip - 2 + i] + linked_ref[1, :, strip - 2 + i]
    first_ref[...] = left_ref[3, 0]
    for f in range(2):
        low_ref[f] = row0_ref[f]
        high_ref[f] = row1_ref[f]
    low_ref[2] = t0_ref[...]
    high_ref[2] = t1_ref[...]
    low_ref[3] = linked_ref[0, :2] + linked_ref[1, :2]
    high_ref[3] = linked_ref[0, tall:] + linked_ref[1, tall:]


def corner_kernel(sc, left_ref, right_ref, north_ref, south_ref, out_ref):
    rows = left_ref.shape[2]
    cols = north_ref.shape[2]

    def fill(source, at):
        for f in range(source.shape[0]):
            for i in range(2):
                out_ref[f, i, :rows] = source[f, i]
                out_ref[f, i, rows : rows + 1] = south_ref[f, 1, at + i : at + i + 1]
                out_ref[f, i, rows + 1 :] = north_ref[f, 0, at + i : at + i + 1]

    @pl.when(sc[0] == 0)
    def _():
        fill(right_ref, cols - 2)

    @pl.when(sc[0] != 0)
    def _():
        fill(left_ref, 0)


def ring_kernel(sc, north_ref, south_ref, ring_ref):
    ring_ref[0] = south_ref[3, 1]
    ring_ref[1] = north_ref[3, 0]


def pack(comp, linked, speeds, heat):
    _, strips, strip, levels = linked.shape
    rows, cols, _ = heat.shape
    outs = (
        shape_of(2, strips, strip // 2, levels), shape_of(4, 2, cols, levels), shape_of(4, 2, cols, levels),
        shape_of(4, 2, rows, levels), shape_of(4, 2, rows, levels), shape_of(rows, levels),
    )
    edge = min(8, cols)
    return pl.pallas_call(
        pack_kernel,
        grid_spec=pltpu.PrefetchScalarGridSpec(
            num_scalar_prefetch=1,
            grid=(1,),
            in_specs=[
                whole(linked),
                pl.BlockSpec((2, 2, cols, levels), lambda i, c: (0, 0, 0, 0)),
                pl.BlockSpec((2, 2, cols, levels), lambda i, c: (0, rows // 2 - 1, 0, 0)),
                pl.BlockSpec((2, rows, edge, levels), lambda i, c: (0, 0, 0, 0)),
                pl.BlockSpec((2, rows, edge, levels), lambda i, c: (0, 0, cols // edge - 1, 0)),
                pl.BlockSpec((2, cols, levels), lambda i, c: (0, 0, 0)),
                pl.BlockSpec((2, cols, levels), lambda i, c: (rows // 2 - 1, 0, 0)),
                pl.BlockSpec((rows, edge, levels), lambda i, c: (0, 0, 0)),
                pl.BlockSpec((rows, edge, levels), lambda i, c: (0, cols // edge - 1, 0)),
            ],
            out_specs=[whole(o) for o in outs],
        ),
        out_shape=outs,
        compiler_params=STREAMED,
        name="pack",
    )(comp, linked, speeds, speeds, speeds, speeds, heat, heat, heat, heat)


def wide_rows(sc, speed_hbm, heat_hbm, linked_hbm, got_ref, north_ref, south_ref, side_ref, edge_ref, ring_ref,
              x_ref, near_ref, absorb_ref, linked_ref, sems):
    rows, cols, levels = heat_hbm.shape
    half = cols // 2
    comp = sc[0]
    first = comp == 0
    width = x_ref.shape[2]
    rim = width - half
    own = pl.ds(pl.multiple_of(comp * half, half), half)
    near = pl.ds(pl.multiple_of(half - rim * comp, 8), rim)
    copies = [pltpu.make_async_copy(linked_hbm, linked_ref, sems.at[0])]
    for f, source in enumerate((speed_hbm.at[0], speed_hbm.at[1], heat_hbm)):
        copies.append(
            pltpu.make_async_copy(source.at[:, own], x_ref.at[f, pl.ds(2, rows), pl.ds(0, half)], sems.at[1 + f])
        )
        copies.append(pltpu.make_async_copy(source.at[:, near], near_ref.at[f], sems.at[4 + f]))
    for copy in copies:
        copy.start()
    place = lax.broadcasted_iota(jnp.int32, (rim, levels), 0)
    none = jnp.zeros((rim, levels), jnp.float32)
    far_place = (1 - comp) * (rim - 2)
    for copy in copies:
        copy.wait()
    for f in range(3):
        x_ref[f, :2, :half] = south_ref[f, :, own]
        x_ref[f, rows + 2 :, :half] = north_ref[f, :, own]
        x_ref[f, 0, half:] = none
        x_ref[f, rows + 3, half:] = none
        for o in range(rows + 2):
            if o == 0:
                r, cells = rows, south_ref[f, 1, near]
            elif o == rows + 1:
                r, cells = rows + 1, north_ref[f, 0, near]
            else:
                r, cells = o - 1, near_ref[f, o - 1]
            for i in range(2):
                cells = jnp.where(place == far_place + i, side_ref[f, i, r : r + 1], cells)
            x_ref[f, o + 1, half:] = cells
    for o, side in ((0, 0), (rows + 1, 1)):
        here = (south_ref[3, 1] if side == 0 else north_ref[3, 0])[:half]
        absorb_ref[o, :half] = jnp.where(first, here, ring_ref[side, half:])
        absorb_ref[o, half:] = none
    for y in range(rows):
        both = linked_ref[0, y] + linked_ref[1, y]
        absorb_ref[y + 1, :half] = jnp.where(first, both[:half], got_ref[1, y])
        cells = jnp.where(first, both[half : half + rim], got_ref[0, y, half - rim :])
        far = jnp.where(first, side_ref[3, 1, y : y + 1], edge_ref[y : y + 1])
        absorb_ref[y + 1, half:] = jnp.where(place == (1 - comp) * (rim - 1), far, cells)


def ocean_kernel(advance, sc, coriolis_ref, *refs):
    if advance == 1:
        *sources, depth_ref, next_ref, tn_ref, inner_ref, rise_ref, x_ref, near_ref, absorb_ref = refs[:-4]
        linked_ref, sems, p_ref, div_ref = refs[-4:]
        wide_rows(sc, *sources, x_ref, near_ref, absorb_ref, linked_ref, sems)
        fields = [x_ref.at[f] for f in range(3)]
    else:
        speed_ref, t_ref, depth_ref, next_ref, tn_ref, rise_ref, p_ref, div_ref = refs
        fields = [speed_ref.at[0], speed_ref.at[1], t_ref]
    tall, width, levels = p_ref.shape
    rows, cols = rise_ref.shape[:2]
    out_width = tn_ref.shape[1]
    p_ref[...] = (
        weight_pull_factor * level_sums(fields[2][...].reshape(tall * width, levels), level_matrix(levels, "above"))
    ).reshape(tall, width, levels)
    lanes = min(128, levels)

    def piece(o, lane):
        part = slice(lane, lane + lanes)
        level = lane + lax.broadcasted_iota(jnp.int32, (width, lanes), 1)

        def beside(x):
            return pltpu.roll(x, width - 1, 0), pltpu.roll(x, 1, 0)

        def field(ref):
            x = ref[o + 1, :, part]
            return (x, *beside(x), ref[o + 2, :, part], ref[o, :, part])

        def wet_at(d):
            return jnp.where(level < depth_ref[d], 1.0, 0.0)

        here = wet_at(o + advance)
        wet = (here, *beside(here), wet_at(o + advance + 1), wet_at(o + advance - 1))
        u, v, t, p = (field(ref) for ref in (*fields, p_ref))
        own = 0.5 * wet[0]
        east = (u[0] + u[1]) * (own * wet[1])
        west = (u[2] + u[0]) * (own * wet[2])
        north = (v[0] + v[3]) * (own * wet[3])
        south = (v[4] + v[0]) * (own * wet[4])
        div_ref[o, :, part] = east - west + north - south
        wets = wet[1] + wet[2] + wet[3] + wet[4]

        def spread(x):
            return wet[1] * x[1] + wet[2] * x[2] + wet[3] * x[3] + wet[4] * x[4] - wets * x[0]

        carry_along = 0.5 * (
            east * (t[0] + t[1]) - west * (t[2] + t[0]) + north * (t[0] + t[3]) - south * (t[4] + t[0])
        )
        change = spreading * spread(t) - carry_along
        if advance == 1:
            change = change + heat_gain * absorb_ref[o, :, part]
        zonal = 0.5 * (wet[1] * (p[1] - p[0]) + wet[2] * (p[0] - p[2]))
        merid = 0.5 * (wet[3] * (p[3] - p[0]) + wet[4] * (p[0] - p[4]))
        turn = coriolis_ref[o + advance - 1]
        results = (
            wet[0] * (u[0] + advance_marine * (turn * v[0] - zonal + viscosity * spread(u) - damping * u[0])),
            wet[0] * (v[0] + advance_marine * (-turn * u[0] - merid + viscosity * spread(v) - damping * v[0])),
            wet[0] * (t[0] + advance_marine * change),
        )
        for ref, value in zip((next_ref.at[0], next_ref.at[1], tn_ref), results):
            ref[o, :, part] = value[:out_width]

    def row(o, carry):
        for lane in range(0, levels, lanes):
            piece(o, lane)
        return carry

    lax.fori_loop(0, tall - 2, row, 0)
    rim = (tall - 2 - rows) // 2
    div = div_ref[rim : rim + rows, :cols].reshape(rows * cols, levels)
    rise_ref[...] = -level_sums(div, level_matrix(levels, "below")).reshape(rows, cols, levels)
    if advance == 1:
        inner_ref[...] = tn_ref[rim : rim + rows, :cols]


def ocean(advance, comp, coriolis, args, depth, rows, cols):
    width, levels = depth.shape[1], args[1].shape[-1]
    patch = shape_of(rows, cols, levels)
    if advance == 1:
        tall = rows + 4
        outs = (shape_of(2, rows + 2, width, levels), shape_of(rows + 2, width, levels), patch, patch)
        scratch = [
            pltpu.VMEM((3, tall, width, levels), jnp.float32),
            pltpu.VMEM((3, rows, width - cols, levels), jnp.float32),
            pltpu.VMEM((rows + 2, width, levels), jnp.float32),
            pltpu.VMEM(args[2].shape, jnp.float32),
            pltpu.SemaphoreType.DMA((7,)),
        ]
    else:
        tall = rows + 2
        outs = (shape_of(2, rows, cols, levels), patch, patch)
        scratch = []
    scratch += [
        pltpu.VMEM((tall, width, levels), jnp.float32), pltpu.VMEM((tall - 2, width, levels), jnp.float32)
    ]
    args = [coriolis, *args, depth]
    own_copies = 3 if advance == 1 else 0
    return pl.pallas_call(
        functools.partial(ocean_kernel, advance),
        grid_spec=pltpu.PrefetchScalarGridSpec(
            num_scalar_prefetch=1,
            grid=(1,),
            in_specs=[SMEM] + [HBM] * own_copies + [whole(x) for x in args[1 + own_copies :]],
            out_specs=[whole(o) for o in outs],
            scratch_shapes=scratch,
        ),
        out_shape=outs,
        compiler_params=PARAMS,
        name=f"ocean{advance}",
    )(comp, *args)


def absorb_kernel(
    sc, y_hbm, t_ref, speed_ref, depth_ref, t2_ref, irr_ref, row0_ref, row1_ref, col0_ref, col1_ref, chl_ref, y_ref, sem
):
    rows, cols, levels = t_ref.shape
    flat = (rows * cols, levels)
    copy = pltpu.make_async_copy(y_hbm.at[:, 0], y_ref, sem)
    copy.start()
    copy.wait()

    def gather(s, carry):
        chl_ref[s] = softplus(y_ref[sc[1 + s]])
        return carry

    lax.fori_loop(0, rows, gather, 0, unroll=2)
    chl = chl_ref[...].reshape(flat)
    sums = level_sums(chl, level_matrix(levels, "prefix"))
    absorbed, irradiance = light(chl, sums, level_of(flat))
    wet = wet_of(depth_ref[0], t_ref.shape)
    both = (absorbed[0] + absorbed[1]).reshape(t_ref.shape)
    t2_ref[...] = t_ref[...] + advance_marine * heat_gain * (wet * both)
    irr_ref[...] = irradiance.reshape(t_ref.shape)
    for f, ref in enumerate((speed_ref.at[0], speed_ref.at[1], t2_ref)):
        row0_ref[f] = ref[0]
        row1_ref[f] = ref[rows - 1]
        for y in range(rows):
            col0_ref[f, pl.ds(y, 1)] = ref[y, :1]
            col1_ref[f, pl.ds(y, 1)] = ref[y, cols - 1 :]


def second_kernel(
    sc, y_ref, irr_ref, t1_ref, r1_ref, depth_ref, share_ref, heat_ref, a_ref, b_ref, g_ref, n_ref, chl_ref
):
    patches, _, cols, levels = y_ref.shape
    flat = (patches * cols, levels)
    whole = (patches, cols, levels)

    def one(s, carry):
        owner = sc[1 + s]
        wet = wet_of(depth_ref[0, s], (cols, levels))
        warm = jnp.exp(heating_speed * t1_ref[s])
        up = half_rise(r1_ref[s])
        y = [y_ref[owner, i] for i in range(len(KEPT))]
        g = uptake_rate * irr_ref[s] * saturation(y[3])
        for ref, i, k in ((a_ref, 0, 0), (b_ref, 1, 1), (n_ref, 3, 4)):
            change = warm * y[i + 1] + share_ref[k] * g + transport(up, y[i])
            ref[s] = wet * (y[i] + step_tracer * change)
        chl_ref[s] = softplus(a_ref[s])
        return carry

    lax.fori_loop(0, patches, one, 0, unroll=4)
    chl = chl_ref[...].reshape(flat)
    absorbed, irradiance = light(chl, level_sums(chl, level_matrix(levels, "prefix")), level_of(flat))
    wet = wet_of(depth_ref[0], whole)
    heat_ref[...] = advance_marine * heat_gain * (wet * (absorbed[0] + absorbed[1]).reshape(whole))
    g_ref[...] = uptake_rate * irradiance.reshape(whole) * saturation(n_ref[...])


def third_kernel(sc, a_ref, b_ref, g_ref, t2_ref, r2_ref, depth_ref, share_ref, band_ref, chl_ref):
    patches, cols, levels = a_ref.shape
    flat = (patches * cols, levels)
    whole = (patches, cols, levels)

    def one(s, carry):
        wet = wet_of(depth_ref[0, s], (cols, levels))
        warm = jnp.exp(heating_speed * t2_ref[s])
        a = a_ref[s]
        change = warm * b_ref[s] + share_ref[0] * g_ref[s] + transport(half_rise(r2_ref[s]), a)
        chl_ref[s] = softplus(wet * (a + step_tracer * change))
        return carry

    lax.fori_loop(0, patches, one, 0, unroll=4)
    chl = chl_ref[...].reshape(flat)
    absorbed, _ = light(chl, level_sums(chl, level_matrix(levels, "prefix")), level_of(flat))
    wet = wet_of(depth_ref[0], whole)
    for band in range(2):
        band_ref[:, band] = wet * absorbed[band].reshape(whole)


def last_ocean_kernel(
    sc, speed_ref, t_ref, north_ref, south_ref, east_ref, west_ref, depth_ref, heat_ref, out_ref, div_ref
):
    rows, cols, levels = t_ref.shape
    place = lax.broadcasted_iota(jnp.int32, (cols, levels), 0)
    sources = (speed_ref.at[0], speed_ref.at[1], t_ref)
    for y in range(rows):
        wet = [wet_of(depth_ref[i, y], (cols, levels)) for i in range(5)]

        def east_of(f):
            return jnp.where(place == cols - 1, east_ref[f, pl.ds(y, 1)], pltpu.roll(sources[f][y], cols - 1, 0))

        def west_of(f):
            return jnp.where(place == 0, west_ref[f, pl.ds(y, 1)], pltpu.roll(sources[f][y], 1, 0))

        def north_of(f):
            return sources[f][y + 1] if y < rows - 1 else north_ref[f]

        def south_of(f):
            return sources[f][y - 1] if y > 0 else south_ref[f]

        u, v, t = (ref[y] for ref in sources)
        own = 0.5 * wet[0]
        east = (u + east_of(0)) * (own * wet[1])
        west = (west_of(0) + u) * (own * wet[2])
        north = (v + north_of(1)) * (own * wet[3])
        south = (south_of(1) + v) * (own * wet[4])
        div_ref[y] = east - west + north - south
        e, w, n, s = east_of(2), west_of(2), north_of(2), south_of(2)
        spread = wet[1] * (e - t) + wet[2] * (w - t) + wet[3] * (n - t) + wet[4] * (s - t)
        carry_along = 0.5 * (east * (t + e) - west * (w + t) + north * (t + n) - south * (s + t))
        change = spreading * spread - carry_along
        out_ref[1, sc[1 + y], 1] = wet[0] * (t + advance_marine * change) + heat_ref[y]
    sums = level_sums(div_ref[...].reshape(rows * cols, levels), level_matrix(levels, "below"))
    div_ref[...] = -sums.reshape(rows, cols, levels)
    for y in range(rows):
        out_ref[1, sc[1 + y], 0] = div_ref[y]
    out_ref[0] = jnp.zeros(out_ref.shape[1:], jnp.float32)


def join_kernel(sc, absorbed_ref, flux_ref, other_ref, out_ref):
    patches, _, half, levels = absorbed_ref.shape

    @pl.when(sc[0] == 0)
    def _():
        for s in range(patches):
            for f in range(2):
                out_ref[f, s, :half] = absorbed_ref[s, f]
                out_ref[f, s, half:] = other_ref[s, f]

    @pl.when(sc[0] != 0)
    def _():
        for s in range(patches):
            for f in range(2):
                for part in range(2):
                    out_ref[f, s, part * half : (part + 1) * half] = flux_ref[part, s, f]


def call(kernel, comp, args, specs, outs, scratch=(), name=None, sems=()):
    return pl.pallas_call(
        kernel,
        grid_spec=pltpu.PrefetchScalarGridSpec(
            num_scalar_prefetch=1,
            grid=(1,),
            in_specs=[spec or whole(a) for spec, a in zip(specs, args)],
            out_specs=[whole(o) for o in outs],
            scratch_shapes=[pltpu.VMEM(s, jnp.float32) for s in scratch] + list(sems),
        ),
        out_shape=outs,
        compiler_params=PARAMS,
        name=name,
    )(comp, *args)


def exchange_rows(low, high):
    count = lax.axis_size("py")
    north = lax.ppermute(low, "py", [((i + 1) % count, i) for i in range(count)])
    south = lax.ppermute(high, "py", [(i, (i + 1) % count) for i in range(count)])
    return north, south


def exchange_cols(low, high):
    count = lax.axis_size("px")
    east = lax.ppermute(low, "px", [((i + 1) % count, i) for i in range(count)])
    west = lax.ppermute(high, "px", [(i, (i + 1) % count) for i in range(count)])
    return east, west


def far_columns(block):
    count = lax.axis_size("px")
    east = [(i, (i + 1) % count) for i in range(count)]
    west = [(count + (i + 1) % count, count + i) for i in range(count)]
    return lax.ppermute(block, ("comp", "px"), east + west)


def east_column(block):
    count = lax.axis_size("px")
    return lax.ppermute(block, ("comp", "px"), [((i + 1) % count, count + i) for i in range(count)])


def exchange_half_cols(low, high):
    count = lax.axis_size("px")
    line = [(h % 2) * count + h // 2 for h in range(2 * count)]
    ahead = [(line[h], line[(h + 1) % len(line)]) for h in range(len(line))]
    east = lax.ppermute(low, ("comp", "px"), [(b, a) for a, b in ahead])
    west = lax.ppermute(high, ("comp", "px"), ahead)
    return east, west


def in_hbm(x):
    return pltpu.with_memory_space_constraint(x, pltpu.HBM)


def in_vmem(x):
    return pltpu.with_memory_space_constraint(x, pltpu.VMEM)


def to_owners(blocks):
    return lax.all_to_all(blocks, ("py", "px"), split_axis=0, concat_axis=0, tiled=True)


def swap(block):
    return lax.ppermute(block, "comp", [(0, 1), (1, 0)])


def pick(blocks, order, axis):
    return jnp.stack(
        [lax.dynamic_index_in_dim(blocks, order[k], axis, keepdims=False) for k in range(order.shape[0])], axis
    )


def table(levels, pattern):
    return level_matrix(levels, pattern).astype(jnp.float32)


def product(values, matrix):
    return jnp.einsum("...j,jk->...k", values, matrix, precision=lax.Precision.HIGHEST)


def general_light(conc, wet, loading):
    chl = jax.nn.softplus(jnp.einsum("f...,f->...", conc, loading, precision=lax.Precision.HIGHEST))
    levels = chl.shape[-1]
    absorbed, irradiance = light(chl, product(chl, table(levels, "prefix")), level_of(chl.shape))
    return wet * jnp.stack(absorbed), irradiance


def general_tracers(conc, rise, heat, irradiance, wet, matrix, share):
    none = jnp.zeros_like(conc[..., :1])
    top = jnp.concatenate([none, 0.5 * (conc[..., 1:] + conc[..., :-1]) * rise[..., 1:]], axis=-1)
    below = jnp.concatenate([top[..., 1:], none], axis=-1)
    mixed = jnp.einsum("ij,j...->i...", matrix, conc, precision=lax.Precision.HIGHEST)
    growth = uptake_rate * irradiance * saturation(conc[0])
    change = (
        jnp.exp(heating_speed * heat) * mixed
        + share.reshape((-1,) + (1,) * (conc.ndim - 1)) * growth + below - top
    )
    return wet * (conc + step_tracer * change)


def general_ocean(u, v, t, absorb, depth, coriolis):
    levels = t.shape[-1]
    fields = jnp.stack([u, v, t])
    north, south = exchange_rows(fields[:, 0], fields[:, -1])
    east, west = exchange_cols(fields[:, :, 0], fields[:, :, -1])
    tall = jnp.concatenate([south[:, None], fields, north[:, None]], axis=1)
    wide = jnp.concatenate([west[:, :, None], fields, east[:, :, None]], axis=2)
    around = (fields, wide[:, :, 2:], wide[:, :, :-2], tall[:, 2:], tall[:, :-2])
    above = table(levels, "above")
    u, v, t = ([x[f] for x in around] for f in range(3))
    p = [weight_pull_factor * product(x, above) for x in t]
    wet = [wet_of(depth[i], t[0].shape) for i in range(5)]

    def spread(x):
        return sum(wet[i] * (x[i] - x[0]) for i in range(1, 5))

    east = 0.5 * (u[0] + u[1]) * wet[0] * wet[1]
    west = 0.5 * (u[2] + u[0]) * wet[2] * wet[0]
    north = 0.5 * (v[0] + v[3]) * wet[0] * wet[3]
    south = 0.5 * (v[4] + v[0]) * wet[4] * wet[0]
    carry_along = 0.5 * (
        east * (t[0] + t[1]) - west * (t[2] + t[0]) + north * (t[0] + t[3]) - south * (t[4] + t[0])
    )
    zonal = 0.5 * (wet[1] * (p[1] - p[0]) + wet[2] * (p[0] - p[2]))
    merid = 0.5 * (wet[3] * (p[3] - p[0]) + wet[4] * (p[0] - p[4]))
    turn = coriolis[:, None, None]
    rise = -product(east - west + north - south, table(levels, "below"))
    return (
        wet[0] * (u[0] + advance_marine * (turn * v[0] - zonal + viscosity * spread(u) - damping * u[0])),
        wet[0] * (v[0] + advance_marine * (-turn * u[0] - merid + viscosity * spread(v) - damping * v[0])),
        wet[0] * (t[0] + advance_marine * (spreading * spread(t) - carry_along + heat_gain * (absorb[0] + absorb[1]))),
        rise,
    )


def general(linked, u, v, t, tracers, depth, tracer_depth, holder_rank, patch_index, coriolis, matrix, share, loading):
    comp_index = lax.axis_index("comp")
    first = comp_index == 0
    fields, patches, strip, levels = tracers.shape
    half = strip // 2
    indices = jnp.arange(patches, dtype=jnp.int32)
    owner_row = lax.dynamic_index_in_dim(holder_rank, patch_index, 0, keepdims=False)
    inverse_row = jnp.sum(jnp.where(owner_row[:, None] == indices[None], indices[:, None], 0), axis=0)

    def own_half(x):
        return lax.dynamic_slice_in_dim(x, comp_index * half, half, x.ndim - 2)

    partner = swap(linked)
    absorb = jnp.where(first, linked, partner)
    flux = own_half(jnp.where(first, partner, linked))
    conc = own_half(tracers)
    wet = wet_of(tracer_depth, conc.shape[1:])
    irradiance = general_light(conc, wet, loading)[1]
    grid = t.shape
    for _ in range(3):
        u, v, t, rise = general_ocean(u, v, t, absorb.reshape((2,) + grid), depth, coriolis)
        conc = general_tracers(conc, flux[0], flux[1], irradiance, wet, matrix, share)
        absorbed, irradiance = general_light(conc, wet, loading)
        both = own_half(pick(jnp.stack([rise, t]).reshape(2, patches, strip, levels), inverse_row, 1))
        send = jnp.concatenate([both, absorbed])
        back = lax.all_to_all(send, ("py", "px"), split_axis=1, concat_axis=1, tiled=True)
        flux = back[:2]
        mine = pick(back[2:], owner_row, 1)
        other = swap(mine)
        absorb = jnp.where(first, jnp.concatenate([mine, other], 2), jnp.concatenate([other, mine], 2))
    other = swap(flux)
    joined = jnp.where(first, jnp.concatenate([flux, other], 2), jnp.concatenate([other, flux], 2))
    return jnp.where(first, absorb, joined)


def shards(
    current_speeds,
    thermal_anomaly,
    solute_amounts,
    delayed_link_source,
    marine_indicator,
    floor_layer_index,
    holder_rank,
    biota_exchange_matrix,
    photic_absorb_share,
    chroma_loading,
):
    comp_index = lax.axis_index("comp")
    row_index = lax.axis_index("py")
    col_index = lax.axis_index("px")
    rows_mesh = lax.axis_size("py")
    cols_mesh = lax.axis_size("px")
    patches = rows_mesh * cols_mesh
    fields, _, columns, levels = solute_amounts.shape
    strip = columns // patches
    half = strip // 2
    patch_index = row_index * cols_mesh + col_index
    first = comp_index == 0

    linked = delayed_link_source.reshape(2, patches, strip, levels)
    tracers = solute_amounts.reshape(fields, patches, strip, levels)
    u0, v0 = current_speeds[0], current_speeds[1]

    column_depth = marine_indicator * floor_layer_index
    wrapped = jnp.concatenate([column_depth[:, -2:], column_depth, column_depth[:, :2]], axis=1)
    padded = jnp.pad(wrapped, ((2, 2), (0, 0)))
    far = lax.dynamic_slice(padded, (row_index * CY, col_index * CX), (CY + 4, CX + 4))
    local = far[1:-1, 1:-1]
    gap = 4
    near = lax.dynamic_slice_in_dim(far, comp_index * half, half + 4, 1)
    wide_depth = jnp.concatenate(
        [near[:, 2:], jnp.zeros((CY + 4, gap), jnp.int32), near[:, :2]], axis=1
    )[..., None]
    depth = jnp.stack([local[1:-1, 1:-1], local[1:-1, 2:], local[1:-1, :-2], local[2:, 1:-1], local[:-2, 1:-1]])
    depth = depth[..., None]
    def depth_of_tracers(column_depth):
        by_strip = (
            column_depth.reshape(rows_mesh, CY, cols_mesh, CX).transpose(0, 2, 1, 3).reshape(patches, patches, strip)
        )
        here = (holder_rank == patch_index)[:, :, None]
        tracer_depth = jnp.sum(jnp.where(here, by_strip, 0), axis=1)
        return lax.dynamic_slice_in_dim(tracer_depth, comp_index * half, half, 1)[..., None]

    owner_row = lax.dynamic_index_in_dim(holder_rank, patch_index, 0, keepdims=False)
    side_index = comp_index.astype(jnp.int32)[None]
    comp = jnp.concatenate([side_index, owner_row])
    ys = (row_index * CY - 1 + jnp.arange(CY + 2, dtype=jnp.int32)).astype(jnp.float32)
    coriolis = coriolis_scale * (2.0 * (ys + 0.5) / (CY * rows_mesh) - 1.0)

    if half % 8 or strip != CX:
        out = general(
            linked, u0, v0, thermal_anomaly, tracers, depth, depth_of_tracers(column_depth), holder_rank, patch_index, coriolis[1:-1],
            biota_exchange_matrix, photic_absorb_share, chroma_loading,
        )
        return out.reshape(1, 2, 1, columns, levels)

    linked, tracers, current_speeds, thermal_anomaly = (
        in_hbm(x) for x in (linked, tracers, current_speeds, thermal_anomaly)
    )
    sent, *edges = pack(side_index, linked, current_speeds, thermal_anomaly)
    got = swap(sent)
    times = functools.partial(jnp.dot, precision=lax.Precision.HIGHEST)
    unit = (jnp.arange(fields) == 0).astype(jnp.float32)
    chain = [jnp.stack([chroma_loading, unit])]
    for _ in range(3):
        chain.append(times(chain[-1], biota_exchange_matrix))
    weights = jnp.stack([c[0] for c in chain] + [c[1] for c in chain[:3]])

    projected, g = project(side_index, tracers, weights)
    low, high, left, right, first_column = edges
    north, south = exchange_rows(low, high)
    left, right, first_column, projected, g = lax.optimization_barrier((left, right, first_column, projected, g))
    edge = east_column(first_column)
    projected, g = in_vmem(projected), in_vmem(g)
    outer = shape_of(4, 2, CY + 2, levels)
    [sides] = call(corner_kernel, side_index, (left, right, north, south), [None] * 4, (outer,), (), "corner")
    column_depth, photic_absorb_share, sides = lax.optimization_barrier((column_depth, photic_absorb_share, sides))
    sides = far_columns(sides)
    tracer_depth = depth_of_tracers(column_depth)
    shares = times(weights, photic_absorb_share)
    kept = first_tracer(side_index, projected, g, got, linked, tracer_depth, shares)
    kept, north, south, sides, edge = lax.optimization_barrier((kept, north, south, sides, edge))
    arrived = to_owners(kept)

    [ring] = call(ring_kernel, side_index, (north, south), [None] * 2, (shape_of(2, CX, levels),), (), "ring")
    args = (current_speeds, thermal_anomaly, linked, got, north, south, sides, edge, swap(ring))
    speeds1, wide_t1, t1, r1 = ocean(1, comp, coriolis, args, wide_depth, CY, half)
    r1 = in_hbm(r1)
    speeds2, t2, r2 = ocean(2, comp, coriolis, (speeds1, wide_t1), wide_depth, CY, half)
    arrived, speeds2, t2 = lax.optimization_barrier((arrived, speeds2, t2))
    speeds2, t2, r2 = in_vmem(speeds2), in_vmem(t2), in_hbm(r2)

    depth_half = pl.BlockSpec((5, CY, half, 1), lambda i, c: (0, 0, c[0], 0))
    piece = shape_of(CY, half, levels)
    scratch = (CY, half, levels)
    line = shape_of(3, half, levels)
    side = shape_of(3, CY, levels)

    t2, irr1, *edges = call(
        absorb_kernel, comp, (arrived, t2, speeds2, depth), [HBM, None, None, depth_half],
        (piece, piece, line, line, side, side), [scratch] * 2, "absorb", [pltpu.SemaphoreType.DMA],
    )
    halos2 = exchange_rows(edges[0], edges[1]) + exchange_half_cols(edges[2], edges[3])
    heat, a, b, g = call(
        second_kernel, comp, (arrived, irr1, t1, r1, depth, shares),
        [None] * 4 + [depth_half, SMEM],
        (piece,) * 4, [scratch] * 2, "second",
    )
    [back] = call(
        last_ocean_kernel, comp, (speeds2, t2, *halos2, depth, heat),
        [None] * 6 + [depth_half, None],
        (shape_of(2, patches, 2, half, levels),), [scratch], "last_ocean",
    )
    flux = lax.all_to_all(
        back.reshape(2 * patches, 2, half, levels), ("comp", "py", "px"), split_axis=0, concat_axis=0, tiled=True
    ).reshape(2, patches, 2, half, levels)
    [absorbed] = call(
        third_kernel, comp, (a, b, g, t2, r2, depth, shares),
        [None] * 5 + [depth_half, SMEM], (shape_of(CY, 2, half, levels),), [scratch], "third",
    )
    other = swap(absorbed)
    [out] = call(
        join_kernel, comp, (absorbed, flux, other), [None] * 3, (shape_of(2, patches, strip, levels),), (), "join"
    )
    return out.reshape(1, 2, 1, columns, levels)


def solution(mesh):
    placed = (
        P(None, "py", "px", None),
        P("py", "px", None),
        P(None, ("py", "px"), None, None),
        P("comp", None, ("py", "px"), None, None),
        P(),
        P(),
        P(),
        P(),
        P(),
        P(),
    )
    return jax.shard_map(
        shards,
        mesh=mesh,
        in_specs=placed,
        out_specs=P("comp", None, ("py", "px"), None, None),
        check_vma=False,
    )
```
